128 devices in a mesh: gx: 16 (over y_lo, x, core), gy: 8 (over y_hi, z).
Axes of the slice: x: 4, y: 4 (y_hi: 2, y_lo: 2; y = y_hi * 2 + y_lo), z: 4, core: 2. Of those that a mesh axis runs over, the one named last changes fastest.
Arguments:
- retained_source: bfloat16 [256, 128, 24, 128], P('gx', 'gy'), may hold values from -6 to 6
- incoming_adjoint: bfloat16 [256, 128, 24, 128], P('gx', 'gy'), may hold values from -6 to 6
- rescale_multiplier: float32 [128], replicated, may hold values from 0.25 to 1.75
- triple_projection_matrix: bfloat16 [128, 384], replicated, may hold values from -0.5 to 0.5
- w_proj: bfloat16 [128, 128], replicated, may hold values from -0.5 to 0.5
- pos_bias: float32 [4, 512, 512], replicated, may hold values from -8 to 320
Outputs:
- grad_input: bfloat16 [256, 128, 24, 128], P('gx', 'gy')
- grad_bias: float32 [4, 512, 512], replicated
- grad_proj: float32 [128, 128], replicated
- grad_qkv: float32 [128, 384], replicated
- multiplier_derivative: float32 [128], replicated
The draws below stay inside these ranges and needn't reach their ends.
All inputs are finite; a program needn't handle non-finite values.
Results may differ from the reference program's by a relative error of at most 0.0095.
Values may be sent and summed in bfloat16 or wider, within the bound.
No kernel may reach another device: no remote copies, remote signals or barrier semaphores. Data moves between devices by JAX's collectives and lax.ppermute only.
A program may use at most 128 MiB of HBM per device.

```python
import jax
import jax.numpy as jnp
from jax import lax

CHANNEL_COUNT = 128
HEADS = 4
WIN = 8
Z = 24
SHIFT = 4
WT = 512
NX = 256
NY = 128


def draw_pos_bias(key, part):
    key = jax.random.fold_in(key, 7)
    keys = jax.random.split(key, 1)
    shape = (HEADS, WIN ** 3, WIN ** 3)
    base = jnp.clip(jax.random.normal(keys[0], shape, jnp.float32), -6.0, 6.0)
    return base


def steps_of(rng, extent, pieces, low, high):
    gain = 1.0
    for dim, shards_of in pieces:
        draws = jax.random.uniform(jax.random.fold_in(jax.random.fold_in(rng, 6), dim), (shards_of,), jnp.float32, low / len(pieces), high / len(pieces))
        gain = gain * jnp.repeat(jnp.exp(draws), extent[dim] // shards_of).reshape((-1,) + (1,) * (len(extent) - 1 - dim))
    return gain


def centred(own_key, dims, width, bound, cuts=(), held_as=jnp.bfloat16):
    entries = width * jax.random.normal(own_key, dims, jnp.float32)
    if cuts:
        entries = entries * steps_of(own_key, dims, cuts, -0.22, 0.18)
    return jnp.clip(entries, -bound, bound).astype(held_as)


def setup_inputs(seed: int = 0) -> dict:
    key_of = jax.random.split(jax.random.key(seed), 7)
    retained_source = centred(key_of[0], (NX, NY, Z, CHANNEL_COUNT), 1.0, 6.0, ((0, 16), (1, 8)))
    incoming_adjoint = centred(key_of[1], (NX, NY, Z, CHANNEL_COUNT), 1.0, 6.0, ((0, 16), (1, 8)))
    rescale_multiplier = jnp.clip(1.0 + 0.15 * jax.random.normal(key_of[2], (CHANNEL_COUNT,), jnp.float32), 0.25, 1.75)
    triple_projection_matrix = centred(key_of[3], (CHANNEL_COUNT, 3 * CHANNEL_COUNT), CHANNEL_COUNT ** -0.5, 0.5)
    w_proj = centred(key_of[4], (CHANNEL_COUNT, CHANNEL_COUNT), CHANNEL_COUNT ** -0.5, 0.5)
    pos_bias = draw_pos_bias(jax.random.fold_in(key_of[6], 71), 0)
    return dict(retained_source=retained_source, incoming_adjoint=incoming_adjoint, rescale_multiplier=rescale_multiplier, triple_projection_matrix=triple_projection_matrix, w_proj=w_proj, pos_bias=pos_bias)


def moment_summary(values):
    floats = values.astype(jnp.float32)
    center = floats - lax.optimization_barrier(jnp.mean(floats, axis=-1, keepdims=True))
    variance = lax.optimization_barrier(jnp.mean(center * center, axis=-1, keepdims=True))
    reciprocal_spread = lax.rsqrt(variance + 1e-05)
    return (center * reciprocal_spread, reciprocal_spread)

def regions(length):
    places = jnp.arange(length, dtype=jnp.int32)
    return (places >= length - WIN).astype(jnp.int32) + (places >= length - SHIFT).astype(jnp.int32)

def to_windows(grid):
    sx, sy, sz, feat = grid.shape
    shaped = grid.reshape(sx // WIN, WIN, sy // WIN, WIN, sz // WIN, WIN, feat)
    return shaped.transpose(0, 2, 4, 1, 3, 5, 6).reshape(-1, WIN * WIN * WIN, feat)

def from_windows(wins, sx, sy, sz):
    feat = wins.shape[-1]
    shaped = wins.reshape(sx // WIN, sy // WIN, sz // WIN, WIN, WIN, WIN, feat)
    return shaped.transpose(0, 3, 1, 4, 2, 5, 6).reshape(sx, sy, sz, feat)

def window_grads(qkv, result_adjoint, label, bias, w_proj):
    tokens, three = qkv.shape
    channel_extent = three // 3
    head_dim = channel_extent // HEADS
    scale = head_dim ** (-0.5)
    query = qkv[:, :channel_extent].astype(jnp.float32).reshape(tokens, HEADS, head_dim)
    keys = qkv[:, channel_extent:2 * channel_extent].astype(jnp.float32).reshape(tokens, HEADS, head_dim)
    values = qkv[:, 2 * channel_extent:].astype(jnp.float32).reshape(tokens, HEADS, head_dim)
    scores = jnp.einsum('qhd,khd->hqk', query, keys) * scale + bias
    allowed = label[:, None] == label[None, :]
    scores = jnp.where(allowed[None], scores, -1e+30)
    top = lax.optimization_barrier(jnp.max(scores, axis=-1, keepdims=True))
    expo = jnp.exp(scores - top)
    prob = expo / lax.optimization_barrier(jnp.sum(expo, axis=-1, keepdims=True))
    prob_b = prob.astype(jnp.bfloat16)
    attended = jnp.einsum('hqk,khd->qhd', prob_b.astype(jnp.float32), values).reshape(tokens, channel_extent).astype(jnp.bfloat16)
    grad_att = jnp.dot(result_adjoint.astype(jnp.float32), w_proj.astype(jnp.float32).T).astype(jnp.bfloat16)
    proj_term = jnp.dot(attended.astype(jnp.float32).T, result_adjoint.astype(jnp.float32))
    grad_heads = grad_att.astype(jnp.float32).reshape(tokens, HEADS, head_dim)
    dprob = jnp.einsum('qhd,khd->hqk', grad_heads, values)
    delta = lax.optimization_barrier(jnp.sum(dprob * prob, axis=-1, keepdims=True))
    dscore = prob * (dprob - delta)
    ds_b = dscore.astype(jnp.bfloat16).astype(jnp.float32)
    dquery = jnp.einsum('hqk,khd->qhd', ds_b, keys) * scale
    dkeys = jnp.einsum('hqk,qhd->khd', ds_b, query) * scale
    dvalues = jnp.einsum('hqk,qhd->khd', prob_b.astype(jnp.float32), grad_heads)
    projection_triple_adjoint = jnp.concatenate([dquery.reshape(tokens, channel_extent), dkeys.reshape(tokens, channel_extent), dvalues.reshape(tokens, channel_extent)], axis=1).astype(jnp.bfloat16)
    return (projection_triple_adjoint, dscore, proj_term)

def reference(retained_source, incoming_adjoint, rescale_multiplier, triple_projection_matrix, w_proj, pos_bias):
    whitened_entries, reciprocal_spread = moment_summary(retained_source)
    standardized_tokens = (whitened_entries * rescale_multiplier).astype(jnp.bfloat16)
    qkv = jnp.dot(standardized_tokens.reshape(-1, CHANNEL_COUNT), triple_projection_matrix, preferred_element_type=jnp.float32).astype(jnp.bfloat16).reshape(NX, NY, Z, 3 * CHANNEL_COUNT)
    rolled_qkv = jnp.roll(qkv, (-SHIFT, -SHIFT, -SHIFT), axis=(0, 1, 2))
    rolled_grad = jnp.roll(incoming_adjoint, (-SHIFT, -SHIFT, -SHIFT), axis=(0, 1, 2))
    label = regions(NX)[:, None, None] * 9 + regions(NY)[None, :, None] * 3 + regions(Z)[None, None, :]
    label_w = to_windows(label[..., None])[..., 0]

    def step(carry, items):
        qkv_w, grad_w, lab_w = items
        projection_triple_adjoint, dscore, proj_term = window_grads(qkv_w, grad_w, lab_w, pos_bias, w_proj)
        return ((carry[0] + dscore, carry[1] + proj_term), projection_triple_adjoint)
    init = (jnp.zeros((HEADS, WT, WT), jnp.float32), jnp.zeros((CHANNEL_COUNT, CHANNEL_COUNT), jnp.float32))
    (grad_bias, grad_proj), dqkv_w = lax.scan(step, init, (to_windows(rolled_qkv), to_windows(rolled_grad), label_w))
    projection_triple_adjoint = jnp.roll(from_windows(dqkv_w, NX, NY, Z), (SHIFT, SHIFT, SHIFT), axis=(0, 1, 2))
    flat_dqkv = projection_triple_adjoint.reshape(-1, 3 * CHANNEL_COUNT)
    grad_qkv = jnp.dot(standardized_tokens.reshape(-1, CHANNEL_COUNT).T, flat_dqkv, preferred_element_type=jnp.float32)
    standardized_adjoint = jnp.dot(flat_dqkv, triple_projection_matrix.T, preferred_element_type=jnp.float32).reshape(NX, NY, Z, CHANNEL_COUNT)
    multiplier_derivative = lax.optimization_barrier(jnp.sum((standardized_adjoint * whitened_entries).reshape(-1, CHANNEL_COUNT), axis=0))
    multiplied_adjoint = standardized_adjoint * rescale_multiplier
    residual_path = reciprocal_spread * (multiplied_adjoint - lax.optimization_barrier(jnp.mean(multiplied_adjoint, axis=-1, keepdims=True)) - whitened_entries * lax.optimization_barrier(jnp.mean(multiplied_adjoint * whitened_entries, axis=-1, keepdims=True)))
    grad_input = (incoming_adjoint.astype(jnp.float32) + residual_path).astype(jnp.bfloat16)
    return (grad_input, grad_bias, grad_proj, grad_qkv, multiplier_derivative)
```

```python
import functools
import math

import jax
import jax.numpy as jnp
from jax import lax
from jax.experimental import pallas as pl
from jax.experimental.pallas import tpu as pltpu
from jax.sharding import PartitionSpec as P

HEADS = 4
HD = 32
C = 128
T = 512
KC = 128
SHIFT = 4
SCALE = HD**-0.5
EXPC = SCALE / math.log(2.0)
BLOCKED = -(2.0**100)
F32 = jnp.float32
BF = jnp.bfloat16


def dot(a, b):
    return lax.dot_general(a, b, (((1,), (0,)), ((), ())), preferred_element_type=F32)


def dot_nt(a, b):
    return lax.dot_general(a, b, (((1,), (1,)), ((), ())), preferred_element_type=F32)


def half_bits(shape, dim):
    token = lax.broadcasted_iota(jnp.int32, shape, dim)
    return [lax.shift_right_logical(token, s) & 1 for s in (8, 5, 2)]


def key_regions():
    lane = lax.broadcasted_iota(jnp.int32, (T, C), 1)
    out = jnp.zeros((T, C), F32)
    for n, bit in enumerate(half_bits((T, C), 0)):
        out = jnp.where(lane == 2 * n, bit.astype(F32), out)
        out = jnp.where(lane == 2 * n + 1, 1.0 - bit.astype(F32), out)
    return out.astype(BF)


def query_regions(edges):
    row = lax.broadcasted_iota(jnp.int32, (16, T), 0)
    out = jnp.zeros((16, T), F32)
    for n, (bit, edge) in enumerate(zip(half_bits((16, T), 1), edges)):
        weight = jnp.where(edge, BLOCKED, 0.0)
        out = jnp.where(row == 2 * n, (1.0 - bit.astype(F32)) * weight, out)
        out = jnp.where(row == 2 * n + 1, bit.astype(F32) * weight, out)
    return out.astype(BF)


def kernel(first, *refs):
    xs_ref, adj_ref, gamma_ref, w_ref, wT_ref, wproj_ref, bias_ref = refs[:7]
    if first:
        gin_ref, dbias_ref, small_ref = refs[7:10]
        scratch = refs[10:]
    else:
        acc_ref, accs_ref = refs[7:9]
        gin_ref, dbias_out, small_ref = refs[9:12]
        dbias_ref = refs[12]
        scratch = refs[13:]
    (biasT_s, xh_s, adj_s, rstd_s, qext_s, gz_s, kext_s, v_s, kT_s, vT_s, gT_s, attT_s, dT_s, dn_s, u_s, e_s, ds_s) = scratch
    step = pl.program_id(0)

    @pl.when(step == 0)
    def _():
        for h in range(HEADS):
            biasT_s[h] = bias_ref[h].T * (1.0 / SCALE)
        if first:
            dbias_ref[...] = jnp.zeros_like(dbias_ref)
            small_ref[...] = jnp.zeros_like(small_ref)
        else:
            dbias_ref[...] = acc_ref[...]
            small_ref[...] = accs_ref[...]
        qext_s[...] = jnp.zeros_like(qext_s)
        gz_s[...] = jnp.zeros_like(gz_s)
        vT_s[...] = jnp.ones_like(vT_s)
        kext_s[:, C:] = key_regions()

    if first:
        edge_x = edge_y = False
    else:
        edge_x = (lax.axis_index("gx") == lax.axis_size("gx") - 1) & (step != 1)
        edge_y = (lax.axis_index("gy") == lax.axis_size("gy") - 1) & (step != 0)
    ones = jnp.full((C, C), 1.0 / C, BF)
    low = lax.broadcasted_iota(jnp.int32, (64, 8, C), 1) < SHIFT
    xb=xs_ref[...].reshape(64*24,C)
    mu=dot(xb,ones)
    cen=xb.astype(F32)-mu
    var=dot((cen*cen).astype(BF),ones)
    rstd=lax.rsqrt(var+1e-5)
    rstd_s[...]=rstd.reshape(64,24,C)
    xh=(cen*rstd).reshape(64,3,8,C)
    a=adj_ref[...].reshape(64,3,8,C).astype(F32)
    for z in range(3):
        z1=(z+1)%3
        xh_s[z]=pltpu.roll(jnp.where(low,xh[:,z1],xh[:,z]),SHIFT,1).reshape(T,C)
        adj_s[z]=pltpu.roll(jnp.where(low,a[:,z1],a[:,z]),SHIFT,1).reshape(T,C).astype(BF)

    def window(z,carry):
        xhat=xh_s[z]
        nrm=(xhat*gamma_ref[...]).astype(BF)
        adj=adj_s[z]
        qkvT=dot_nt(wT_ref[...],nrm).astype(BF)
        kT_s[...]=qkvT[C:2*C]
        regions=query_regions((edge_x,edge_y,z==2))
        for h in range(HEADS):
            vT_s[h,:HD]=qkvT[2*C+HD*h:2*C+HD*(h+1)]
            qext_s[h,HD*h:HD*(h+1)]=qkvT[HD*h:HD*(h+1)]
            qext_s[h,C:C+16]=regions
        kv=dot(nrm,w_ref[:,C:]).astype(BF)
        kext_s[:,:C]=kv[:,:C]
        v_s[...]=kv[:,C:]
        gT_s[...]=dot_nt(wproj_ref[...],adj).astype(BF)
        st={}
        def A(h):
            mx=None
            for kc in range(T//KC):
                ks=slice(kc*KC,(kc+1)*KC)
                u=dot(kext_s[ks],qext_s[h])+biasT_s[h,ks]
                u_s[h%2,ks]=u
                c=jnp.max(u.reshape(KC//8,8,T),axis=0)
                mx=c if mx is None else jnp.maximum(mx,c)
            st["m",h]=jnp.max(mx,axis=0,keepdims=True)
        def B(h):
            m=st["m",h]
            o=None
            for kc in range(T//KC):
                ks=slice(kc*KC,(kc+1)*KC)
                e_s[h%2,ks]=jnp.exp2((u_s[h%2,ks]-m)*EXPC).astype(BF)
            o=dot(vT_s[h],e_s[h%2])
            hs=slice(HD*h,HD*(h+1))
            rl=1.0/o[HD:HD+1]
            gs=(gT_s[hs].astype(F32)*rl).astype(BF)
            on=o[:HD]*rl
            attT_s[hs]=on.astype(BF)
            st["delta",h]=jnp.sum(gs.astype(F32)*on,axis=0,keepdims=True)
            gz_s[h,hs]=gs
        def Cc(h):
            delta=st["delta",h]
            for kc in range(T//KC):
                ks=slice(kc*KC,(kc+1)*KC)
                dp=dot(v_s[ks],gz_s[h])
                ds=e_s[h%2,ks].astype(F32)*(dp-delta)
                ds_s[h%2,ks]=ds.astype(BF)
                dbias_ref[h,ks]+=ds
        def D(h):
            hs=slice(HD*h,HD*(h+1))
            dT_s[hs]=(dot(kT_s[hs],ds_s[h%2])*SCALE).astype(BF)
            dT_s[C+HD*h:C+HD*(h+1)]=(dot_nt(qext_s[h,hs],ds_s[h%2])*SCALE).astype(BF)
            dT_s[2*C+HD*h:2*C+HD*(h+1)]=dot_nt(gz_s[h,hs],e_s[h%2]).astype(BF)

        A(0)
        B(0)
        A(1)
        Cc(0)
        B(1)
        D(0)
        A(2)
        Cc(1)
        B(2)
        D(1)
        A(3)
        Cc(2)
        B(3)
        D(2)
        Cc(3)
        D(3)
        dT=dT_s[...]
        small_ref[:C]+=dot(attT_s[...],adj)
        small_ref[C:4*C]+=dot(dT,nrm)
        dn=dot(w_ref[...],dT).T
        p=dn*xhat
        small_ref[4*C:]+=jnp.sum(p.reshape(64,8,C),axis=0)
        g=dn*gamma_ref[...]
        gm=dot(g.astype(BF),ones)
        gx=dot((p*gamma_ref[...]).astype(BF),ones)
        dn_s[z]=(g-gm-xhat*gx)
        return carry
    lax.fori_loop(0,3,window,0)
    for zc in range(3):
        lo=dn_s[(zc+2)%3].reshape(64,8,C)
        hi=dn_s[zc].reshape(64,8,C)
        r=pltpu.roll(jnp.where(low,hi,lo),SHIFT,1)
        res=a[:,zc]+rstd_s[:,8*zc:8*zc+8]*r
        gin_ref[:,:,8*zc:8*zc+8]=res.astype(BF).reshape(8,8,8,C)

    if not first:
        @pl.when(step == pl.num_programs(0) - 1)
        def _():
            for h in range(HEADS):
                dbias_out[h] = dbias_ref[h].T.astype(BF)


def sublayer(first, blocks, operands):
    def whole(shape):
        return pl.BlockSpec(shape, lambda i: (0,) * len(shape))

    block = pl.BlockSpec((pl.Squeezed(), 8, 8, 24, C), lambda i: (i, 0, 0, 0, 0))
    square = (HEADS, T, T)
    ins = [block, block, whole((1, C)), whole((C, 3 * C)), whole((3 * C, C)), whole((C, C)), whole(square)]
    scratch = []
    if not first:
        ins += [whole(square), whole((4 * C + 8, C))]
        scratch = [pltpu.VMEM(square, F32)]
    scratch += [
        pltpu.VMEM(square, F32),
        pltpu.VMEM((3, T, C), F32),
        pltpu.VMEM((3, T, C), BF),
        pltpu.VMEM((64, 24, C), F32),
        pltpu.VMEM((HEADS, 2 * C, T), BF),
        pltpu.VMEM((HEADS, C, T), BF),
        pltpu.VMEM((T, 2 * C), BF),
        pltpu.VMEM((T, C), BF),
        pltpu.VMEM((C, T), BF),
        pltpu.VMEM((HEADS, 48, T), BF),
        pltpu.VMEM((C, T), BF),
        pltpu.VMEM((C, T), BF),
        pltpu.VMEM((3 * C, T), BF),
        pltpu.VMEM((3, T, C), F32),
        pltpu.VMEM((2, T, T), F32),
        pltpu.VMEM((2, T, T), BF),
        pltpu.VMEM((2, T, T), BF),
    ]
    return pl.pallas_call(
        functools.partial(kernel, first),
        grid=(blocks,),
        in_specs=ins,
        out_specs=[block, whole(square), whole((4 * C + 8, C))],
        out_shape=[
            jax.ShapeDtypeStruct((blocks, 8, 8, 24, C), BF),
            jax.ShapeDtypeStruct(square, F32 if first else BF),
            jax.ShapeDtypeStruct((4 * C + 8, C), F32),
        ],
        scratch_shapes=scratch,
        compiler_params=pltpu.CompilerParams(vmem_limit_bytes=58 * 1024 * 1024),
        cost_estimate=pl.CostEstimate(flops=blocks * 12 * 10**9, bytes_accessed=blocks * 10**7, transcendentals=0),
        name="window_grads",
    )(*operands)


def shifted(values, by_x, by_y):
    nx, ny = lax.axis_size("gx"), lax.axis_size("gy")
    if not by_y:
        return lax.ppermute(values, "gx", [(i, (i + by_x) % nx) for i in range(nx)])
    if not by_x:
        return lax.ppermute(values, "gy", [(i, (i + by_y) % ny) for i in range(ny)])
    pairs = [(i * ny + j, (i + by_x) % nx * ny + (j + by_y) % ny) for i in range(nx) for j in range(ny)]
    return lax.ppermute(values, ("gx", "gy"), pairs)


def flip_pairs(order):
    pairs = []
    for i in range(16):
        for j in range(8):
            axis, bit = order[i & 1]
            k, l = (i ^ bit, j) if axis == "gx" else (i, j ^ bit)
            pairs.append((i * 8 + j, k * 8 + l))
    return pairs


STEPS = [
    (("gx", 1), ("gx", 1)),
    (("gx", 2), ("gy", 1)),
    (("gx", 4), ("gy", 2)),
    (("gy", 1), ("gx", 2)),
    (("gy", 2), ("gx", 4)),
    (("gx", 8), ("gy", 4)),
    (("gy", 4), ("gx", 8)),
]


def my_bit(order):
    gx, gy = lax.axis_index("gx"), lax.axis_index("gy")
    bits = [((gx if axis == "gx" else gy) // bit) % 2 for axis, bit in order]
    return jnp.where(gx % 2 == 0, bits[0], bits[1])


def summed(values):
    for order in STEPS:
        half = values.shape[0] // 2
        mine = my_bit(order)
        away = lax.dynamic_slice_in_dim(values, (1 - mine) * half, half)
        keep = lax.dynamic_slice_in_dim(values, mine * half, half)
        got = lax.ppermute(away, ("gx", "gy"), flip_pairs(order))
        values = (keep.astype(F32) + got.astype(F32)).astype(BF)
    for order in reversed(STEPS):
        mine = my_bit(order)
        got = lax.ppermute(values, ("gx", "gy"), flip_pairs(order))
        values = jnp.where(mine == 0, jnp.concatenate([values, got]), jnp.concatenate([got, values]))
    return values


def body(retained_source, incoming_adjoint, rescale_multiplier, triple_projection_matrix, w_proj, pos_bias):
    both = jnp.stack([retained_source, incoming_adjoint])
    from_x = shifted(both[:, :4, 4:], -1, 0)
    from_y = shifted(both[:, 4:, :4], 0, -1)
    from_xy = shifted(both[:, :4, :4], -1, -1)
    params = (
        rescale_multiplier.reshape(1, C),
        triple_projection_matrix,
        triple_projection_matrix.T,
        w_proj,
        pos_bias,
    )
    inner = both[:, 4:12, 4:12]
    gin_a, acc, acc_small = sublayer(True, 1, (inner[0][None], inner[1][None]) + params)
    rim = jnp.stack(
        [
            jnp.concatenate([both[:, 12:, 4:12], from_x[:, :, :8]], axis=1),
            jnp.concatenate([both[:, 4:12, 12:], from_y[:, :8]], axis=2),
            jnp.concatenate(
                [
                    jnp.concatenate([both[:, 12:, 12:], from_y[:, 8:]], axis=2),
                    jnp.concatenate([from_x[:, :, 8:], from_xy], axis=2),
                ],
                axis=1,
            ),
        ],
        axis=1,
    )
    gin_b, grad_bias, small = sublayer(False, 3, (rim[0], rim[1]) + params + (acc, acc_small))
    bx, by, bc = gin_b[0], gin_b[1], gin_b[2]
    back_x = shifted(jnp.concatenate([bx[4:], bc[4:, :4]], axis=1), 1, 0)
    back_y = shifted(jnp.concatenate([by[:, 4:], bc[:4, 4:]], axis=0), 0, 1)
    back_xy = shifted(bc[4:, 4:], 1, 1)
    grad_input = jnp.concatenate(
        [
            jnp.concatenate([back_xy, back_x], axis=1),
            jnp.concatenate([back_y[:8], gin_a[0], by[:, :4]], axis=1),
            jnp.concatenate([back_y[8:], bx[:4], bc[:4, :4]], axis=1),
        ],
        axis=0,
    )
    rows = HEADS * T * T // C
    packed = jnp.concatenate([grad_bias.reshape(rows, C), small.astype(BF), jnp.zeros((1024 - small.shape[0], C), BF)])
    total = summed(packed)
    grad_bias = total[:rows].astype(F32).reshape(HEADS, T, T)
    rest = total[rows : rows + small.shape[0]].astype(F32)
    return (grad_input, grad_bias, rest[:C], rest[C : 4 * C].T, jnp.sum(rest[4 * C :], axis=0))


def solution(mesh):
    placed = (P("gx", "gy", None, None), P("gx", "gy", None, None), P(), P(), P(), P())
    return jax.shard_map(
        body,
        mesh=mesh,
        in_specs=placed,
        out_specs=(P("gx", "gy", None, None), P(), P(), P(), P()),
        check_vma=False,
    )
```

```python
import functools
import math

import jax
import jax.numpy as jnp
from jax import lax
from jax.experimental import pallas as pl
from jax.experimental.pallas import tpu as pltpu
from jax.sharding import PartitionSpec as P

HEADS = 4
HD = 32
C = 128
T = 512
KC = 128
HALF = 2 * T + C
SHIFT = 4
SCALE = HD**-0.5
EXPC = SCALE / math.log(2.0)
BLOCKED = -(2.0**100)
F32 = jnp.float32
BF = jnp.bfloat16


def dot(a, b):
    return lax.dot_general(a, b, (((1,), (0,)), ((), ())), preferred_element_type=F32)


def dot_nt(a, b):
    return lax.dot_general(a, b, (((1,), (1,)), ((), ())), preferred_element_type=F32)


def half_bits(shape, dim):
    token = lax.broadcasted_iota(jnp.int32, shape, dim)
    return [lax.shift_right_logical(token, s) & 1 for s in (8, 5, 2)]


def key_regions():
    lane = lax.broadcasted_iota(jnp.int32, (T, C), 1)
    out = jnp.zeros((T, C), F32)
    for n, bit in enumerate(half_bits((T, C), 0)):
        out = jnp.where(lane == 2 * n, bit.astype(F32), out)
        out = jnp.where(lane == 2 * n + 1, 1.0 - bit.astype(F32), out)
    return out.astype(BF)


def query_regions(edges):
    row = lax.broadcasted_iota(jnp.int32, (16, T), 0)
    out = jnp.zeros((16, T), F32)
    for n, (bit, edge) in enumerate(zip(half_bits((16, T), 1), edges)):
        weight = jnp.where(edge, BLOCKED, 0.0)
        out = jnp.where(row == 2 * n, (1.0 - bit.astype(F32)) * weight, out)
        out = jnp.where(row == 2 * n + 1, bit.astype(F32) * weight, out)
    return out.astype(BF)


INNER = [(0, 0, 4, 4, 0, 0, 8, 8)]
RIM = [
    (0, 0, 12, 4, 0, 0, 4, 8),
    (0, 1, 0, 0, 4, 0, 4, 8),
    (1, 0, 4, 12, 0, 0, 8, 4),
    (1, 2, 0, 0, 0, 4, 8, 4),
    (2, 0, 12, 12, 0, 0, 4, 4),
    (2, 1, 0, 8, 4, 0, 4, 4),
    (2, 2, 8, 0, 0, 4, 4, 4),
    (2, 3, 0, 0, 4, 4, 4, 4),
]


def kernel(first, *refs):
    pieces = INNER if first else RIM
    xs_hbm, adj_hbm, gamma_ref, w_ref, wT_ref, wproj_ref, bias_ref = refs[:7]
    if first:
        gin_hbm, dbias_ref, small_ref = refs[7:10]
        rest = refs[10:]
        ends = [gin_hbm]
    else:
        halos = refs[7:10]
        acc_ref, accs_ref, _ = refs[10:13]
        ends = refs[13:17]
        away_ref, keep_ref = refs[17:19]
        dbias_ref, small_ref = refs[19:21]
        rest = refs[21:]
    in_sem, out_sem, blk_s, gin_s = rest[:4]
    (biasT_s, xh_s, adj_s, rstd_s, qext_s, gz_s, kext_s, v_s, kT_s, vT_s, gT_s, attT_s, dT_s, dn_s, u_s, e_s, ds_s) = rest[4:]

    def arriving(n, which):
        block, origin, x, y, bx, by, ex, ey = pieces[n]
        if origin:
            src = halos[origin - 1].at[which, pl.ds(x, ex), pl.ds(y, ey)]
        else:
            src = (adj_hbm if which else xs_hbm).at[pl.ds(x, ex), pl.ds(y, ey)]
        dst = blk_s.at[which, block, pl.ds(bx, ex), pl.ds(by, ey)]
        return pltpu.make_async_copy(src, dst, in_sem.at[which, n])

    def leaving(n):
        block, origin, x, y, bx, by, ex, ey = pieces[n]
        src = gin_s.at[block, pl.ds(bx, ex), pl.ds(by, ey)]
        return pltpu.make_async_copy(src, ends[origin].at[pl.ds(x, ex), pl.ds(y, ey)], out_sem.at[n])

    step = pl.program_id(0)

    @pl.when(step == 0)
    def _():
        for n in range(len(pieces)):
            arriving(n, 0).start()
            arriving(n, 1).start()
        for h in range(HEADS):
            biasT_s[h] = bias_ref[h].T * (1.0 / SCALE)
        if first:
            dbias_ref[...] = jnp.zeros_like(dbias_ref)
            small_ref[...] = jnp.zeros_like(small_ref)
        else:
            dbias_ref[...] = acc_ref[...]
            small_ref[...] = accs_ref[...]
        qext_s[...] = jnp.zeros_like(qext_s)
        gz_s[...] = jnp.zeros_like(gz_s)
        vT_s[...] = jnp.ones_like(vT_s)
        kext_s[:, C:] = key_regions()

    if first:
        edge_x = edge_y = False
    else:
        edge_x = (lax.axis_index("gx") == lax.axis_size("gx") - 1) & (step != 1)
        edge_y = (lax.axis_index("gy") == lax.axis_size("gy") - 1) & (step != 0)
    for block in sorted({p[0] for p in pieces}):

        @pl.when(step == block)
        def _(block=block):
            for n, piece in enumerate(pieces):
                if piece[0] == block:
                    arriving(n, 0).wait()
                    arriving(n, 1).wait()

    ones = jnp.full((C, C), 1.0 / C, BF)
    low = lax.broadcasted_iota(jnp.int32, (64, 8, C), 1) < SHIFT
    xb=blk_s[0, step].reshape(64*24,C)
    mu=dot(xb,ones)
    cen=xb.astype(F32)-mu
    var=dot((cen*cen).astype(BF),ones)
    rstd=lax.rsqrt(var+1e-5)
    rstd_s[...]=rstd.reshape(64,24,C)
    xh=(cen*rstd).reshape(64,3,8,C)
    a=blk_s[1, step].reshape(64,3,8,C).astype(F32)
    for z in range(3):
        z1=(z+1)%3
        xh_s[z]=pltpu.roll(jnp.where(low,xh[:,z1],xh[:,z]),SHIFT,1).reshape(T,C)
        adj_s[z]=pltpu.roll(jnp.where(low,a[:,z1],a[:,z]),SHIFT,1).reshape(T,C).astype(BF)

    def window(z,carry):
        xhat=xh_s[z]
        nrm=(xhat*gamma_ref[...]).astype(BF)
        adj=adj_s[z]
        qkvT=dot_nt(wT_ref[...],nrm).astype(BF)
        kT_s[...]=qkvT[C:2*C]
        regions=query_regions((edge_x,edge_y,z==2))
        for h in range(HEADS):
            vT_s[h,:HD]=qkvT[2*C+HD*h:2*C+HD*(h+1)]
            qext_s[h,HD*h:HD*(h+1)]=qkvT[HD*h:HD*(h+1)]
            qext_s[h,C:C+16]=regions
        kv=dot(nrm,w_ref[:,C:]).astype(BF)
        kext_s[:,:C]=kv[:,:C]
        v_s[...]=kv[:,C:]
        gT_s[...]=dot_nt(wproj_ref[...],adj).astype(BF)
        st={}
        def A(h):
            mx=None
            for kc in range(T//KC):
                ks=slice(kc*KC,(kc+1)*KC)
                u=dot(kext_s[ks],qext_s[h])+biasT_s[h,ks]
                u_s[h%2,ks]=u
                c=jnp.max(u.reshape(KC//8,8,T),axis=0)
                mx=c if mx is None else jnp.maximum(mx,c)
            st["m",h]=jnp.max(mx,axis=0,keepdims=True)
        def B(h):
            m=st["m",h]
            o=None
            for kc in range(T//KC):
                ks=slice(kc*KC,(kc+1)*KC)
                e_s[h%2,ks]=jnp.exp2((u_s[h%2,ks]-m)*EXPC).astype(BF)
            o=dot(vT_s[h],e_s[h%2])
            hs=slice(HD*h,HD*(h+1))
            rl=1.0/o[HD:HD+1]
            gs=(gT_s[hs].astype(F32)*rl).astype(BF)
            on=o[:HD]*rl
            attT_s[hs]=on.astype(BF)
            st["delta",h]=jnp.sum(gs.astype(F32)*on,axis=0,keepdims=True)
            gz_s[h,hs]=gs
        def Cc(h):
            delta=st["delta",h]
            for kc in range(T//KC):
                ks=slice(kc*KC,(kc+1)*KC)
                dp=dot(v_s[ks],gz_s[h])
                ds=e_s[h%2,ks].astype(F32)*(dp-delta)
                ds_s[h%2,ks]=ds.astype(BF)
                dbias_ref[h,ks]+=ds
        def D(h):
            hs=slice(HD*h,HD*(h+1))
            dT_s[hs]=(dot(kT_s[hs],ds_s[h%2])*SCALE).astype(BF)
            dT_s[C+HD*h:C+HD*(h+1)]=(dot_nt(qext_s[h,hs],ds_s[h%2])*SCALE).astype(BF)
            dT_s[2*C+HD*h:2*C+HD*(h+1)]=dot_nt(gz_s[h,hs],e_s[h%2]).astype(BF)

        A(0)
        B(0)
        A(1)
        Cc(0)
        B(1)
        D(0)
        A(2)
        Cc(1)
        B(2)
        D(1)
        A(3)
        Cc(2)
        B(3)
        D(2)
        Cc(3)
        D(3)
        dT=dT_s[...]
        small_ref[:C]+=dot(attT_s[...],adj)
        small_ref[C:4*C]+=dot(dT,nrm)
        dn=dot(w_ref[...],dT).T
        p=dn*xhat
        small_ref[4*C:]+=jnp.sum(p.reshape(64,8,C),axis=0)
        g=dn*gamma_ref[...]
        gm=dot(g.astype(BF),ones)
        gx=dot((p*gamma_ref[...]).astype(BF),ones)
        dn_s[z]=(g-gm-xhat*gx)
        return carry
    lax.fori_loop(0,3,window,0)
    for zc in range(3):
        lo=dn_s[(zc+2)%3].reshape(64,8,C)
        hi=dn_s[zc].reshape(64,8,C)
        r=pltpu.roll(jnp.where(low,hi,lo),SHIFT,1)
        res=a[:,zc]+rstd_s[:,8*zc:8*zc+8]*r
        gin_s[step,:,:,8*zc:8*zc+8]=res.astype(BF).reshape(8,8,8,C)

    for block in sorted({p[0] for p in pieces}):

        @pl.when(step == block)
        def _(block=block):
            for n, piece in enumerate(pieces):
                if piece[0] == block:
                    leaving(n).start()

    @pl.when(step == pl.num_programs(0) - 1)
    def _():
        if not first:
            mine = lax.axis_index("gx") % 2
            table = jnp.concatenate([small_ref[:C], small_ref[C : 4 * C].T], axis=1)
            gain = jnp.concatenate(
                [jnp.sum(small_ref[4 * C :], axis=0, keepdims=True), jnp.zeros((1, 3 * C), F32)], axis=1
            )
            gain = jnp.where(lax.broadcasted_iota(jnp.int32, (C, T), 0) == 0, gain, 0.0)
            for j in range(2):
                away_ref[j * T : (j + 1) * T] = dbias_ref[2 * (1 - mine) + j].T.astype(BF)
                keep_ref[j * T : (j + 1) * T] = dbias_ref[2 * mine + j].T
            away_ref[2 * T :] = jnp.where(mine == 1, table, gain).astype(BF)
            keep_ref[2 * T :] = jnp.where(mine == 0, table, gain)
        for n in range(len(pieces)):
            leaving(n).wait()


def sublayer(first, operands):
    def whole(shape):
        return pl.BlockSpec(shape, lambda i: (0,) * len(shape))

    anywhere = pl.BlockSpec(memory_space=pl.ANY)
    square = (HEADS, T, T)
    small = (4 * C + 8, C)
    grid_shape = (16, 16, 24, C)
    blocks = 1 if first else 3
    pieces = INNER if first else RIM
    ins = [anywhere, anywhere, whole((1, C)), whole((C, 3 * C)), whole((3 * C, C)), whole((C, C)), whole(square)]
    if first:
        outs = [anywhere, whole(square), whole(small)]
        shapes = [(grid_shape, BF), (square, F32), (small, F32)]
        scratch = []
        aliases = {}
    else:
        ins += [anywhere] * 3 + [whole(square), whole(small), anywhere]
        outs = [anywhere] * 4 + [whole((HALF, T)), whole((HALF, T))]
        shapes = [(grid_shape, BF), ((4, 12, 24, C), BF), ((12, 4, 24, C), BF), ((4, 4, 24, C), BF), ((HALF, T), BF), ((HALF, T), F32)]
        scratch = [pltpu.VMEM(square, F32), pltpu.VMEM(small, F32)]
        aliases = {12: 0}
    scratch += [
        pltpu.SemaphoreType.DMA((2, len(pieces))),
        pltpu.SemaphoreType.DMA((len(pieces),)),
        pltpu.VMEM((2, blocks, 8, 8, 24, C), BF),
        pltpu.VMEM((blocks, 8, 8, 24, C), BF),
        pltpu.VMEM(square, F32),
        pltpu.VMEM((3, T, C), F32),
        pltpu.VMEM((3, T, C), BF),
        pltpu.VMEM((64, 24, C), F32),
        pltpu.VMEM((HEADS, 2 * C, T), BF),
        pltpu.VMEM((HEADS, C, T), BF),
        pltpu.VMEM((T, 2 * C), BF),
        pltpu.VMEM((T, C), BF),
        pltpu.VMEM((C, T), BF),
        pltpu.VMEM((HEADS, 48, T), BF),
        pltpu.VMEM((C, T), BF),
        pltpu.VMEM((C, T), BF),
        pltpu.VMEM((3 * C, T), BF),
        pltpu.VMEM((3, T, C), F32),
        pltpu.VMEM((2, T, T), F32),
        pltpu.VMEM((2, T, T), BF),
        pltpu.VMEM((2, T, T), BF),
    ]
    return pl.pallas_call(
        functools.partial(kernel, first),
        grid=(blocks,),
        in_specs=ins,
        out_specs=outs,
        out_shape=[jax.ShapeDtypeStruct(shape, dtype) for shape, dtype in shapes],
        scratch_shapes=scratch,
        input_output_aliases=aliases,
        compiler_params=pltpu.CompilerParams(vmem_limit_bytes=58 * 1024 * 1024),
        cost_estimate=pl.CostEstimate(flops=blocks * 12 * 10**9, bytes_accessed=blocks * 10**7, transcendentals=0),
        name="inner_windows" if first else "rim_windows",
    )(*operands)


def spread_kernel(mine_ref, own_ref, got_ref, out_ref):
    @pl.when(pl.program_id(0) == 0)
    def _():
        out_ref[...] = own_ref[...].astype(F32)

    @pl.when(pl.program_id(0) == 1)
    def _():
        out_ref[...] = got_ref[...].astype(F32)


def spread(mine, own, got):
    return pl.pallas_call(
        spread_kernel,
        grid_spec=pltpu.PrefetchScalarGridSpec(
            num_scalar_prefetch=1,
            grid=(2, 2),
            in_specs=[
                pl.BlockSpec((T, T), lambda s, j, m: (jnp.where(s == 0, j, 1), 0)),
                pl.BlockSpec((T, T), lambda s, j, m: (jnp.where(s == 0, 0, j), 0)),
            ],
            out_specs=pl.BlockSpec((pl.Squeezed(), T, T), lambda s, j, m: (jnp.where(s == 0, m[0], 1 - m[0]) * 2 + j, 0, 0)),
        ),
        out_shape=jax.ShapeDtypeStruct((HEADS, T, T), F32),
        name="spread",
    )(mine.reshape(1), own, got)


def shifted(values, by_x, by_y):
    nx, ny = lax.axis_size("gx"), lax.axis_size("gy")
    if not by_y:
        return lax.ppermute(values, "gx", [(i, (i + by_x) % nx) for i in range(nx)])
    if not by_x:
        return lax.ppermute(values, "gy", [(i, (i + by_y) % ny) for i in range(ny)])
    pairs = [(i * ny + j, (i + by_x) % nx * ny + (j + by_y) % ny) for i in range(nx) for j in range(ny)]
    return lax.ppermute(values, ("gx", "gy"), pairs)


CORE = (("gx", 1), ("gx", 1))
HALVED = [
    (("gx", 2), ("gy", 1)),
    (("gx", 4), ("gy", 2)),
    (("gx", 8), ("gy", 4)),
]
WHOLE = [
    (("gy", 1), ("gx", 2)),
    (("gy", 2), ("gx", 4)),
    (("gy", 4), ("gx", 8)),
]


def swap(values, order):
    pairs = []
    for i in range(16):
        for j in range(8):
            axis, bit = order[i & 1]
            k, l = (i ^ bit, j) if axis == "gx" else (i, j ^ bit)
            pairs.append((i * 8 + j, k * 8 + l))
    return lax.ppermute(values, ("gx", "gy"), pairs)


def my_bit(order):
    gx, gy = lax.axis_index("gx"), lax.axis_index("gy")
    bits = [((gx if axis == "gx" else gy) // bit) % 2 for axis, bit in order]
    return jnp.where(gx % 2 == 0, bits[0], bits[1])


def summed(away, keep):
    values = keep + swap(away, CORE).astype(F32)
    for order in HALVED:
        half = values.shape[0] // 2
        mine = my_bit(order)
        away = lax.dynamic_slice_in_dim(values, (1 - mine) * half, half).astype(BF)
        keep = lax.dynamic_slice_in_dim(values, mine * half, half)
        values = keep + swap(away, order).astype(F32)
    for order in WHOLE:
        values = values + swap(values, order)
    values = values.astype(BF)
    for order in reversed(HALVED):
        mine = my_bit(order)
        got = swap(values, order)
        values = jnp.where(mine == 0, jnp.concatenate([values, got]), jnp.concatenate([got, values]))
    return values, swap(values, CORE)


def body(retained_source, incoming_adjoint, rescale_multiplier, triple_projection_matrix, w_proj, pos_bias):
    both = (retained_source, incoming_adjoint)
    from_x = shifted(jnp.stack([v[:4, 4:] for v in both]), -1, 0)
    from_y = shifted(jnp.stack([v[4:, :4] for v in both]), 0, -1)
    from_xy = shifted(jnp.stack([v[:4, :4] for v in both]), -1, -1)
    params = (
        rescale_multiplier.reshape(1, C),
        triple_projection_matrix,
        triple_projection_matrix.T,
        w_proj,
        pos_bias,
    )
    gin, acc, acc_small = sublayer(True, both + params)
    gin, back_x, back_y, back_xy, away, keep = sublayer(False, both + params + (from_x, from_y, from_xy, acc, acc_small, gin))
    back_x = shifted(back_x, 1, 0)
    back_y = shifted(back_y, 0, 1)
    back_xy = shifted(back_xy, 1, 1)
    gin = lax.dynamic_update_slice(gin, back_x, (0, 4, 0, 0))
    gin = lax.dynamic_update_slice(gin, back_y, (4, 0, 0, 0))
    gin = lax.dynamic_update_slice(gin, back_xy, (0, 0, 0, 0))
    own, got = summed(away, keep)
    mine = lax.axis_index("gx") % 2
    grad_bias = spread(mine, own, got)
    table = jnp.where(mine == 0, own[2 * T :], got[2 * T :]).astype(F32)
    gain = jnp.where(mine == 0, got[2 * T, :C], own[2 * T, :C]).astype(F32)
    return (gin, grad_bias, table[:, :C], table[:, C:], gain)


def solution(mesh):
    placed = (P("gx", "gy", None, None), P("gx", "gy", None, None), P(), P(), P(), P())
    return jax.shard_map(
        body,
        mesh=mesh,
        in_specs=placed,
        out_specs=(P("gx", "gy", None, None), P(), P(), P(), P()),
        check_vma=False,
    )
```

```python
import functools
import math

import jax
import jax.numpy as jnp
from jax import lax
from jax.experimental import pallas as pl
from jax.experimental.pallas import tpu as pltpu
from jax.sharding import PartitionSpec as P

HEADS = 4
HD = 32
C = 128
T = 512
KC = 256
HALF = 2 * T + C
SHIFT = 4
SCALE = HD**-0.5
EXPC = SCALE / math.log(2.0)
BLOCKED = -(2.0**100)
F32 = jnp.float32
BF = jnp.bfloat16


def dot(a, b):
    return lax.dot_general(a, b, (((1,), (0,)), ((), ())), preferred_element_type=F32)


def dot_nt(a, b):
    return lax.dot_general(a, b, (((1,), (1,)), ((), ())), preferred_element_type=F32)


def half_bits(shape, dim):
    token = lax.broadcasted_iota(jnp.int32, shape, dim)
    return [lax.shift_right_logical(token, s) & 1 for s in (8, 5, 2)]


def key_regions():
    lane = lax.broadcasted_iota(jnp.int32, (T, C), 1)
    out = jnp.zeros((T, C), F32)
    for n, bit in enumerate(half_bits((T, C), 0)):
        out = jnp.where(lane == 2 * n, bit.astype(F32), out)
        out = jnp.where(lane == 2 * n + 1, 1.0 - bit.astype(F32), out)
    return out.astype(BF)


def query_regions(edges):
    row = lax.broadcasted_iota(jnp.int32, (16, T), 0)
    out = jnp.zeros((16, T), F32)
    for n, (bit, edge) in enumerate(zip(half_bits((16, T), 1), edges)):
        weight = jnp.where(edge, BLOCKED, 0.0)
        out = jnp.where(row == 2 * n, (1.0 - bit.astype(F32)) * weight, out)
        out = jnp.where(row == 2 * n + 1, bit.astype(F32) * weight, out)
    return out.astype(BF)


INNER = [(0, 0, 4, 4, 0, 0, 8, 8)]
RIM = [
    (0, 0, 12, 4, 0, 0, 4, 8),
    (0, 1, 0, 0, 4, 0, 4, 8),
    (1, 0, 4, 12, 0, 0, 8, 4),
    (1, 2, 0, 0, 0, 4, 8, 4),
    (2, 0, 12, 12, 0, 0, 4, 4),
    (2, 1, 0, 8, 4, 0, 4, 4),
    (2, 2, 8, 0, 0, 4, 4, 4),
    (2, 3, 0, 0, 4, 4, 4, 4),
]


def arriving(pieces, arrays, blk_s, sem, n, which):
    block, origin, x, y, bx, by, ex, ey = pieces[n]
    if origin:
        src = arrays[1 + origin].at[which, pl.ds(x, ex), pl.ds(y, ey)]
    else:
        src = arrays[which].at[pl.ds(x, ex), pl.ds(y, ey)]
    return pltpu.make_async_copy(src, blk_s.at[which, block, pl.ds(bx, ex), pl.ds(by, ey)], sem.at[which, n])


def start_all(pieces, arrays, blk_s, sem):
    for n in range(len(pieces)):
        for which in range(2):
            arriving(pieces, arrays, blk_s, sem, n, which).start()


def wait_block(pieces, arrays, blk_s, sem, step):
    for block in sorted({p[0] for p in pieces}):

        @pl.when(step == block)
        def _(block=block):
            for n, piece in enumerate(pieces):
                if piece[0] == block:
                    for which in range(2):
                        arriving(pieces, arrays, blk_s, sem, n, which).wait()


def standardized(block):
    ones = jnp.full((C, C), 1.0 / C, BF)
    flat = block.reshape(64 * 24, C)
    centred = flat.astype(F32) - dot(flat, ones)
    rstd = lax.rsqrt(dot((centred * centred).astype(BF), ones) + 1e-5)
    return (centred * rstd).reshape(64, 3, 8, C), rstd.reshape(64, 3, 8, C)


def kernel(first, *refs):
    pieces = INNER if first else RIM
    arrays = refs[:2] if first else refs[:5]
    refs = refs[len(arrays) :]
    gamma_ref, w_ref, wT_ref, wproj_ref, bias_hbm = refs[:5]
    refs = refs[5:]
    if first:
        dT_ref, dbias_ref, small_ref = refs[:3]
        refs = refs[3:]
    else:
        acc_hbm, accs_ref = refs[:2]
        dT_ref, away_ref, keep_ref = refs[2:5]
        dbias_ref, small_ref, acc_s, acc_sem = refs[5:9]
        refs = refs[9:]
    (in_sem, bias_sem, blk_s, bias_s, biasT_s, xh_s, adj_s, qext_s, gz_s, kext_s, v_s, kT_s, vT_s, gT_s, attT_s, u_s, e_s, ds_s) = refs
    step = pl.program_id(0)

    def bias_copy(h):
        return pltpu.make_async_copy(bias_hbm.at[h], bias_s.at[h], bias_sem.at[h])

    @pl.when(step == 0)
    def _():
        start_all(pieces, arrays, blk_s, in_sem)
        for h in range(HEADS):
            bias_copy(h).start()
        if not first:
            pltpu.make_async_copy(acc_hbm, acc_s, acc_sem).start()
        dbias_ref[...] = jnp.zeros_like(dbias_ref)
        small_ref[...] = jnp.zeros_like(small_ref)
        qext_s[...] = jnp.zeros_like(qext_s)
        gz_s[...] = jnp.zeros_like(gz_s)
        vT_s[...] = jnp.ones_like(vT_s)
        kext_s[:, C:] = key_regions()

    if first:
        edge_x = edge_y = False
    else:
        edge_x = (lax.axis_index("gx") == lax.axis_size("gx") - 1) & (step != 1)
        edge_y = (lax.axis_index("gy") == lax.axis_size("gy") - 1) & (step != 0)
    wait_block(pieces, arrays, blk_s, in_sem, step)
    low = lax.broadcasted_iota(jnp.int32, (64, 8, C), 1) < SHIFT
    xh, _ = standardized(blk_s[0, step])
    a = blk_s[1, step].reshape(64, 3, 8, C).astype(F32)
    for z in range(3):
        z1 = (z + 1) % 3
        xh_s[z] = pltpu.roll(jnp.where(low, xh[:, z1], xh[:, z]) * gamma_ref[...], SHIFT, 1).reshape(T, C).astype(BF)
        adj_s[z] = pltpu.roll(jnp.where(low, a[:, z1], a[:, z]), SHIFT, 1).reshape(T, C).astype(BF)

    @pl.when(step == 0)
    def _():
        for h in range(HEADS):
            bias_copy(h).wait()
            biasT_s[h] = bias_s[h].T * (1.0 / SCALE)

    def window(z, carry):
        nrm = xh_s[z]
        adj = adj_s[z]
        qkvT = dot_nt(wT_ref[...], nrm).astype(BF)
        kT_s[...] = qkvT[C : 2 * C]
        regions = query_regions((edge_x, edge_y, z == 2))
        for h in range(HEADS):
            vT_s[h, :HD] = qkvT[2 * C + HD * h : 2 * C + HD * (h + 1)]
            qext_s[h, HD * h : HD * (h + 1)] = qkvT[HD * h : HD * (h + 1)]
            qext_s[h, C : C + 16] = regions
        kv = dot(nrm, w_ref[:, C:]).astype(BF)
        kext_s[:, :C] = kv[:, :C]
        v_s[...] = kv[:, C:]
        gT_s[...] = dot_nt(wproj_ref[...], adj).astype(BF)
        chunks = T // KC
        held = {}

        def scores(h, c):
            ks = slice(c * KC, (c + 1) * KC)
            u = dot(kext_s[ks], qext_s[h]) + biasT_s[h, ks]
            u_s[h % 2, ks] = u
            top = jnp.max(u.reshape(KC // 8, 8, T), axis=0)
            held["top", h] = top if c == 0 else jnp.maximum(top, held["top", h])
            if c == chunks - 1:
                held["top", h] = jnp.max(held["top", h], axis=0, keepdims=True)

        def weights(h, c):
            ks = slice(c * KC, (c + 1) * KC)
            e = jnp.exp2((u_s[h % 2, ks] - held["top", h]) * EXPC).astype(BF)
            e_s[h % 3, ks] = e
            o = dot(vT_s[h, :, ks], e)
            held["o", h] = o if c == 0 else o + held["o", h]
            if c == chunks - 1:
                o = held["o", h]
                hs = slice(HD * h, HD * (h + 1))
                inverse = 1.0 / o[HD : HD + 1]
                gs = (gT_s[hs].astype(F32) * inverse).astype(BF)
                attended = o[:HD] * inverse
                attT_s[hs] = attended.astype(BF)
                held["delta", h] = jnp.sum(gs.astype(F32) * attended, axis=0, keepdims=True)
                gz_s[h, hs] = gs

        def score_grads(h, c):
            ks = slice(c * KC, (c + 1) * KC)
            dp = dot(v_s[ks], gz_s[h])
            ds = e_s[h % 3, ks].astype(F32) * (dp - held["delta", h])
            ds_s[h % 2, ks] = ds.astype(BF)
            dbias_ref[h, ks] += ds

        def qkv_grads(h, c):
            hs = slice(HD * h, HD * (h + 1))
            ks = slice(c * KC, (c + 1) * KC)
            dq = dot(kT_s[hs, ks], ds_s[h % 2, ks])
            held["dq", h] = dq if c == 0 else dq + held["dq", h]
            dT_ref[z, C + HD * h : C + HD * (h + 1), ks] = (dot_nt(qext_s[h, hs], ds_s[h % 2, ks]) * SCALE).astype(BF)
            dT_ref[z, 2 * C + HD * h : 2 * C + HD * (h + 1), ks] = dot_nt(gz_s[h, hs], e_s[h % 3, ks]).astype(BF)
            if c == chunks - 1:
                dT_ref[z, hs] = (held["dq", h] * SCALE).astype(BF)

        for turn in range(HEADS + 3):
            for c in range(chunks):
                for lag, stage in ((3, qkv_grads), (2, score_grads), (1, weights), (0, scores)):
                    if 0 <= turn - lag < HEADS:
                        stage(turn - lag, c)
        small_ref[:C] += dot(attT_s[...], adj)
        small_ref[C:] += dot(dT_ref[z], nrm)
        return carry

    lax.fori_loop(0, 3, window, 0)

    if not first:

        @pl.when(step == pl.num_programs(0) - 1)
        def _():
            pltpu.make_async_copy(acc_hbm, acc_s, acc_sem).wait()
            mine = lax.axis_index("gx") % 2
            small = small_ref[...] + accs_ref[...]
            table = jnp.concatenate([small[:C], small[C:].T], axis=1)
            for j in range(2):
                h = 2 * (1 - mine) + j
                away_ref[j * T : (j + 1) * T] = (dbias_ref[h] + acc_s[h]).T.astype(BF)
                h = 2 * mine + j
                keep_ref[j * T : (j + 1) * T] = (dbias_ref[h] + acc_s[h]).T
            away_ref[2 * T :] = jnp.where(mine == 1, table, 0.0).astype(BF)
            keep_ref[2 * T :] = jnp.where(mine == 0, table, 0.0)


def finish_kernel(first, *refs):
    pieces = INNER if first else RIM
    arrays = refs[:2] if first else refs[:5]
    refs = refs[len(arrays) :]
    gamma_ref, w_ref, dT_ref = refs[:3]
    ends = refs[4:5] if first else refs[3:7]
    in_sem, out_sem, blk_s, gin_s = refs[-4:]
    step = pl.program_id(0)

    def leaving(n):
        block, origin, x, y, bx, by, ex, ey = pieces[n]
        src = gin_s.at[block, pl.ds(bx, ex), pl.ds(by, ey)]
        return pltpu.make_async_copy(src, ends[origin].at[pl.ds(x, ex), pl.ds(y, ey)], out_sem.at[n])

    @pl.when(step == 0)
    def _():
        start_all(pieces, arrays, blk_s, in_sem)

    wait_block(pieces, arrays, blk_s, in_sem, step)
    low = lax.broadcasted_iota(jnp.int32, (64, 8, C), 1) < SHIFT
    ones = jnp.full((C, C), 1.0 / C, BF)
    xh, rstd = standardized(blk_s[0, step])
    a = blk_s[1, step].reshape(64, 3, 8, C).astype(F32)
    windows = [pltpu.roll(dot(w_ref[...], dT_ref[z]).T.reshape(64, 8, C), SHIFT, 1) for z in range(3)]
    for z in range(3):
        xhat = xh[:, z].reshape(T, C)
        g = jnp.where(low, windows[(z + 2) % 3], windows[z]).reshape(T, C) * gamma_ref[...]
        mean = dot(g.astype(BF), ones)
        slope = dot((g * xhat).astype(BF), ones)
        grad = a[:, z] + rstd[:, z] * (g - mean - xhat * slope).reshape(64, 8, C)
        gin_s[step, :, :, 8 * z : 8 * z + 8] = grad.astype(BF).reshape(8, 8, 8, C)
    for block in sorted({p[0] for p in pieces}):

        @pl.when(step == block)
        def _(block=block):
            for n, piece in enumerate(pieces):
                if piece[0] == block:
                    leaving(n).start()

    @pl.when(step == pl.num_programs(0) - 1)
    def _():
        for n in range(len(pieces)):
            leaving(n).wait()


def whole(shape):
    return pl.BlockSpec(shape, lambda i: (0,) * len(shape))


ANYWHERE = pl.BlockSpec(memory_space=pl.ANY)
DT_BLOCK = pl.BlockSpec((pl.Squeezed(), 3, 3 * C, T), lambda i: (i, 0, 0, 0))
DT_SHAPE = (3, 3 * C, T)


def sublayer(first, arrays, params, carried=()):
    square = (HEADS, T, T)
    small = (4 * C, C)
    blocks = 1 if first else 3
    pieces = INNER if first else RIM
    ins = [ANYWHERE] * len(arrays) + [whole((1, C)), whole((C, 3 * C)), whole((3 * C, C)), whole((C, C)), ANYWHERE]
    if first:
        outs = [DT_BLOCK, whole(square), whole(small)]
        shapes = [((blocks,) + DT_SHAPE, BF), (square, F32), (small, F32)]
        scratch = []
    else:
        ins += [ANYWHERE, whole(small)]
        outs = [DT_BLOCK, whole((HALF, T)), whole((HALF, T))]
        shapes = [((blocks,) + DT_SHAPE, BF), ((HALF, T), BF), ((HALF, T), F32)]
        scratch = [pltpu.VMEM(square, F32), pltpu.VMEM(small, F32), pltpu.VMEM(square, F32), pltpu.SemaphoreType.DMA]
    scratch += [
        pltpu.SemaphoreType.DMA((2, len(pieces))),
        pltpu.SemaphoreType.DMA((HEADS,)),
        pltpu.VMEM((2, blocks, 8, 8, 24, C), BF),
        pltpu.VMEM(square, F32),
        pltpu.VMEM(square, F32),
        pltpu.VMEM((3, T, C), BF),
        pltpu.VMEM((3, T, C), BF),
        pltpu.VMEM((HEADS, 2 * C, T), BF),
        pltpu.VMEM((HEADS, C, T), BF),
        pltpu.VMEM((T, 2 * C), BF),
        pltpu.VMEM((T, C), BF),
        pltpu.VMEM((C, T), BF),
        pltpu.VMEM((HEADS, 48, T), BF),
        pltpu.VMEM((C, T), BF),
        pltpu.VMEM((C, T), BF),
        pltpu.VMEM((2, T, T), F32),
        pltpu.VMEM((3, T, T), BF),
        pltpu.VMEM((2, T, T), BF),
    ]
    return pl.pallas_call(
        functools.partial(kernel, first),
        grid=(blocks,),
        in_specs=ins,
        out_specs=outs,
        out_shape=[jax.ShapeDtypeStruct(shape, dtype) for shape, dtype in shapes],
        scratch_shapes=scratch,
        compiler_params=pltpu.CompilerParams(vmem_limit_bytes=58 * 1024 * 1024),
        cost_estimate=pl.CostEstimate(flops=blocks * 12 * 10**9, bytes_accessed=blocks * 10**7, transcendentals=0),
        name="inner_windows" if first else "rim_windows",
    )(*arrays, *params, *carried)


def finish(first, arrays, gamma, w, dT, carried=()):
    blocks = 1 if first else 3
    pieces = INNER if first else RIM
    shapes = [(16, 16, 24, C)] if first else [(16, 16, 24, C), (4, 12, 24, C), (12, 4, 24, C), (4, 4, 24, C)]
    return pl.pallas_call(
        functools.partial(finish_kernel, first),
        grid=(blocks,),
        in_specs=[ANYWHERE] * len(arrays) + [whole((1, C)), whole((C, 3 * C)), DT_BLOCK] + [ANYWHERE] * len(carried),
        out_specs=[ANYWHERE] * len(shapes),
        out_shape=[jax.ShapeDtypeStruct(shape, BF) for shape in shapes],
        scratch_shapes=[
            pltpu.SemaphoreType.DMA((2, len(pieces))),
            pltpu.SemaphoreType.DMA((len(pieces),)),
            pltpu.VMEM((2, blocks, 8, 8, 24, C), BF),
            pltpu.VMEM((blocks, 8, 8, 24, C), BF),
        ],
        input_output_aliases={len(arrays) + 3: 0} if first else {},
        compiler_params=pltpu.CompilerParams(vmem_limit_bytes=32 * 1024 * 1024),
        cost_estimate=pl.CostEstimate(flops=blocks * 10**9, bytes_accessed=blocks * 3 * 10**6, transcendentals=0),
        name="inner_finish" if first else "rim_finish",
    )(*arrays, gamma, w, dT, *carried)


def spread_kernel(mine_ref, own_ref, got_ref, out_ref):
    @pl.when(pl.program_id(0) == 0)
    def _():
        out_ref[...] = own_ref[...].astype(F32)

    @pl.when(pl.program_id(0) == 1)
    def _():
        out_ref[...] = got_ref[...].astype(F32)


def spread(mine, own, got):
    return pl.pallas_call(
        spread_kernel,
        grid_spec=pltpu.PrefetchScalarGridSpec(
            num_scalar_prefetch=1,
            grid=(2, 2),
            in_specs=[
                pl.BlockSpec((T, T), lambda s, j, m: (jnp.where(s == 0, j, 1), 0)),
                pl.BlockSpec((T, T), lambda s, j, m: (jnp.where(s == 0, 0, j), 0)),
            ],
            out_specs=pl.BlockSpec((pl.Squeezed(), T, T), lambda s, j, m: (jnp.where(s == 0, m[0], 1 - m[0]) * 2 + j, 0, 0)),
        ),
        out_shape=jax.ShapeDtypeStruct((HEADS, T, T), F32),
        name="spread",
    )(mine.reshape(1), own, got)


def shifted(values, by_x, by_y):
    nx, ny = lax.axis_size("gx"), lax.axis_size("gy")
    if not by_y:
        return lax.ppermute(values, "gx", [(i, (i + by_x) % nx) for i in range(nx)])
    if not by_x:
        return lax.ppermute(values, "gy", [(i, (i + by_y) % ny) for i in range(ny)])
    pairs = [(i * ny + j, (i + by_x) % nx * ny + (j + by_y) % ny) for i in range(nx) for j in range(ny)]
    return lax.ppermute(values, ("gx", "gy"), pairs)


CORE = ("gx", 1, 2)
ACROSS_X = ("gx", 2, 4)
ACROSS_Z = ("gy", 1, 4)
ACROSS_Y = ("y", 0, 4)


def moved(i, j, digit, by):
    axis, stride, size = digit
    if axis == "y":
        y = (j // 4 * 2 + i // 8 + by) % 4
        return y % 2 * 8 + i % 8, y // 2 * 4 + j % 4
    place = i if axis == "gx" else j
    old = place // stride % size
    place += ((old + by) % size - old) * stride
    return (place, j) if axis == "gx" else (i, place)


def send(values, digits, by):
    pairs = []
    for i in range(16):
        for j in range(8):
            k, l = moved(i, j, digits[i % 2], by)
            pairs.append((i * 8 + j, k * 8 + l))
    return lax.ppermute(values, ("gx", "gy"), pairs)


def my_digit(digits):
    gx, gy = lax.axis_index("gx"), lax.axis_index("gy")
    return jnp.where(gx % 2 == 0, *[(gx if axis == "gx" else gy) // stride % size for axis, stride, size in digits])


def scattered(values, digits):
    mine = my_digit(digits)
    rows = values.shape[0] // 4
    got = [send(lax.dynamic_slice_in_dim(values, (mine + by) % 4 * rows, rows).astype(BF), digits, by) for by in (2, 1, 3)]
    values = lax.dynamic_slice_in_dim(values, mine * rows, rows)
    for part in got:
        values = values + part.astype(F32)
    return values


def gathered(values, digits):
    mine = my_digit(digits)
    rows = values.shape[0]
    out = jnp.zeros((4 * rows,) + values.shape[1:], values.dtype)
    out = lax.dynamic_update_slice_in_dim(out, values, mine * rows, 0)
    for by in (2, 1, 3):
        out = lax.dynamic_update_slice_in_dim(out, send(values, digits, by), (mine - by) % 4 * rows, 0)
    return out


def summed(away, keep, beside):
    values = keep + send(away, (CORE, CORE), 1).astype(F32)
    values = scattered(values, (ACROSS_X, ACROSS_Z))
    values = scattered(values, (ACROSS_Z, ACROSS_X))
    values, *beside = lax.optimization_barrier((values, *beside))
    got = {by: send(values, (ACROSS_Y, ACROSS_Y), by) for by in (2, 1, 3)}
    values = ((values + got[2]) + (got[1] + got[3])).astype(BF)
    values = gathered(values, (ACROSS_Z, ACROSS_X))
    values = gathered(values, (ACROSS_X, ACROSS_Z))
    return values, send(values, (CORE, CORE), 1), beside


def body(retained_source, incoming_adjoint, rescale_multiplier, triple_projection_matrix, w_proj, pos_bias):
    both = (retained_source, incoming_adjoint)
    from_x = shifted(jnp.stack([v[:4, 4:] for v in both]), -1, 0)
    from_y = shifted(jnp.stack([v[4:, :4] for v in both]), 0, -1)
    from_xy = shifted(jnp.stack([v[:4, :4] for v in both]), -1, -1)
    w = triple_projection_matrix
    gamma = rescale_multiplier.reshape(1, C)
    params = (gamma, w, w.T, w_proj, pos_bias)
    inner_dT, acc, acc_small = sublayer(True, both, params)
    around = both + (from_x, from_y, from_xy)
    rim_dT, away, keep = sublayer(False, around, params, (acc, acc_small))
    gin, back_x, back_y, back_xy = finish(False, around, gamma, w, rim_dT)
    back = (shifted(back_x, 1, 0), shifted(back_y, 0, 1), shifted(back_xy, 1, 1))
    own, got, back = summed(away, keep, back)
    (gin,) = finish(True, both, gamma, w, inner_dT, (gin,))
    for values, place in zip(back, ((0, 4), (4, 0), (0, 0))):
        gin = lax.dynamic_update_slice(gin, values, place + (0, 0))
    mine = lax.axis_index("gx") % 2
    grad_bias = spread(mine, own, got)
    table = jnp.where(mine == 0, own[2 * T :], got[2 * T :]).astype(F32)
    grad_qkv = table[:, C:]
    gain = jnp.sum(grad_qkv * w.astype(F32), axis=1) / rescale_multiplier
    return (gin, grad_bias, table[:, :C], grad_qkv, gain)


def solution(mesh):
    placed = (P("gx", "gy", None, None), P("gx", "gy", None, None), P(), P(), P(), P())
    return jax.shard_map(
        body,
        mesh=mesh,
        in_specs=placed,
        out_specs=(P("gx", "gy", None, None), P(), P(), P(), P()),
        check_vma=False,
    )
```

```python
import functools
import math

import jax
import jax.numpy as jnp
from jax import lax
from jax.experimental import pallas as pl
from jax.experimental.pallas import tpu as pltpu
from jax.sharding import PartitionSpec as P

HEADS = 4
HD = 32
C = 128
T = 512
KC = 256
HALF = 2 * T + C
SHIFT = 4
SCALE = HD**-0.5
EXPC = SCALE / math.log(2.0)
BLOCKED = -(2.0**100)
F32 = jnp.float32
BF = jnp.bfloat16


def dot(a, b):
    return lax.dot_general(a, b, (((1,), (0,)), ((), ())), preferred_element_type=F32)


def dot_nt(a, b):
    return lax.dot_general(a, b, (((1,), (1,)), ((), ())), preferred_element_type=F32)


def half_bits(shape, dim):
    token = lax.broadcasted_iota(jnp.int32, shape, dim)
    return [lax.shift_right_logical(token, s) & 1 for s in (8, 5, 2)]


def key_regions():
    lane = lax.broadcasted_iota(jnp.int32, (T, C), 1)
    out = jnp.zeros((T, C), F32)
    for n, bit in enumerate(half_bits((T, C), 0)):
        out = jnp.where(lane == 2 * n, bit.astype(F32), out)
        out = jnp.where(lane == 2 * n + 1, 1.0 - bit.astype(F32), out)
    return out.astype(BF)


def query_regions(edges):
    row = lax.broadcasted_iota(jnp.int32, (16, T), 0)
    out = jnp.zeros((16, T), F32)
    for n, (bit, edge) in enumerate(zip(half_bits((16, T), 1), edges)):
        weight = jnp.where(edge, BLOCKED, 0.0)
        out = jnp.where(row == 2 * n, (1.0 - bit.astype(F32)) * weight, out)
        out = jnp.where(row == 2 * n + 1, bit.astype(F32) * weight, out)
    return out.astype(BF)


INNER = [(0, 0, 4, 4, 0, 0, 8, 8)]
RIM = [
    (0, 0, 12, 4, 0, 0, 4, 8),
    (0, 1, 0, 0, 4, 0, 4, 8),
    (1, 0, 4, 12, 0, 0, 8, 4),
    (1, 2, 0, 0, 0, 4, 8, 4),
    (2, 0, 12, 12, 0, 0, 4, 4),
    (2, 1, 0, 8, 4, 0, 4, 4),
    (2, 2, 8, 0, 0, 4, 4, 4),
    (2, 3, 0, 0, 4, 4, 4, 4),
]


def arriving(pieces, arrays, blk_s, sem, n, which):
    block, origin, x, y, bx, by, ex, ey = pieces[n]
    if origin:
        src = arrays[1 + origin].at[which, pl.ds(x, ex), pl.ds(y, ey)]
    else:
        src = arrays[which].at[pl.ds(x, ex), pl.ds(y, ey)]
    return pltpu.make_async_copy(src, blk_s.at[which, block, pl.ds(bx, ex), pl.ds(by, ey)], sem.at[which, n])


def start_all(pieces, arrays, blk_s, sem):
    for n in range(len(pieces)):
        for which in range(2):
            arriving(pieces, arrays, blk_s, sem, n, which).start()


def wait_block(pieces, arrays, blk_s, sem, step):
    for block in sorted({p[0] for p in pieces}):

        @pl.when(step == block)
        def _(block=block):
            for n, piece in enumerate(pieces):
                if piece[0] == block:
                    for which in range(2):
                        arriving(pieces, arrays, blk_s, sem, n, which).wait()


def standardized(block):
    ones = jnp.full((C, C), 1.0 / C, BF)
    flat = block.reshape(64 * 24, C)
    centred = flat.astype(F32) - dot(flat, ones)
    rstd = lax.rsqrt(dot((centred * centred).astype(BF), ones) + 1e-5)
    return (centred * rstd).reshape(64, 3, 8, C), rstd.reshape(64, 3, 8, C)


def kernel(first, *refs):
    pieces = INNER if first else RIM
    arrays = refs[:2] if first else refs[:5]
    refs = refs[len(arrays) :]
    gamma_ref, w_ref, wT_ref, wproj_ref, bias_hbm = refs[:5]
    refs = refs[5:]
    if first:
        dT_ref, dbias_ref, small_ref = refs[:3]
        refs = refs[3:]
    else:
        acc_hbm, accs_ref = refs[:2]
        dT_ref, away_ref, keep_ref = refs[2:5]
        dbias_ref, small_ref, acc_sem = refs[5:8]
        refs = refs[8:]
    (in_sem, bias_sem, blk_s, bias_s, biasT_s, xh_s, adj_s, qext_s, gz_s, kext_s, v_s, kT_s, vT_s, gT_s, attT_s, u_s, e_s, ds_s) = refs
    step = pl.program_id(0)

    def bias_copy(h):
        return pltpu.make_async_copy(bias_hbm.at[h], bias_s.at[h], bias_sem.at[h])

    @pl.when(step == 0)
    def _():
        start_all(pieces, arrays, blk_s, in_sem)
        for h in range(HEADS):
            bias_copy(h).start()
        if first:
            dbias_ref[...] = jnp.zeros_like(dbias_ref)
            small_ref[...] = jnp.zeros_like(small_ref)
        else:
            pltpu.make_async_copy(acc_hbm, dbias_ref, acc_sem).start()
            small_ref[...] = accs_ref[...]
        qext_s[...] = jnp.zeros_like(qext_s)
        gz_s[...] = jnp.zeros_like(gz_s)
        vT_s[...] = jnp.ones_like(vT_s)
        kext_s[:, C:] = key_regions()

    if first:
        edge_x = edge_y = False
    else:
        edge_x = (lax.axis_index("gx") == lax.axis_size("gx") - 1) & (step != 1)
        edge_y = (lax.axis_index("gy") == lax.axis_size("gy") - 1) & (step != 0)
    wait_block(pieces, arrays, blk_s, in_sem, step)
    low = lax.broadcasted_iota(jnp.int32, (64, 8, C), 1) < SHIFT
    xh, _ = standardized(blk_s[0, step])
    a = blk_s[1, step].reshape(64, 3, 8, C).astype(F32)
    for z in range(3):
        z1 = (z + 1) % 3
        xh_s[z] = pltpu.roll(jnp.where(low, xh[:, z1], xh[:, z]) * gamma_ref[...], SHIFT, 1).reshape(T, C).astype(BF)
        adj_s[z] = pltpu.roll(jnp.where(low, a[:, z1], a[:, z]), SHIFT, 1).reshape(T, C).astype(BF)

    @pl.when(step == 0)
    def _():
        for h in range(HEADS):
            bias_copy(h).wait()
            biasT_s[h] = bias_s[h].T * (1.0 / SCALE)
        if not first:
            pltpu.make_async_copy(acc_hbm, dbias_ref, acc_sem).wait()

    def window(z, carry):
        nrm = xh_s[z]
        adj = adj_s[z]
        qkvT = dot_nt(wT_ref[...], nrm).astype(BF)
        kT_s[...] = qkvT[C : 2 * C]
        regions = query_regions((edge_x, edge_y, z == 2))
        for h in range(HEADS):
            vT_s[h, :HD] = qkvT[2 * C + HD * h : 2 * C + HD * (h + 1)]
            qext_s[h, HD * h : HD * (h + 1)] = qkvT[HD * h : HD * (h + 1)]
            qext_s[h, C : C + 16] = regions
        kv = dot(nrm, w_ref[:, C:]).astype(BF)
        kext_s[:, :C] = kv[:, :C]
        v_s[...] = kv[:, C:]
        gT_s[...] = dot_nt(wproj_ref[...], adj).astype(BF)
        chunks = T // KC
        held = {}

        def scores(h, c):
            ks = slice(c * KC, (c + 1) * KC)
            u = dot(kext_s[ks], qext_s[h]) + biasT_s[h, ks]
            u_s[h % 2, ks] = u
            top = jnp.max(u.reshape(KC // 8, 8, T), axis=0)
            held["top", h] = top if c == 0 else jnp.maximum(top, held["top", h])
            if c == chunks - 1:
                held["top", h] = jnp.max(held["top", h], axis=0, keepdims=True)

        def weights(h, c):
            ks = slice(c * KC, (c + 1) * KC)
            e = jnp.exp2((u_s[h % 2, ks] - held["top", h]) * EXPC).astype(BF)
            e_s[h % 3, ks] = e
            o = dot(vT_s[h, :, ks], e)
            held["o", h] = o if c == 0 else o + held["o", h]
            if c == chunks - 1:
                o = held["o", h]
                hs = slice(HD * h, HD * (h + 1))
                inverse = 1.0 / o[HD : HD + 1]
                gs = (gT_s[hs].astype(F32) * inverse).astype(BF)
                attended = o[:HD] * inverse
                attT_s[hs] = attended.astype(BF)
                held["delta", h] = jnp.sum(gs.astype(F32) * attended, axis=0, keepdims=True)
                gz_s[h, hs] = gs

        def score_grads(h, c):
            ks = slice(c * KC, (c + 1) * KC)
            dp = dot(v_s[ks], gz_s[h])
            ds = e_s[h % 3, ks].astype(F32) * (dp - held["delta", h])
            ds_s[h % 2, ks] = ds.astype(BF)
            dbias_ref[h, ks] += ds

        def qkv_grads(h, c):
            hs = slice(HD * h, HD * (h + 1))
            ks = slice(c * KC, (c + 1) * KC)
            dq = dot(kT_s[hs, ks], ds_s[h % 2, ks])
            held["dq", h] = dq if c == 0 else dq + held["dq", h]
            dT_ref[z, C + HD * h : C + HD * (h + 1), ks] = (dot_nt(qext_s[h, hs], ds_s[h % 2, ks]) * SCALE).astype(BF)
            dT_ref[z, 2 * C + HD * h : 2 * C + HD * (h + 1), ks] = dot_nt(gz_s[h, hs], e_s[h % 3, ks]).astype(BF)
            if c == chunks - 1:
                dT_ref[z, hs] = (held["dq", h] * SCALE).astype(BF)

        for turn in range(HEADS + 3):
            for c in range(chunks):
                for lag, stage in ((3, qkv_grads), (2, score_grads), (1, weights), (0, scores)):
                    if 0 <= turn - lag < HEADS:
                        stage(turn - lag, c)
        small_ref[:C] += dot(attT_s[...], adj)
        small_ref[C:] += dot(dT_ref[z], nrm)
        return carry

    lax.fori_loop(0, 3, window, 0)

    if not first:

        @pl.when(step == pl.num_programs(0) - 1)
        def _():
            mine = lax.axis_index("gx") % 2
            table = jnp.concatenate([small_ref[:C], small_ref[C:].T], axis=1)
            for j in range(2):
                away_ref[j * T : (j + 1) * T] = dbias_ref[2 * (1 - mine) + j].T.astype(BF)
                keep_ref[j * T : (j + 1) * T] = dbias_ref[2 * mine + j].T
            away_ref[2 * T :] = jnp.where(mine == 1, table, 0.0).astype(BF)
            keep_ref[2 * T :] = jnp.where(mine == 0, table, 0.0)


def finish_kernel(first, *refs):
    pieces = INNER if first else RIM
    arrays = refs[:2] if first else refs[:5]
    refs = refs[len(arrays) :]
    gamma_ref, w_ref, dT_ref = refs[:3]
    ends = refs[4:5] if first else refs[3:7]
    in_sem, out_sem, blk_s, gin_s = refs[-4:]
    step = pl.program_id(0)

    def leaving(n):
        block, origin, x, y, bx, by, ex, ey = pieces[n]
        src = gin_s.at[block, pl.ds(bx, ex), pl.ds(by, ey)]
        return pltpu.make_async_copy(src, ends[origin].at[pl.ds(x, ex), pl.ds(y, ey)], out_sem.at[n])

    @pl.when(step == 0)
    def _():
        start_all(pieces, arrays, blk_s, in_sem)

    wait_block(pieces, arrays, blk_s, in_sem, step)
    low = lax.broadcasted_iota(jnp.int32, (64, 8, C), 1) < SHIFT
    ones = jnp.full((C, C), 1.0 / C, BF)
    xh, rstd = standardized(blk_s[0, step])
    a = blk_s[1, step].reshape(64, 3, 8, C).astype(F32)
    windows = [pltpu.roll(dot(w_ref[...], dT_ref[z]).T.reshape(64, 8, C), SHIFT, 1) for z in range(3)]
    for z in range(3):
        xhat = xh[:, z].reshape(T, C)
        g = jnp.where(low, windows[(z + 2) % 3], windows[z]).reshape(T, C) * gamma_ref[...]
        mean = dot(g.astype(BF), ones)
        slope = dot((g * xhat).astype(BF), ones)
        grad = a[:, z] + rstd[:, z] * (g - mean - xhat * slope).reshape(64, 8, C)
        gin_s[step, :, :, 8 * z : 8 * z + 8] = grad.astype(BF).reshape(8, 8, 8, C)
    for block in sorted({p[0] for p in pieces}):

        @pl.when(step == block)
        def _(block=block):
            for n, piece in enumerate(pieces):
                if piece[0] == block:
                    leaving(n).start()

    @pl.when(step == pl.num_programs(0) - 1)
    def _():
        for n in range(len(pieces)):
            leaving(n).wait()


def whole(shape):
    return pl.BlockSpec(shape, lambda i: (0,) * len(shape))


ANYWHERE = pl.BlockSpec(memory_space=pl.ANY)
DT_BLOCK = pl.BlockSpec((pl.Squeezed(), 3, 3 * C, T), lambda i: (i, 0, 0, 0))
DT_SHAPE = (3, 3 * C, T)


def sublayer(first, arrays, params, carried=()):
    square = (HEADS, T, T)
    small = (4 * C, C)
    blocks = 1 if first else 3
    pieces = INNER if first else RIM
    ins = [ANYWHERE] * len(arrays) + [whole((1, C)), whole((C, 3 * C)), whole((3 * C, C)), whole((C, C)), ANYWHERE]
    if first:
        outs = [DT_BLOCK, whole(square), whole(small)]
        shapes = [((blocks,) + DT_SHAPE, BF), (square, F32), (small, F32)]
        scratch = []
    else:
        ins += [ANYWHERE, whole(small)]
        outs = [DT_BLOCK, whole((HALF, T)), whole((HALF, T))]
        shapes = [((blocks,) + DT_SHAPE, BF), ((HALF, T), BF), ((HALF, T), F32)]
        scratch = [pltpu.VMEM(square, F32), pltpu.VMEM(small, F32), pltpu.SemaphoreType.DMA]
    scratch += [
        pltpu.SemaphoreType.DMA((2, len(pieces))),
        pltpu.SemaphoreType.DMA((HEADS,)),
        pltpu.VMEM((2, blocks, 8, 8, 24, C), BF),
        pltpu.VMEM(square, F32),
        pltpu.VMEM(square, F32),
        pltpu.VMEM((3, T, C), BF),
        pltpu.VMEM((3, T, C), BF),
        pltpu.VMEM((HEADS, 2 * C, T), BF),
        pltpu.VMEM((HEADS, C, T), BF),
        pltpu.VMEM((T, 2 * C), BF),
        pltpu.VMEM((T, C), BF),
        pltpu.VMEM((C, T), BF),
        pltpu.VMEM((HEADS, 48, T), BF),
        pltpu.VMEM((C, T), BF),
        pltpu.VMEM((C, T), BF),
        pltpu.VMEM((2, T, T), F32),
        pltpu.VMEM((3, T, T), BF),
        pltpu.VMEM((2, T, T), BF),
    ]
    return pl.pallas_call(
        functools.partial(kernel, first),
        grid=(blocks,),
        in_specs=ins,
        out_specs=outs,
        out_shape=[jax.ShapeDtypeStruct(shape, dtype) for shape, dtype in shapes],
        scratch_shapes=scratch,
        compiler_params=pltpu.CompilerParams(vmem_limit_bytes=58 * 1024 * 1024),
        cost_estimate=pl.CostEstimate(flops=blocks * 12 * 10**9, bytes_accessed=blocks * 10**7, transcendentals=0),
        name="inner_windows" if first else "rim_windows",
    )(*arrays, *params, *carried)


def finish(first, arrays, gamma, w, dT, carried=()):
    blocks = 1 if first else 3
    pieces = INNER if first else RIM
    shapes = [(16, 16, 24, C)] if first else [(16, 16, 24, C), (4, 12, 24, C), (12, 4, 24, C), (4, 4, 24, C)]
    return pl.pallas_call(
        functools.partial(finish_kernel, first),
        grid=(blocks,),
        in_specs=[ANYWHERE] * len(arrays) + [whole((1, C)), whole((C, 3 * C)), DT_BLOCK] + [ANYWHERE] * len(carried),
        out_specs=[ANYWHERE] * len(shapes),
        out_shape=[jax.ShapeDtypeStruct(shape, BF) for shape in shapes],
        scratch_shapes=[
            pltpu.SemaphoreType.DMA((2, len(pieces))),
            pltpu.SemaphoreType.DMA((len(pieces),)),
            pltpu.VMEM((2, blocks, 8, 8, 24, C), BF),
            pltpu.VMEM((blocks, 8, 8, 24, C), BF),
        ],
        input_output_aliases={len(arrays) + 3: 0} if first else {},
        compiler_params=pltpu.CompilerParams(vmem_limit_bytes=60 * 1024 * 1024),
        cost_estimate=pl.CostEstimate(flops=blocks * 10**9, bytes_accessed=blocks * 3 * 10**6, transcendentals=0),
        name="inner_finish" if first else "rim_finish",
    )(*arrays, gamma, w, dT, *carried)


def spread_own_kernel(mine_ref, own_ref, out_ref):
    out_ref[...] = own_ref[...].astype(F32)


def spread_own(mine, own):
    return pl.pallas_call(
        spread_own_kernel,
        grid_spec=pltpu.PrefetchScalarGridSpec(
            num_scalar_prefetch=1,
            grid=(2,),
            in_specs=[pl.BlockSpec((T, T), lambda j, m: (j, 0))],
            out_specs=pl.BlockSpec((pl.Squeezed(), T, T), lambda j, m: (2 * m[0] + j, 0, 0)),
        ),
        out_shape=jax.ShapeDtypeStruct((HEADS, T, T), F32),
        name="spread_own",
    )(mine, own)


def spread_got_kernel(mine_ref, got_ref, own_rest_ref, got_rest_ref, gamma_ref, w_ref, _, out_ref, proj_ref, qkv_ref, gain_ref):
    out_ref[...] = got_ref[...].astype(F32)

    @pl.when(pl.program_id(0) == 0)
    def _():
        table = jnp.where(mine_ref[0] == 0, own_rest_ref[...].astype(F32), got_rest_ref[...].astype(F32))
        proj_ref[...] = table[:, :C]
        qkv_ref[...] = table[:, C:]
        along = (table[:, C:] * w_ref[...].astype(F32)).T
        gain_ref[...] = jnp.sum(along, axis=0, keepdims=True) / gamma_ref[...]


def spread_got(mine, own, got, gamma, w, grad_bias):
    rest = pl.BlockSpec((C, T), lambda j, m: (2 * T // C, 0))

    def all_of(shape):
        return pl.BlockSpec(shape, lambda j, m: (0,) * len(shape))

    return pl.pallas_call(
        spread_got_kernel,
        grid_spec=pltpu.PrefetchScalarGridSpec(
            num_scalar_prefetch=1,
            grid=(2,),
            in_specs=[pl.BlockSpec((T, T), lambda j, m: (j, 0)), rest, rest, all_of((1, C)), all_of((C, 3 * C)), ANYWHERE],
            out_specs=[
                pl.BlockSpec((pl.Squeezed(), T, T), lambda j, m: (2 * (1 - m[0]) + j, 0, 0)),
                all_of((C, C)),
                all_of((C, 3 * C)),
                all_of((1, C)),
            ],
        ),
        out_shape=[
            jax.ShapeDtypeStruct((HEADS, T, T), F32),
            jax.ShapeDtypeStruct((C, C), F32),
            jax.ShapeDtypeStruct((C, 3 * C), F32),
            jax.ShapeDtypeStruct((1, C), F32),
        ],
        input_output_aliases={6: 0},
        name="spread_got",
    )(mine, got, own, got, gamma, w, grad_bias)


def shifted(values, by_x, by_y):
    nx, ny = lax.axis_size("gx"), lax.axis_size("gy")
    if not by_y:
        return lax.ppermute(values, "gx", [(i, (i + by_x) % nx) for i in range(nx)])
    if not by_x:
        return lax.ppermute(values, "gy", [(i, (i + by_y) % ny) for i in range(ny)])
    pairs = [(i * ny + j, (i + by_x) % nx * ny + (j + by_y) % ny) for i in range(nx) for j in range(ny)]
    return lax.ppermute(values, ("gx", "gy"), pairs)


CORE = ("gx", 1, 2)
ACROSS_X = ("gx", 2, 4)
ACROSS_Z = ("gy", 1, 4)
ACROSS_Y = ("y", 0, 4)


def moved(i, j, digit, by):
    axis, stride, size = digit
    if axis == "y":
        y = (j // 4 * 2 + i // 8 + by) % 4
        return y % 2 * 8 + i % 8, y // 2 * 4 + j % 4
    place = i if axis == "gx" else j
    old = place // stride % size
    place += ((old + by) % size - old) * stride
    return (place, j) if axis == "gx" else (i, place)


def send(values, digits, by):
    pairs = []
    for i in range(16):
        for j in range(8):
            k, l = moved(i, j, digits[i % 2], by)
            pairs.append((i * 8 + j, k * 8 + l))
    return lax.ppermute(values, ("gx", "gy"), pairs)


def my_digit(digits):
    gx, gy = lax.axis_index("gx"), lax.axis_index("gy")
    return jnp.where(gx % 2 == 0, *[(gx if axis == "gx" else gy) // stride % size for axis, stride, size in digits])


def parts_sent(values, digits):
    mine = my_digit(digits)
    rows = values.shape[0] // 4
    got = [send(lax.dynamic_slice_in_dim(values, (mine + by) % 4 * rows, rows).astype(BF), digits, by) for by in (2, 1, 3)]
    return lax.dynamic_slice_in_dim(values, mine * rows, rows), got


def added(values, got):
    for part in got:
        values = values + part.astype(F32)
    return values


def all_sent(values, digits):
    return {by: send(values, digits, by) for by in (2, 1, 3)}


def gathered(values, got, digits):
    mine = my_digit(digits)
    rows = values.shape[0]
    out = jnp.zeros((4 * rows,) + values.shape[1:], values.dtype)
    out = lax.dynamic_update_slice_in_dim(out, values, mine * rows, 0)
    for by in (2, 1, 3):
        out = lax.dynamic_update_slice_in_dim(out, got[by], (mine - by) % 4 * rows, 0)
    return out


def body(retained_source, incoming_adjoint, rescale_multiplier, triple_projection_matrix, w_proj, pos_bias):
    both = (retained_source, incoming_adjoint)
    from_x = shifted(jnp.stack([v[:4, 4:] for v in both]), -1, 0)
    from_y = shifted(jnp.stack([v[4:, :4] for v in both]), 0, -1)
    from_xy = shifted(jnp.stack([v[:4, :4] for v in both]), -1, -1)
    w = triple_projection_matrix
    gamma = rescale_multiplier.reshape(1, C)
    params = (gamma, w, w.T, w_proj, pos_bias)
    inner_dT, acc, acc_small = sublayer(True, both, params)
    around = both + (from_x, from_y, from_xy)
    rim_dT, away, keep = sublayer(False, around, params, (acc, acc_small))

    first, second, third = (ACROSS_X, ACROSS_Z), (ACROSS_Z, ACROSS_X), (ACROSS_Y, ACROSS_Y)
    values = keep + send(away, (CORE, CORE), 1).astype(F32)
    values, got = parts_sent(values, first)
    gin, back_x, back_y, back_xy = finish(False, around, gamma, w, rim_dT)
    values, got, back_x, back_y, back_xy = lax.optimization_barrier((values, got, back_x, back_y, back_xy))
    back = (shifted(back_x, 1, 0), shifted(back_y, 0, 1), shifted(back_xy, 1, 1))
    values, got = parts_sent(added(values, got), second)
    (gin,) = finish(True, both, gamma, w, inner_dT, (gin,))
    values, got, gin = lax.optimization_barrier((values, got, gin))
    values = added(values, got)
    got = all_sent(values, third)
    values = ((values + got[2]) + (got[1] + got[3])).astype(BF)
    got = all_sent(values, second)
    values, got, back = lax.optimization_barrier((values, got, back))
    values = gathered(values, got, second)
    got = all_sent(values, first)
    for part, place in zip(back, ((0, 4), (4, 0), (0, 0))):
        gin = lax.dynamic_update_slice(gin, part, place + (0, 0))
    values, got, gin = lax.optimization_barrier((values, got, gin))
    own = gathered(values, got, first)
    got = send(own, (CORE, CORE), 1)
    mine = (lax.axis_index("gx") % 2).reshape(1)
    grad_bias = spread_own(mine, own)
    grad_bias, got = lax.optimization_barrier((grad_bias, got))
    grad_bias, grad_proj, grad_qkv, gain = spread_got(mine, own, got, gamma, w, grad_bias)
    return (gin, grad_bias, grad_proj, grad_qkv, gain.reshape(C))


def solution(mesh):
    placed = (P("gx", "gy", None, None), P("gx", "gy", None, None), P(), P(), P(), P())
    return jax.shard_map(
        body,
        mesh=mesh,
        in_specs=placed,
        out_specs=(P("gx", "gy", None, None), P(), P(), P(), P()),
        check_vma=False,
    )
```

```python
import functools
import math

import jax
import jax.numpy as jnp
from jax import lax
from jax.experimental import pallas as pl
from jax.experimental.pallas import tpu as pltpu
from jax.sharding import PartitionSpec as P

HEADS = 4
HD = 32
C = 128
T = 512
KC = 256
HALF = 2 * T + C
SHIFT = 4
SCALE = HD**-0.5
EXPC = SCALE / math.log(2.0)
BLOCKED = -(2.0**100)
F32 = jnp.float32
BF = jnp.bfloat16


def dot(a, b):
    return lax.dot_general(a, b, (((1,), (0,)), ((), ())), preferred_element_type=F32)


def dot_nt(a, b):
    return lax.dot_general(a, b, (((1,), (1,)), ((), ())), preferred_element_type=F32)


def half_bits(shape, dim):
    token = lax.broadcasted_iota(jnp.int32, shape, dim)
    return [lax.shift_right_logical(token, s) & 1 for s in (8, 5, 2)]


def key_regions():
    lane = lax.broadcasted_iota(jnp.int32, (T, C), 1)
    out = jnp.zeros((T, C), F32)
    for n, bit in enumerate(half_bits((T, C), 0)):
        out = jnp.where(lane == 2 * n, bit.astype(F32), out)
        out = jnp.where(lane == 2 * n + 1, 1.0 - bit.astype(F32), out)
    return out.astype(BF)


def query_regions(edges):
    row = lax.broadcasted_iota(jnp.int32, (16, T), 0)
    out = jnp.zeros((16, T), F32)
    for n, (bit, edge) in enumerate(zip(half_bits((16, T), 1), edges)):
        weight = jnp.where(edge, BLOCKED, 0.0)
        out = jnp.where(row == 2 * n, (1.0 - bit.astype(F32)) * weight, out)
        out = jnp.where(row == 2 * n + 1, bit.astype(F32) * weight, out)
    return out.astype(BF)


INNER = [(0, 0, 4, 4, 0, 0, 8, 8)]
RIM = [
    (0, 0, 12, 4, 0, 0, 4, 8),
    (0, 1, 0, 0, 4, 0, 4, 8),
    (1, 0, 4, 12, 0, 0, 8, 4),
    (1, 2, 0, 0, 0, 4, 8, 4),
    (2, 0, 12, 12, 0, 0, 4, 4),
    (2, 1, 0, 8, 4, 0, 4, 4),
    (2, 2, 8, 0, 0, 4, 4, 4),
    (2, 3, 0, 0, 4, 4, 4, 4),
]


def arriving(pieces, arrays, blk_s, sem, n, which):
    block, origin, x, y, bx, by, ex, ey = pieces[n]
    if origin:
        src = arrays[1 + origin].at[which, pl.ds(x, ex), pl.ds(y, ey)]
    else:
        src = arrays[which].at[pl.ds(x, ex), pl.ds(y, ey)]
    return pltpu.make_async_copy(src, blk_s.at[which, block, pl.ds(bx, ex), pl.ds(by, ey)], sem.at[which, n])


def start_all(pieces, arrays, blk_s, sem):
    for n in range(len(pieces)):
        for which in range(2):
            arriving(pieces, arrays, blk_s, sem, n, which).start()


def wait_block(pieces, arrays, blk_s, sem, step):
    for block in sorted({p[0] for p in pieces}):

        @pl.when(step == block)
        def _(block=block):
            for n, piece in enumerate(pieces):
                if piece[0] == block:
                    for which in range(2):
                        arriving(pieces, arrays, blk_s, sem, n, which).wait()


def standardized(block):
    ones = jnp.full((C, C), 1.0 / C, BF)
    flat = block.reshape(64 * 24, C)
    centred = flat.astype(F32) - dot(flat, ones)
    rstd = lax.rsqrt(dot((centred * centred).astype(BF), ones) + 1e-5)
    return (centred * rstd).reshape(64, 3, 8, C), rstd.reshape(64, 3, 8, C)


def kernel(first, *refs):
    pieces = INNER if first else RIM
    arrays = refs[:2] if first else refs[:5]
    refs = refs[len(arrays) :]
    gamma_ref, w_ref, wproj_ref, bias_hbm = refs[:4]
    refs = refs[4:]
    if first:
        dT_ref, small_ref, acc_hbm, biasT_hbm = refs[:4]
        bias_s, out_sem = refs[4:6]
        refs = refs[6:]
    else:
        acc_hbm, accs_ref = refs[:2]
        dT_ref, away_ref, keep_ref = refs[2:5]
        small_ref, acc_s, acc_sem = refs[5:8]
        refs = refs[8:]
    (in_sem, bias_sem, blk_s, dbias_ref, biasT_s, wT_s, xh_s, adj_s, qext_s, gz_s, kext_s, v_s, kT_s, vT_s, gT_s, attT_s, u_s, e_s, ds_s) = refs
    step = pl.program_id(0)

    def bias_copy(h):
        return pltpu.make_async_copy(bias_hbm.at[h], (bias_s if first else biasT_s).at[h], bias_sem.at[h])

    def out_copy(n, h):
        src, dst = ((dbias_ref, acc_hbm), (biasT_s, biasT_hbm))[n]
        return pltpu.make_async_copy(src.at[h], dst.at[h], out_sem.at[n, h])

    @pl.when(step == 0)
    def _():
        start_all(pieces, arrays, blk_s, in_sem)
        for h in range(HEADS):
            bias_copy(h).start()
        if not first:
            pltpu.make_async_copy(acc_hbm, acc_s, acc_sem).start()
            dbias_ref[...] = jnp.zeros_like(dbias_ref)
        small_ref[...] = jnp.zeros_like(small_ref)
        wT_s[...] = w_ref[...].astype(F32).T.astype(BF)
        qext_s[...] = jnp.zeros_like(qext_s)
        gz_s[...] = jnp.zeros_like(gz_s)
        vT_s[...] = jnp.ones_like(vT_s)
        kext_s[:, C:] = key_regions()

    if first:
        edge_x = edge_y = False
    else:
        edge_x = (lax.axis_index("gx") == lax.axis_size("gx") - 1) & (step != 1)
        edge_y = (lax.axis_index("gy") == lax.axis_size("gy") - 1) & (step != 0)
    wait_block(pieces, arrays, blk_s, in_sem, step)
    low = lax.broadcasted_iota(jnp.int32, (64, 8, C), 1) < SHIFT
    xh, _ = standardized(blk_s[0, step])
    a = blk_s[1, step].reshape(64, 3, 8, C).astype(F32)
    for z in range(3):
        z1 = (z + 1) % 3
        xh_s[z] = pltpu.roll(jnp.where(low, xh[:, z1], xh[:, z]) * gamma_ref[...], SHIFT, 1).reshape(T, C).astype(BF)
        adj_s[z] = pltpu.roll(jnp.where(low, a[:, z1], a[:, z]), SHIFT, 1).reshape(T, C).astype(BF)

    if not first:

        @pl.when(step == 0)
        def _():
            for h in range(HEADS):
                bias_copy(h).wait()

    def window(z, opening=False, closing=False):
        nrm = xh_s[z]
        adj = adj_s[z]
        qkvT = dot_nt(wT_s[...], nrm).astype(BF)
        kT_s[...] = qkvT[C : 2 * C]
        regions = query_regions((edge_x, edge_y, z == 2))
        for h in range(HEADS):
            vT_s[h, :HD] = qkvT[2 * C + HD * h : 2 * C + HD * (h + 1)]
            qext_s[h, HD * h : HD * (h + 1)] = qkvT[HD * h : HD * (h + 1)]
            qext_s[h, C : C + 16] = regions
        kv = dot(nrm, w_ref[:, C:]).astype(BF)
        kext_s[:, :C] = kv[:, :C]
        v_s[...] = kv[:, C:]
        gT_s[...] = dot_nt(wproj_ref[...], adj).astype(BF)
        chunks = T // KC
        held = {}

        def scores(h, c):
            ks = slice(c * KC, (c + 1) * KC)
            if opening and c == 0:
                bias_copy(h).wait()
                biasT_s[h] = bias_s[h].T * (1.0 / SCALE)
                out_copy(1, h).start()
            u = dot(kext_s[ks], qext_s[h]) + biasT_s[h, ks]
            u_s[h % 2, ks] = u
            top = jnp.max(u.reshape(KC // 8, 8, T), axis=0)
            held["top", h] = top if c == 0 else jnp.maximum(top, held["top", h])
            if c == chunks - 1:
                held["top", h] = jnp.max(held["top", h], axis=0, keepdims=True)

        def weights(h, c):
            ks = slice(c * KC, (c + 1) * KC)
            e = jnp.exp2((u_s[h % 2, ks] - held["top", h]) * EXPC).astype(BF)
            e_s[h % 3, ks] = e
            o = dot(vT_s[h, :, ks], e)
            held["o", h] = o if c == 0 else o + held["o", h]
            if c == chunks - 1:
                o = held["o", h]
                hs = slice(HD * h, HD * (h + 1))
                inverse = 1.0 / o[HD : HD + 1]
                gs = (gT_s[hs].astype(F32) * inverse).astype(BF)
                attended = o[:HD] * inverse
                attT_s[hs] = attended.astype(BF)
                held["delta", h] = jnp.sum(gs.astype(F32) * attended, axis=0, keepdims=True)
                gz_s[h, hs] = gs

        def score_grads(h, c):
            ks = slice(c * KC, (c + 1) * KC)
            dp = dot(v_s[ks], gz_s[h])
            ds = e_s[h % 3, ks].astype(F32) * (dp - held["delta", h])
            ds_s[h % 2, ks] = ds.astype(BF)
            if opening:
                dbias_ref[h, ks] = ds
            else:
                dbias_ref[h, ks] += ds
            if closing and c == chunks - 1:
                out_copy(0, h).start()

        def qkv_grads(h, c):
            hs = slice(HD * h, HD * (h + 1))
            if c == 0:
                dk = dot_nt(qext_s[h, hs], ds_s[h % 2]) * SCALE
                dT_ref[z, C + HD * h : C + HD * (h + 1)] = dk.astype(BF)
            if c == chunks - 1:
                dT_ref[z, 2 * C + HD * h : 2 * C + HD * (h + 1)] = dot_nt(gz_s[h, hs], e_s[h % 3]).astype(BF)
                dT_ref[z, hs] = (dot(kT_s[hs], ds_s[h % 2]) * SCALE).astype(BF)

        for turn in range(HEADS + 3):
            for c in range(chunks):
                for lag, stage in ((3, qkv_grads), (2, score_grads), (1, weights), (0, scores)):
                    if 0 <= turn - lag < HEADS:
                        stage(turn - lag, c)
        small_ref[:C] += dot(attT_s[...], adj)
        small_ref[C:] += dot(dT_ref[z], nrm)

    if first:
        for z in range(3):
            window(z, opening=z == 0, closing=z == 2)
        for h in range(HEADS):
            for n in range(2):
                out_copy(n, h).wait()
    else:
        lax.fori_loop(0, 3, lambda z, carry: (window(z), carry)[1], 0)

        @pl.when(step == pl.num_programs(0) - 1)
        def _():
            pltpu.make_async_copy(acc_hbm, acc_s, acc_sem).wait()
            mine = lax.axis_index("gx") % 2
            small = small_ref[...] + accs_ref[...]
            table = jnp.concatenate([small[:C], small[C:].T], axis=1)
            for j in range(2):
                h = 2 * (1 - mine) + j
                away_ref[j * T : (j + 1) * T] = (dbias_ref[h] + acc_s[h]).T.astype(BF)
                h = 2 * mine + j
                keep_ref[j * T : (j + 1) * T] = (dbias_ref[h] + acc_s[h]).T
            away_ref[2 * T :] = jnp.where(mine == 1, table, 0.0).astype(BF)
            keep_ref[2 * T :] = jnp.where(mine == 0, table, 0.0)


def finish_kernel(first, *refs):
    pieces = INNER if first else RIM
    arrays = refs[:2] if first else refs[:5]
    refs = refs[len(arrays) :]
    gamma_ref, w_ref, dT_ref = refs[:3]
    ends = refs[4:5] if first else refs[3:7]
    in_sem, out_sem, blk_s, gin_s = refs[-4:]
    step = pl.program_id(0)

    def leaving(n):
        block, origin, x, y, bx, by, ex, ey = pieces[n]
        src = gin_s.at[block, pl.ds(bx, ex), pl.ds(by, ey)]
        return pltpu.make_async_copy(src, ends[origin].at[pl.ds(x, ex), pl.ds(y, ey)], out_sem.at[n])

    @pl.when(step == 0)
    def _():
        start_all(pieces, arrays, blk_s, in_sem)

    wait_block(pieces, arrays, blk_s, in_sem, step)
    low = lax.broadcasted_iota(jnp.int32, (64, 8, C), 1) < SHIFT
    ones = jnp.full((C, C), 1.0 / C, BF)
    xh, rstd = standardized(blk_s[0, step])
    a = blk_s[1, step].reshape(64, 3, 8, C).astype(F32)
    windows = [pltpu.roll(dot(w_ref[...], dT_ref[z]).T.reshape(64, 8, C), SHIFT, 1) for z in range(3)]
    for z in range(3):
        xhat = xh[:, z].reshape(T, C)
        g = jnp.where(low, windows[(z + 2) % 3], windows[z]).reshape(T, C) * gamma_ref[...]
        mean = dot(g.astype(BF), ones)
        slope = dot((g * xhat).astype(BF), ones)
        grad = a[:, z] + rstd[:, z] * (g - mean - xhat * slope).reshape(64, 8, C)
        gin_s[step, :, :, 8 * z : 8 * z + 8] = grad.astype(BF).reshape(8, 8, 8, C)
    for block in sorted({p[0] for p in pieces}):

        @pl.when(step == block)
        def _(block=block):
            for n, piece in enumerate(pieces):
                if piece[0] == block:
                    leaving(n).start()

    @pl.when(step == pl.num_programs(0) - 1)
    def _():
        for n in range(len(pieces)):
            leaving(n).wait()


def whole(shape):
    return pl.BlockSpec(shape, lambda i: (0,) * len(shape))


ANYWHERE = pl.BlockSpec(memory_space=pl.ANY)
DT_BLOCK = pl.BlockSpec((pl.Squeezed(), 3, 3 * C, T), lambda i: (i, 0, 0, 0))
DT_SHAPE = (3, 3 * C, T)


def sublayer(first, arrays, params, carried=()):
    square = (HEADS, T, T)
    small = (4 * C, C)
    blocks = 1 if first else 3
    pieces = INNER if first else RIM
    ins = [ANYWHERE] * len(arrays) + [whole((1, C)), whole((C, 3 * C)), whole((C, C)), ANYWHERE]
    if first:
        outs = [DT_BLOCK, whole(small), ANYWHERE, ANYWHERE]
        shapes = [((blocks,) + DT_SHAPE, BF), (small, F32), (square, F32), (square, F32)]
        scratch = [pltpu.VMEM(square, F32), pltpu.SemaphoreType.DMA((2, HEADS))]
    else:
        ins += [ANYWHERE, whole(small)]
        outs = [DT_BLOCK, whole((HALF, T)), whole((HALF, T))]
        shapes = [((blocks,) + DT_SHAPE, BF), ((HALF, T), BF), ((HALF, T), F32)]
        scratch = [pltpu.VMEM(small, F32), pltpu.VMEM(square, F32), pltpu.SemaphoreType.DMA]
    scratch += [
        pltpu.SemaphoreType.DMA((2, len(pieces))),
        pltpu.SemaphoreType.DMA((HEADS,)),
        pltpu.VMEM((2, blocks, 8, 8, 24, C), BF),
        pltpu.VMEM(square, F32),
        pltpu.VMEM(square, F32),
        pltpu.VMEM((3 * C, C), BF),
        pltpu.VMEM((3, T, C), BF),
        pltpu.VMEM((3, T, C), BF),
        pltpu.VMEM((HEADS, 2 * C, T), BF),
        pltpu.VMEM((HEADS, C, T), BF),
        pltpu.VMEM((T, 2 * C), BF),
        pltpu.VMEM((T, C), BF),
        pltpu.VMEM((C, T), BF),
        pltpu.VMEM((HEADS, 48, T), BF),
        pltpu.VMEM((C, T), BF),
        pltpu.VMEM((C, T), BF),
        pltpu.VMEM((2, T, T), F32),
        pltpu.VMEM((3, T, T), BF),
        pltpu.VMEM((2, T, T), BF),
    ]
    return pl.pallas_call(
        functools.partial(kernel, first),
        grid=(blocks,),
        in_specs=ins,
        out_specs=outs,
        out_shape=[jax.ShapeDtypeStruct(shape, dtype) for shape, dtype in shapes],
        scratch_shapes=scratch,
        compiler_params=pltpu.CompilerParams(vmem_limit_bytes=58 * 1024 * 1024),
        cost_estimate=pl.CostEstimate(flops=blocks * 12 * 10**9, bytes_accessed=blocks * 10**7, transcendentals=0),
        name="inner_windows" if first else "rim_windows",
    )(*arrays, *params, *carried)


def finish(first, arrays, gamma, w, dT, carried=()):
    blocks = 1 if first else 3
    pieces = INNER if first else RIM
    shapes = [(16, 16, 24, C)] if first else [(16, 16, 24, C), (4, 12, 24, C), (12, 4, 24, C), (4, 4, 24, C)]
    return pl.pallas_call(
        functools.partial(finish_kernel, first),
        grid=(blocks,),
        in_specs=[ANYWHERE] * len(arrays) + [whole((1, C)), whole((C, 3 * C)), DT_BLOCK] + [ANYWHERE] * len(carried),
        out_specs=[ANYWHERE] * len(shapes),
        out_shape=[jax.ShapeDtypeStruct(shape, BF) for shape in shapes],
        scratch_shapes=[
            pltpu.SemaphoreType.DMA((2, len(pieces))),
            pltpu.SemaphoreType.DMA((len(pieces),)),
            pltpu.VMEM((2, blocks, 8, 8, 24, C), BF),
            pltpu.VMEM((blocks, 8, 8, 24, C), BF),
        ],
        input_output_aliases={len(arrays) + 3: 0} if first else {},
        compiler_params=pltpu.CompilerParams(vmem_limit_bytes=60 * 1024 * 1024),
        cost_estimate=pl.CostEstimate(flops=blocks * 10**9, bytes_accessed=blocks * 3 * 10**6, transcendentals=0),
        name="inner_finish" if first else "rim_finish",
    )(*arrays, gamma, w, dT, *carried)


def spread_own_kernel(mine_ref, own_ref, out_ref):
    out_ref[...] = own_ref[...].astype(F32)


def spread_own(mine, own):
    return pl.pallas_call(
        spread_own_kernel,
        grid_spec=pltpu.PrefetchScalarGridSpec(
            num_scalar_prefetch=1,
            grid=(2,),
            in_specs=[pl.BlockSpec((T, T), lambda j, m: (j, 0))],
            out_specs=pl.BlockSpec((pl.Squeezed(), T, T), lambda j, m: (2 * m[0] + j, 0, 0)),
        ),
        out_shape=jax.ShapeDtypeStruct((HEADS, T, T), F32),
        compiler_params=pltpu.CompilerParams(vmem_limit_bytes=60 * 1024 * 1024),
        name="spread_own",
    )(mine, own)


def spread_got_kernel(mine_ref, got_ref, own_rest_ref, got_rest_ref, gamma_ref, w_ref, _, out_ref, proj_ref, qkv_ref, gain_ref):
    out_ref[...] = got_ref[...].astype(F32)

    @pl.when(pl.program_id(0) == 0)
    def _():
        table = jnp.where(mine_ref[0] == 0, own_rest_ref[...].astype(F32), got_rest_ref[...].astype(F32))
        proj_ref[...] = table[:, :C]
        qkv_ref[...] = table[:, C:]
        along = (table[:, C:] * w_ref[...].astype(F32)).T
        gain_ref[...] = jnp.sum(along, axis=0, keepdims=True) / gamma_ref[...]


def spread_got(mine, own, got, gamma, w, grad_bias):
    rest = pl.BlockSpec((C, T), lambda j, m: (2 * T // C, 0))

    def all_of(shape):
        return pl.BlockSpec(shape, lambda j, m: (0,) * len(shape))

    return pl.pallas_call(
        spread_got_kernel,
        grid_spec=pltpu.PrefetchScalarGridSpec(
            num_scalar_prefetch=1,
            grid=(2,),
            in_specs=[pl.BlockSpec((T, T), lambda j, m: (j, 0)), rest, rest, all_of((1, C)), all_of((C, 3 * C)), ANYWHERE],
            out_specs=[
                pl.BlockSpec((pl.Squeezed(), T, T), lambda j, m: (2 * (1 - m[0]) + j, 0, 0)),
                all_of((C, C)),
                all_of((C, 3 * C)),
                all_of((1, C)),
            ],
        ),
        out_shape=[
            jax.ShapeDtypeStruct((HEADS, T, T), F32),
            jax.ShapeDtypeStruct((C, C), F32),
            jax.ShapeDtypeStruct((C, 3 * C), F32),
            jax.ShapeDtypeStruct((1, C), F32),
        ],
        input_output_aliases={6: 0},
        compiler_params=pltpu.CompilerParams(vmem_limit_bytes=60 * 1024 * 1024),
        name="spread_got",
    )(mine, got, own, got, gamma, w, grad_bias)


def shifted(values, by_x, by_y):
    nx, ny = lax.axis_size("gx"), lax.axis_size("gy")
    if not by_y:
        return lax.ppermute(values, "gx", [(i, (i + by_x) % nx) for i in range(nx)])
    if not by_x:
        return lax.ppermute(values, "gy", [(i, (i + by_y) % ny) for i in range(ny)])
    pairs = [(i * ny + j, (i + by_x) % nx * ny + (j + by_y) % ny) for i in range(nx) for j in range(ny)]
    return lax.ppermute(values, ("gx", "gy"), pairs)


CORE = ("gx", 1, 2)
ACROSS_X = ("gx", 2, 4)
ACROSS_Z = ("gy", 1, 4)
ACROSS_Y = ("y", 0, 4)


def moved(i, j, digit, by):
    axis, stride, size = digit
    if axis == "y":
        y = (j // 4 * 2 + i // 8 + by) % 4
        return y % 2 * 8 + i % 8, y // 2 * 4 + j % 4
    place = i if axis == "gx" else j
    old = place // stride % size
    place += ((old + by) % size - old) * stride
    return (place, j) if axis == "gx" else (i, place)


def send(values, digits, by):
    pairs = []
    for i in range(16):
        for j in range(8):
            k, l = moved(i, j, digits[i % 2], by)
            pairs.append((i * 8 + j, k * 8 + l))
    return lax.ppermute(values, ("gx", "gy"), pairs)


def my_digit(digits):
    gx, gy = lax.axis_index("gx"), lax.axis_index("gy")
    return jnp.where(gx % 2 == 0, *[(gx if axis == "gx" else gy) // stride % size for axis, stride, size in digits])


def parts_sent(values, digits):
    mine = my_digit(digits)
    rows = values.shape[0] // 4
    got = [send(lax.dynamic_slice_in_dim(values, (mine + by) % 4 * rows, rows).astype(BF), digits, by) for by in (2, 1, 3)]
    return lax.dynamic_slice_in_dim(values, mine * rows, rows), got


def added(values, got):
    for part in got:
        values = values + part.astype(F32)
    return values


def all_sent(values, digits):
    return {by: send(values, digits, by) for by in (2, 1, 3)}


def gathered(values, got, digits):
    mine = my_digit(digits)
    rows = values.shape[0]
    out = jnp.zeros((4 * rows,) + values.shape[1:], values.dtype)
    out = lax.dynamic_update_slice_in_dim(out, values, mine * rows, 0)
    for by in (2, 1, 3):
        out = lax.dynamic_update_slice_in_dim(out, got[by], (mine - by) % 4 * rows, 0)
    return out


def body(retained_source, incoming_adjoint, rescale_multiplier, triple_projection_matrix, w_proj, pos_bias):
    both = (retained_source, incoming_adjoint)
    from_x = shifted(jnp.stack([v[:4, 4:] for v in both]), -1, 0)
    from_y = shifted(jnp.stack([v[4:, :4] for v in both]), 0, -1)
    from_xy = shifted(jnp.stack([v[:4, :4] for v in both]), -1, -1)
    w = triple_projection_matrix
    gamma = rescale_multiplier.reshape(1, C)
    inner_dT, acc_small, acc, biasT = sublayer(True, both, (gamma, w, w_proj, pos_bias))
    around = both + (from_x, from_y, from_xy)
    rim_dT, away, keep = sublayer(False, around, (gamma, w, w_proj, biasT), (acc, acc_small))

    first, second, third = (ACROSS_X, ACROSS_Z), (ACROSS_Z, ACROSS_X), (ACROSS_Y, ACROSS_Y)
    values = keep + send(away, (CORE, CORE), 1).astype(F32)
    values, got = parts_sent(values, first)
    gin, back_x, back_y, back_xy = finish(False, around, gamma, w, rim_dT)
    values, got, back_x, back_y, back_xy = lax.optimization_barrier((values, got, back_x, back_y, back_xy))
    back = (shifted(back_x, 1, 0), shifted(back_y, 0, 1), shifted(back_xy, 1, 1))
    values, got = parts_sent(added(values, got), second)
    values = added(values, got)
    got = all_sent(values, third)
    values = ((values + got[2]) + (got[1] + got[3])).astype(BF)
    got = all_sent(values, second)
    values, got, back = lax.optimization_barrier((values, got, back))
    values = gathered(values, got, second)
    got = all_sent(values, first)
    (gin, inner_dT) = lax.optimization_barrier((gin, inner_dT, values))[:2]
    (gin,) = finish(True, both, gamma, w, inner_dT, (gin,))
    for part, place in zip(back, ((0, 4), (4, 0), (0, 0))):
        gin = lax.dynamic_update_slice(gin, part, place + (0, 0))
    values, got, gin = lax.optimization_barrier((values, got, gin))
    own = gathered(values, got, first)
    got = send(own, (CORE, CORE), 1)
    mine = (lax.axis_index("gx") % 2).reshape(1)
    grad_bias = spread_own(mine, own)
    grad_bias, got = lax.optimization_barrier((grad_bias, got))
    grad_bias, grad_proj, grad_qkv, gain = spread_got(mine, own, got, gamma, w, grad_bias)
    return (gin, grad_bias, grad_proj, grad_qkv, gain.reshape(C))


def solution(mesh):
    placed = (P("gx", "gy", None, None), P("gx", "gy", None, None), P(), P(), P(), P())
    return jax.shard_map(
        body,
        mesh=mesh,
        in_specs=placed,
        out_specs=(P("gx", "gy", None, None), P(), P(), P(), P()),
        check_vma=False,
    )
```

```python
import functools
import math

import jax
import jax.numpy as jnp
from jax import lax
from jax.experimental import pallas as pl
from jax.experimental.pallas import tpu as pltpu
from jax.sharding import PartitionSpec as P

HEADS = 4
HD = 32
C = 128
T = 512
KC = 256
HALF = 2 * T + C
SHIFT = 4
SCALE = HD**-0.5
EXPC = SCALE / math.log(2.0)
BLOCKED = -(2.0**100)
F32 = jnp.float32
BF = jnp.bfloat16


def dot(a, b):
    return lax.dot_general(a, b, (((1,), (0,)), ((), ())), preferred_element_type=F32)


def dot_nt(a, b):
    return lax.dot_general(a, b, (((1,), (1,)), ((), ())), preferred_element_type=F32)


def half_bits(shape, dim):
    token = lax.broadcasted_iota(jnp.int32, shape, dim)
    return [lax.shift_right_logical(token, s) & 1 for s in (8, 5, 2)]


def key_regions():
    lane = lax.broadcasted_iota(jnp.int32, (T, C), 1)
    out = jnp.zeros((T, C), F32)
    for n, bit in enumerate(half_bits((T, C), 0)):
        out = jnp.where(lane == 2 * n, bit.astype(F32), out)
        out = jnp.where(lane == 2 * n + 1, 1.0 - bit.astype(F32), out)
    return out.astype(BF)


def query_regions(edges):
    row = lax.broadcasted_iota(jnp.int32, (16, T), 0)
    out = jnp.zeros((16, T), F32)
    for n, (bit, edge) in enumerate(zip(half_bits((16, T), 1), edges)):
        weight = jnp.where(edge, BLOCKED, 0.0)
        out = jnp.where(row == 2 * n, (1.0 - bit.astype(F32)) * weight, out)
        out = jnp.where(row == 2 * n + 1, bit.astype(F32) * weight, out)
    return out.astype(BF)


INNER = [(0, 0, 4, 4, 0, 0, 8, 8)]
RIM = [
    (0, 0, 12, 4, 0, 0, 4, 8),
    (0, 1, 0, 0, 4, 0, 4, 8),
    (1, 0, 4, 12, 0, 0, 8, 4),
    (1, 2, 0, 0, 0, 4, 8, 4),
    (2, 0, 12, 12, 0, 0, 4, 4),
    (2, 1, 0, 8, 4, 0, 4, 4),
    (2, 2, 8, 0, 0, 4, 4, 4),
    (2, 3, 0, 0, 4, 4, 4, 4),
]


def arriving(pieces, arrays, blk_s, sem, n, which):
    block, origin, x, y, bx, by, ex, ey = pieces[n]
    if origin:
        src = arrays[1 + origin].at[which, pl.ds(x, ex), pl.ds(y, ey)]
    else:
        src = arrays[which].at[pl.ds(x, ex), pl.ds(y, ey)]
    return pltpu.make_async_copy(src, blk_s.at[which, block, pl.ds(bx, ex), pl.ds(by, ey)], sem.at[which, n])


def start_all(pieces, arrays, blk_s, sem):
    for n in range(len(pieces)):
        for which in range(2):
            arriving(pieces, arrays, blk_s, sem, n, which).start()


def wait_block(pieces, arrays, blk_s, sem, step):
    for block in sorted({p[0] for p in pieces}):

        @pl.when(step == block)
        def _(block=block):
            for n, piece in enumerate(pieces):
                if piece[0] == block:
                    for which in range(2):
                        arriving(pieces, arrays, blk_s, sem, n, which).wait()


def standardized(block):
    ones = jnp.full((C, C), 1.0 / C, BF)
    flat = block.reshape(64 * 24, C)
    centred = flat.astype(F32) - dot(flat, ones)
    rstd = lax.rsqrt(dot((centred * centred).astype(BF), ones) + 1e-5)
    return (centred * rstd).reshape(64, 3, 8, C), rstd.reshape(64, 3, 8, C)


def kernel(first, *refs):
    pieces = INNER if first else RIM
    arrays = refs[:2] if first else refs[:5]
    refs = refs[len(arrays) :]
    gamma_ref, w_ref, wproj_ref, bias_hbm = refs[:4]
    refs = refs[4:]
    if first:
        dT_ref, small_ref, acc_hbm, biasT_hbm = refs[:4]
        bias_s, out_sem = refs[4:6]
        refs = refs[6:]
    else:
        acc_hbm, accs_ref = refs[:2]
        dT_ref, away_ref, keep_ref = refs[2:5]
        small_ref, acc_s, acc_sem = refs[5:8]
        refs = refs[8:]
    (in_sem, bias_sem, blk_s, dbias_ref, biasT_s, wT_s, xh_s, adj_s, qext_s, gz_s, kext_s, v_s, kT_s, vT_s, gT_s, attT_s, u_s, e_s, ds_s) = refs
    step = pl.program_id(0)

    def bias_copy(h):
        return pltpu.make_async_copy(bias_hbm.at[h], (bias_s if first else biasT_s).at[h], bias_sem.at[h])

    def out_copy(n, h):
        src, dst = ((dbias_ref, acc_hbm), (biasT_s, biasT_hbm))[n]
        return pltpu.make_async_copy(src.at[h], dst.at[h], out_sem.at[n, h])

    @pl.when(step == 0)
    def _():
        start_all(pieces, arrays, blk_s, in_sem)
        for h in range(HEADS):
            bias_copy(h).start()
        if not first:
            pltpu.make_async_copy(acc_hbm, acc_s, acc_sem).start()
            dbias_ref[...] = jnp.zeros_like(dbias_ref)
        small_ref[...] = jnp.zeros_like(small_ref)
        wT_s[...] = w_ref[...].astype(F32).T.astype(BF)
        qext_s[...] = jnp.zeros_like(qext_s)
        gz_s[...] = jnp.zeros_like(gz_s)
        vT_s[...] = jnp.ones_like(vT_s)
        kext_s[:, C:] = key_regions()

    if first:
        edge_x = edge_y = False
    else:
        edge_x = (lax.axis_index("gx") == lax.axis_size("gx") - 1) & (step != 1)
        edge_y = (lax.axis_index("gy") == lax.axis_size("gy") - 1) & (step != 0)
    wait_block(pieces, arrays, blk_s, in_sem, step)
    low = lax.broadcasted_iota(jnp.int32, (64, 8, C), 1) < SHIFT
    xh, _ = standardized(blk_s[0, step])
    a = blk_s[1, step].reshape(64, 3, 8, C).astype(F32)
    for z in range(3):
        z1 = (z + 1) % 3
        xh_s[z] = pltpu.roll(jnp.where(low, xh[:, z1], xh[:, z]) * gamma_ref[...], SHIFT, 1).reshape(T, C).astype(BF)
        adj_s[z] = pltpu.roll(jnp.where(low, a[:, z1], a[:, z]), SHIFT, 1).reshape(T, C).astype(BF)

    if not first:

        @pl.when(step == 0)
        def _():
            for h in range(HEADS):
                bias_copy(h).wait()

    def window(z, opening=False, closing=False):
        nrm = xh_s[z]
        adj = adj_s[z]
        qkvT = dot_nt(wT_s[...], nrm).astype(BF)
        kT_s[...] = qkvT[C : 2 * C]
        regions = query_regions((edge_x, edge_y, z == 2))
        for h in range(HEADS):
            vT_s[h, :HD] = qkvT[2 * C + HD * h : 2 * C + HD * (h + 1)]
            qext_s[h, HD * h : HD * (h + 1)] = qkvT[HD * h : HD * (h + 1)]
            qext_s[h, C : C + 16] = regions
        kv = dot(nrm, w_ref[:, C:]).astype(BF)
        kext_s[:, :C] = kv[:, :C]
        v_s[...] = kv[:, C:]
        gT_s[...] = dot_nt(wproj_ref[...], adj).astype(BF)
        chunks = T // KC
        held = {}

        def scores(h, c):
            ks = slice(c * KC, (c + 1) * KC)
            if opening and c == 0:
                bias_copy(h).wait()
                biasT_s[h] = bias_s[h].T * (1.0 / SCALE)
                out_copy(1, h).start()
            u = dot(kext_s[ks], qext_s[h]) + biasT_s[h, ks]
            u_s[h % 2, ks] = u
            top = jnp.max(u.reshape(KC // 8, 8, T), axis=0)
            held["top", h] = top if c == 0 else jnp.maximum(top, held["top", h])
            if c == chunks - 1:
                held["top", h] = jnp.max(held["top", h], axis=0, keepdims=True)

        def weights(h, c):
            ks = slice(c * KC, (c + 1) * KC)
            e = jnp.exp2((u_s[h % 2, ks] - held["top", h]) * EXPC).astype(BF)
            e_s[h % 3, ks] = e
            o = dot(vT_s[h, :, ks], e)
            held["o", h] = o if c == 0 else o + held["o", h]
            if c == chunks - 1:
                o = held["o", h]
                hs = slice(HD * h, HD * (h + 1))
                inverse = 1.0 / o[HD : HD + 1]
                gs = (gT_s[hs].astype(F32) * inverse).astype(BF)
                attended = o[:HD] * inverse
                attT_s[hs] = attended.astype(BF)
                held["delta", h] = jnp.sum(gs.astype(F32) * attended, axis=0, keepdims=True)
                gz_s[h, hs] = gs

        def score_grads(h, c):
            ks = slice(c * KC, (c + 1) * KC)
            dp = dot(v_s[ks], gz_s[h])
            ds = e_s[h % 3, ks].astype(F32) * (dp - held["delta", h])
            ds_s[h % 2, ks] = ds.astype(BF)
            if opening:
                dbias_ref[h, ks] = ds
            else:
                dbias_ref[h, ks] += ds
            if closing and c == chunks - 1:
                out_copy(0, h).start()

        def qkv_grads(h, c):
            hs = slice(HD * h, HD * (h + 1))
            if c == 0:
                dk = dot_nt(qext_s[h, hs], ds_s[h % 2]) * SCALE
                dT_ref[z, C + HD * h : C + HD * (h + 1)] = dk.astype(BF)
            if c == chunks - 1:
                dT_ref[z, 2 * C + HD * h : 2 * C + HD * (h + 1)] = dot_nt(gz_s[h, hs], e_s[h % 3]).astype(BF)
                dT_ref[z, hs] = (dot(kT_s[hs], ds_s[h % 2]) * SCALE).astype(BF)

        for turn in range(HEADS + 3):
            for c in range(chunks):
                for lag, stage in ((3, qkv_grads), (2, score_grads), (1, weights), (0, scores)):
                    if 0 <= turn - lag < HEADS:
                        stage(turn - lag, c)
        small_ref[:C] += dot(attT_s[...], adj)
        small_ref[C:] += dot(dT_ref[z], nrm)

    if first:
        for z in range(3):
            window(z, opening=z == 0, closing=z == 2)
        for h in range(HEADS):
            for n in range(2):
                out_copy(n, h).wait()
    else:
        lax.fori_loop(0, 3, lambda z, carry: (window(z), carry)[1], 0)

        @pl.when(step == pl.num_programs(0) - 1)
        def _():
            pltpu.make_async_copy(acc_hbm, acc_s, acc_sem).wait()
            mine = lax.axis_index("gx") % 2
            small = small_ref[...] + accs_ref[...]
            table = jnp.concatenate([small[:C], small[C:].T], axis=1)
            for j in range(2):
                h = 2 * (1 - mine) + j
                away_ref[j * T : (j + 1) * T] = (dbias_ref[h] + acc_s[h]).T.astype(BF)
                h = 2 * mine + j
                keep_ref[j * T : (j + 1) * T] = (dbias_ref[h] + acc_s[h]).T.astype(BF)
            away_ref[2 * T :] = jnp.where(mine == 1, table, 0.0).astype(BF)
            keep_ref[2 * T :] = jnp.where(mine == 0, table, 0.0).astype(BF)


def finish_kernel(first, *refs):
    pieces = INNER if first else RIM
    arrays = refs[:2] if first else refs[:5]
    refs = refs[len(arrays) :]
    gamma_ref, w_ref, dT_ref = refs[:3]
    ends = refs[4:5] if first else refs[3:7]
    in_sem, out_sem, blk_s, gin_s = refs[-4:]
    step = pl.program_id(0)

    def leaving(n):
        block, origin, x, y, bx, by, ex, ey = pieces[n]
        src = gin_s.at[block, pl.ds(bx, ex), pl.ds(by, ey)]
        return pltpu.make_async_copy(src, ends[origin].at[pl.ds(x, ex), pl.ds(y, ey)], out_sem.at[n])

    @pl.when(step == 0)
    def _():
        start_all(pieces, arrays, blk_s, in_sem)

    wait_block(pieces, arrays, blk_s, in_sem, step)
    low = lax.broadcasted_iota(jnp.int32, (64, 8, C), 1) < SHIFT
    ones = jnp.full((C, C), 1.0 / C, BF)
    xh, rstd = standardized(blk_s[0, step])
    a = blk_s[1, step].reshape(64, 3, 8, C).astype(F32)
    windows = [pltpu.roll(dot(w_ref[...], dT_ref[z]).T.reshape(64, 8, C), SHIFT, 1) for z in range(3)]
    for z in range(3):
        xhat = xh[:, z].reshape(T, C)
        g = jnp.where(low, windows[(z + 2) % 3], windows[z]).reshape(T, C) * gamma_ref[...]
        mean = dot(g.astype(BF), ones)
        slope = dot((g * xhat).astype(BF), ones)
        grad = a[:, z] + rstd[:, z] * (g - mean - xhat * slope).reshape(64, 8, C)
        gin_s[step, :, :, 8 * z : 8 * z + 8] = grad.astype(BF).reshape(8, 8, 8, C)
    for block in sorted({p[0] for p in pieces}):

        @pl.when(step == block)
        def _(block=block):
            for n, piece in enumerate(pieces):
                if piece[0] == block:
                    leaving(n).start()

    @pl.when(step == pl.num_programs(0) - 1)
    def _():
        for n in range(len(pieces)):
            leaving(n).wait()


def whole(shape):
    return pl.BlockSpec(shape, lambda i: (0,) * len(shape))


ANYWHERE = pl.BlockSpec(memory_space=pl.ANY)
DT_BLOCK = pl.BlockSpec((pl.Squeezed(), 3, 3 * C, T), lambda i: (i, 0, 0, 0))
DT_SHAPE = (3, 3 * C, T)


def sublayer(first, arrays, params, carried=()):
    square = (HEADS, T, T)
    small = (4 * C, C)
    blocks = 1 if first else 3
    pieces = INNER if first else RIM
    ins = [ANYWHERE] * len(arrays) + [whole((1, C)), whole((C, 3 * C)), whole((C, C)), ANYWHERE]
    if first:
        outs = [DT_BLOCK, whole(small), ANYWHERE, ANYWHERE]
        shapes = [((blocks,) + DT_SHAPE, BF), (small, F32), (square, F32), (square, F32)]
        scratch = [pltpu.VMEM(square, F32), pltpu.SemaphoreType.DMA((2, HEADS))]
    else:
        ins += [ANYWHERE, whole(small)]
        outs = [DT_BLOCK, whole((HALF, T)), whole((HALF, T))]
        shapes = [((blocks,) + DT_SHAPE, BF), ((HALF, T), BF), ((HALF, T), BF)]
        scratch = [pltpu.VMEM(small, F32), pltpu.VMEM(square, F32), pltpu.SemaphoreType.DMA]
    scratch += [
        pltpu.SemaphoreType.DMA((2, len(pieces))),
        pltpu.SemaphoreType.DMA((HEADS,)),
        pltpu.VMEM((2, blocks, 8, 8, 24, C), BF),
        pltpu.VMEM(square, F32),
        pltpu.VMEM(square, F32),
        pltpu.VMEM((3 * C, C), BF),
        pltpu.VMEM((3, T, C), BF),
        pltpu.VMEM((3, T, C), BF),
        pltpu.VMEM((HEADS, 2 * C, T), BF),
        pltpu.VMEM((HEADS, C, T), BF),
        pltpu.VMEM((T, 2 * C), BF),
        pltpu.VMEM((T, C), BF),
        pltpu.VMEM((C, T), BF),
        pltpu.VMEM((HEADS, 48, T), BF),
        pltpu.VMEM((C, T), BF),
        pltpu.VMEM((C, T), BF),
        pltpu.VMEM((2, T, T), F32),
        pltpu.VMEM((3, T, T), BF),
        pltpu.VMEM((2, T, T), BF),
    ]
    return pl.pallas_call(
        functools.partial(kernel, first),
        grid=(blocks,),
        in_specs=ins,
        out_specs=outs,
        out_shape=[jax.ShapeDtypeStruct(shape, dtype) for shape, dtype in shapes],
        scratch_shapes=scratch,
        compiler_params=pltpu.CompilerParams(vmem_limit_bytes=58 * 1024 * 1024),
        cost_estimate=pl.CostEstimate(flops=blocks * 12 * 10**9, bytes_accessed=blocks * 10**7, transcendentals=0),
        name="inner_windows" if first else "rim_windows",
    )(*arrays, *params, *carried)


def finish(first, arrays, gamma, w, dT, carried=()):
    blocks = 1 if first else 3
    pieces = INNER if first else RIM
    shapes = [(16, 16, 24, C)] if first else [(16, 16, 24, C), (4, 12, 24, C), (12, 4, 24, C), (4, 4, 24, C)]
    return pl.pallas_call(
        functools.partial(finish_kernel, first),
        grid=(blocks,),
        in_specs=[ANYWHERE] * len(arrays) + [whole((1, C)), whole((C, 3 * C)), DT_BLOCK] + [ANYWHERE] * len(carried),
        out_specs=[ANYWHERE] * len(shapes),
        out_shape=[jax.ShapeDtypeStruct(shape, BF) for shape in shapes],
        scratch_shapes=[
            pltpu.SemaphoreType.DMA((2, len(pieces))),
            pltpu.SemaphoreType.DMA((len(pieces),)),
            pltpu.VMEM((2, blocks, 8, 8, 24, C), BF),
            pltpu.VMEM((blocks, 8, 8, 24, C), BF),
        ],
        input_output_aliases={len(arrays) + 3: 0} if first else {},
        compiler_params=pltpu.CompilerParams(vmem_limit_bytes=60 * 1024 * 1024),
        cost_estimate=pl.CostEstimate(flops=blocks * 10**9, bytes_accessed=blocks * 3 * 10**6, transcendentals=0),
        name="inner_finish" if first else "rim_finish",
    )(*arrays, gamma, w, dT, *carried)


def spread_own_kernel(mine_ref, own_ref, out_ref):
    out_ref[...] = own_ref[...].astype(F32)


def spread_own(mine, own):
    return pl.pallas_call(
        spread_own_kernel,
        grid_spec=pltpu.PrefetchScalarGridSpec(
            num_scalar_prefetch=1,
            grid=(2,),
            in_specs=[pl.BlockSpec((T, T), lambda j, m: (j, 0))],
            out_specs=pl.BlockSpec((pl.Squeezed(), T, T), lambda j, m: (2 * m[0] + j, 0, 0)),
        ),
        out_shape=jax.ShapeDtypeStruct((HEADS, T, T), F32),
        compiler_params=pltpu.CompilerParams(vmem_limit_bytes=8 * 1024 * 1024),
        name="spread_own",
    )(mine, own)


def spread_got_kernel(mine_ref, got_ref, own_rest_ref, got_rest_ref, gamma_ref, w_ref, _, out_ref, proj_ref, qkv_ref, gain_ref):
    out_ref[...] = got_ref[...].astype(F32)

    @pl.when(pl.program_id(0) == 0)
    def _():
        table = jnp.where(mine_ref[0] == 0, own_rest_ref[...].astype(F32), got_rest_ref[...].astype(F32))
        proj_ref[...] = table[:, :C]
        qkv_ref[...] = table[:, C:]
        along = (table[:, C:] * w_ref[...].astype(F32)).T
        gain_ref[...] = jnp.sum(along, axis=0, keepdims=True) / gamma_ref[...]


def spread_got(mine, own, got, gamma, w, grad_bias):
    rest = pl.BlockSpec((C, T), lambda j, m: (2 * T // C, 0))

    def all_of(shape):
        return pl.BlockSpec(shape, lambda j, m: (0,) * len(shape))

    return pl.pallas_call(
        spread_got_kernel,
        grid_spec=pltpu.PrefetchScalarGridSpec(
            num_scalar_prefetch=1,
            grid=(2,),
            in_specs=[pl.BlockSpec((T, T), lambda j, m: (j, 0)), rest, rest, all_of((1, C)), all_of((C, 3 * C)), ANYWHERE],
            out_specs=[
                pl.BlockSpec((pl.Squeezed(), T, T), lambda j, m: (2 * (1 - m[0]) + j, 0, 0)),
                all_of((C, C)),
                all_of((C, 3 * C)),
                all_of((1, C)),
            ],
        ),
        out_shape=[
            jax.ShapeDtypeStruct((HEADS, T, T), F32),
            jax.ShapeDtypeStruct((C, C), F32),
            jax.ShapeDtypeStruct((C, 3 * C), F32),
            jax.ShapeDtypeStruct((1, C), F32),
        ],
        input_output_aliases={6: 0},
        compiler_params=pltpu.CompilerParams(vmem_limit_bytes=8 * 1024 * 1024),
        name="spread_got",
    )(mine, got, own, got, gamma, w, grad_bias)


def rims_kernel(xs_hbm, adj_hbm, to_x, to_y, to_xy, sem):
    copies = []
    for which, src in enumerate((xs_hbm, adj_hbm)):
        for n, (dst, x, y, ex, ey) in enumerate(((to_x, 0, 4, 4, 12), (to_y, 4, 0, 12, 4), (to_xy, 0, 0, 4, 4))):
            part = src.at[pl.ds(x, ex), pl.ds(y, ey)]
            copies.append(pltpu.make_async_copy(part, dst.at[which], sem.at[which, n]))
    for copy in copies:
        copy.start()
    for copy in copies:
        copy.wait()


def rims(both):
    return pl.pallas_call(
        rims_kernel,
        in_specs=[ANYWHERE] * 2,
        out_specs=[ANYWHERE] * 3,
        out_shape=[jax.ShapeDtypeStruct((2,) + shape + (24, C), BF) for shape in ((4, 12), (12, 4), (4, 4))],
        scratch_shapes=[pltpu.SemaphoreType.DMA((2, 3))],
        compiler_params=pltpu.CompilerParams(vmem_limit_bytes=60 * 1024 * 1024),
        name="rims",
    )(*both)


def shifted(values, by_x, by_y):
    nx, ny = lax.axis_size("gx"), lax.axis_size("gy")
    if not by_y:
        return lax.ppermute(values, "gx", [(i, (i + by_x) % nx) for i in range(nx)])
    if not by_x:
        return lax.ppermute(values, "gy", [(i, (i + by_y) % ny) for i in range(ny)])
    pairs = [(i * ny + j, (i + by_x) % nx * ny + (j + by_y) % ny) for i in range(nx) for j in range(ny)]
    return lax.ppermute(values, ("gx", "gy"), pairs)


CORE = ("gx", 1, 2)
ACROSS_X = ("gx", 2, 4)
ACROSS_Z = ("gy", 1, 4)
ACROSS_Y = ("y", 0, 4)


def moved(i, j, digit, by):
    axis, stride, size = digit
    if axis == "y":
        y = (j // 4 * 2 + i // 8 + by) % 4
        return y % 2 * 8 + i % 8, y // 2 * 4 + j % 4
    place = i if axis == "gx" else j
    old = place // stride % size
    place += ((old + by) % size - old) * stride
    return (place, j) if axis == "gx" else (i, place)


def send(values, digits, by):
    pairs = []
    for i in range(16):
        for j in range(8):
            k, l = moved(i, j, digits[i % 2], by)
            pairs.append((i * 8 + j, k * 8 + l))
    return lax.ppermute(values, ("gx", "gy"), pairs)


def my_digit(digits):
    gx, gy = lax.axis_index("gx"), lax.axis_index("gy")
    return jnp.where(gx % 2 == 0, *[(gx if axis == "gx" else gy) // stride % size for axis, stride, size in digits])


def parts_sent(values, digits):
    mine = my_digit(digits)
    rows = values.shape[0] // 4
    got = [send(lax.dynamic_slice_in_dim(values, (mine + by) % 4 * rows, rows).astype(BF), digits, by) for by in (2, 1, 3)]
    return lax.dynamic_slice_in_dim(values, mine * rows, rows), got


def added(values, got):
    for part in got:
        values = values + part.astype(F32)
    return values


def all_sent(values, digits):
    return {by: send(values, digits, by) for by in (2, 1, 3)}


def gathered(values, got, digits):
    mine = my_digit(digits)
    rows = values.shape[0]
    out = jnp.zeros((4 * rows,) + values.shape[1:], values.dtype)
    out = lax.dynamic_update_slice_in_dim(out, values, mine * rows, 0)
    for by in (2, 1, 3):
        out = lax.dynamic_update_slice_in_dim(out, got[by], (mine - by) % 4 * rows, 0)
    return out


def body(retained_source, incoming_adjoint, rescale_multiplier, triple_projection_matrix, w_proj, pos_bias):
    both = (retained_source, incoming_adjoint)
    to_x, to_y, to_xy = rims(both)
    from_x, from_y, from_xy = shifted(to_x, -1, 0), shifted(to_y, 0, -1), shifted(to_xy, -1, -1)
    w = triple_projection_matrix
    gamma = rescale_multiplier.reshape(1, C)
    inner_dT, acc_small, acc, biasT = sublayer(True, both, (gamma, w, w_proj, pos_bias))
    around = both + (from_x, from_y, from_xy)
    rim_dT, away, keep = sublayer(False, around, (gamma, w, w_proj, biasT), (acc, acc_small))

    first, second, third = (ACROSS_X, ACROSS_Z), (ACROSS_Z, ACROSS_X), (ACROSS_Y, ACROSS_Y)
    values = keep.astype(F32) + send(away, (CORE, CORE), 1).astype(F32)
    values, got = parts_sent(values, first)
    gin, back_x, back_y, back_xy = finish(False, around, gamma, w, rim_dT)
    values, got, back_x, back_y, back_xy = lax.optimization_barrier((values, got, back_x, back_y, back_xy))
    back = (shifted(back_x, 1, 0), shifted(back_y, 0, 1), shifted(back_xy, 1, 1))
    values, got = parts_sent(added(values, got), second)
    values = added(values, got)
    got = all_sent(values, third)
    values = ((values + got[2]) + (got[1] + got[3])).astype(BF)
    got = all_sent(values, second)
    values, got, back = lax.optimization_barrier((values, got, back))
    values = gathered(values, got, second)
    got = all_sent(values, first)
    (gin, inner_dT) = lax.optimization_barrier((gin, inner_dT, values))[:2]
    (gin,) = finish(True, both, gamma, w, inner_dT, (gin,))
    for part, place in zip(back, ((0, 4), (4, 0), (0, 0))):
        gin = lax.dynamic_update_slice(gin, part, place + (0, 0))
    values, got, gin = lax.optimization_barrier((values, got, gin))
    own = gathered(values, got, first)
    got = send(own, (CORE, CORE), 1)
    mine = (lax.axis_index("gx") % 2).reshape(1)
    grad_bias = spread_own(mine, own)
    grad_bias, got = lax.optimization_barrier((grad_bias, got))
    grad_bias, grad_proj, grad_qkv, gain = spread_got(mine, own, got, gamma, w, grad_bias)
    return (gin, grad_bias, grad_proj, grad_qkv, gain.reshape(C))


def solution(mesh):
    placed = (P("gx", "gy", None, None), P("gx", "gy", None, None), P(), P(), P(), P())
    return jax.shard_map(
        body,
        mesh=mesh,
        in_specs=placed,
        out_specs=(P("gx", "gy", None, None), P(), P(), P(), P()),
        check_vma=False,
    )
```

```python
import functools
import math

import jax
import jax.numpy as jnp
from jax import lax
from jax.experimental import pallas as pl
from jax.experimental.pallas import tpu as pltpu
from jax.sharding import PartitionSpec as P

HEADS = 4
HD = 32
C = 128
T = 512
KC = 256
HALF = 2 * T + C
SHIFT = 4
SCALE = HD**-0.5
EXPC = SCALE / math.log(2.0)
BLOCKED = -(2.0**100)
F32 = jnp.float32
BF = jnp.bfloat16


def dot(a, b):
    return lax.dot_general(a, b, (((1,), (0,)), ((), ())), preferred_element_type=F32)


def dot_nt(a, b):
    return lax.dot_general(a, b, (((1,), (1,)), ((), ())), preferred_element_type=F32)


def half_bits(shape, dim):
    token = lax.broadcasted_iota(jnp.int32, shape, dim)
    return [lax.shift_right_logical(token, s) & 1 for s in (8, 5, 2)]


def key_regions():
    lane = lax.broadcasted_iota(jnp.int32, (T, C), 1)
    out = jnp.zeros((T, C), F32)
    for n, bit in enumerate(half_bits((T, C), 0)):
        out = jnp.where(lane == 2 * n, bit.astype(F32), out)
        out = jnp.where(lane == 2 * n + 1, 1.0 - bit.astype(F32), out)
    return out.astype(BF)


def query_regions(edges):
    row = lax.broadcasted_iota(jnp.int32, (16, T), 0)
    out = jnp.zeros((16, T), F32)
    for n, (bit, edge) in enumerate(zip(half_bits((16, T), 1), edges)):
        weight = jnp.where(edge, BLOCKED, 0.0)
        out = jnp.where(row == 2 * n, (1.0 - bit.astype(F32)) * weight, out)
        out = jnp.where(row == 2 * n + 1, bit.astype(F32) * weight, out)
    return out.astype(BF)


INNER = [(0, 0, 4, 4, 0, 0, 8, 8)]
RIM = [
    (0, 0, 12, 4, 0, 0, 4, 8),
    (0, 1, 0, 0, 4, 0, 4, 8),
    (1, 0, 4, 12, 0, 0, 8, 4),
    (1, 2, 0, 0, 0, 4, 8, 4),
    (2, 0, 12, 12, 0, 0, 4, 4),
    (2, 1, 0, 8, 4, 0, 4, 4),
    (2, 2, 8, 0, 0, 4, 4, 4),
    (2, 3, 0, 0, 4, 4, 4, 4),
]


def arriving(pieces, arrays, blk_s, sem, n, which):
    block, origin, x, y, bx, by, ex, ey = pieces[n]
    if origin:
        src = arrays[1 + origin].at[which, pl.ds(x, ex), pl.ds(y, ey)]
    else:
        src = arrays[which].at[pl.ds(x, ex), pl.ds(y, ey)]
    return pltpu.make_async_copy(src, blk_s.at[which, block, pl.ds(bx, ex), pl.ds(by, ey)], sem.at[which, n])


def start_all(pieces, arrays, blk_s, sem):
    for n in range(len(pieces)):
        for which in range(2):
            arriving(pieces, arrays, blk_s, sem, n, which).start()


def wait_block(pieces, arrays, blk_s, sem, step):
    for block in sorted({p[0] for p in pieces}):

        @pl.when(step == block)
        def _(block=block):
            for n, piece in enumerate(pieces):
                if piece[0] == block:
                    for which in range(2):
                        arriving(pieces, arrays, blk_s, sem, n, which).wait()


def standardized(block):
    ones = jnp.full((C, C), 1.0 / C, BF)
    flat = block.reshape(64 * 24, C)
    centred = flat.astype(F32) - dot(flat, ones)
    rstd = lax.rsqrt(dot((centred * centred).astype(BF), ones) + 1e-5)
    return (centred * rstd).reshape(64, 3, 8, C), rstd.reshape(64, 3, 8, C)


def kernel(first, *refs):
    pieces = INNER if first else RIM
    arrays = refs[:2] if first else refs[:5]
    refs = refs[len(arrays) :]
    gamma_ref, w_ref, wproj_ref, bias_hbm = refs[:4]
    refs = refs[4:]
    if first:
        dT_ref, small_ref, acc_hbm, biasT_hbm = refs[:4]
        bias_s, out_sem = refs[4:6]
        refs = refs[6:]
    else:
        acc_hbm, accs_ref = refs[:2]
        dT_ref, away_ref, keep_ref = refs[2:5]
        small_ref, acc_s, acc_sem = refs[5:8]
        refs = refs[8:]
    (in_sem, bias_sem, blk_s, dbias_ref, biasT_s, wT_s, xh_s, adj_s, qext_s, gz_s, kext_s, v_s, kT_s, vT_s, gT_s, attT_s, u_s, e_s, ds_s) = refs
    step = pl.program_id(0)

    def bias_copy(h):
        return pltpu.make_async_copy(bias_hbm.at[h], (bias_s if first else biasT_s).at[h], bias_sem.at[h])

    def out_copy(n, h):
        src, dst = ((dbias_ref, acc_hbm), (biasT_s, biasT_hbm))[n]
        return pltpu.make_async_copy(src.at[h], dst.at[h], out_sem.at[n, h])

    @pl.when(step == 0)
    def _():
        start_all(pieces, arrays, blk_s, in_sem)
        for h in range(HEADS):
            bias_copy(h).start()
        if not first:
            pltpu.make_async_copy(acc_hbm, acc_s, acc_sem).start()
            dbias_ref[...] = jnp.zeros_like(dbias_ref)
        small_ref[...] = jnp.zeros_like(small_ref)
        wT_s[...] = w_ref[...].astype(F32).T.astype(BF)
        qext_s[...] = jnp.zeros_like(qext_s)
        gz_s[...] = jnp.zeros_like(gz_s)
        vT_s[...] = jnp.ones_like(vT_s)
        kext_s[:, C:] = key_regions()

    if first:
        edge_x = edge_y = False
    else:
        edge_x = (lax.axis_index("gx") == lax.axis_size("gx") - 1) & (step != 1)
        edge_y = (lax.axis_index("gy") == lax.axis_size("gy") - 1) & (step != 0)
    wait_block(pieces, arrays, blk_s, in_sem, step)
    low = lax.broadcasted_iota(jnp.int32, (64, 8, C), 1) < SHIFT
    xh, _ = standardized(blk_s[0, step])
    a = blk_s[1, step].reshape(64, 3, 8, C).astype(F32)
    for z in range(3):
        z1 = (z + 1) % 3
        xh_s[z] = pltpu.roll(jnp.where(low, xh[:, z1], xh[:, z]) * gamma_ref[...], SHIFT, 1).reshape(T, C).astype(BF)
        adj_s[z] = pltpu.roll(jnp.where(low, a[:, z1], a[:, z]), SHIFT, 1).reshape(T, C).astype(BF)

    if not first:

        @pl.when(step == 0)
        def _():
            for h in range(HEADS):
                bias_copy(h).wait()

    def window(z, opening=False, closing=False):
        nrm = xh_s[z]
        adj = adj_s[z]
        qkvT = dot_nt(wT_s[...], nrm).astype(BF)
        kT_s[...] = qkvT[C : 2 * C]
        regions = query_regions((edge_x, edge_y, z == 2))
        for h in range(HEADS):
            vT_s[h, :HD] = qkvT[2 * C + HD * h : 2 * C + HD * (h + 1)]
            qext_s[h, HD * h : HD * (h + 1)] = qkvT[HD * h : HD * (h + 1)]
            qext_s[h, C : C + 16] = regions
        kv = dot(nrm, w_ref[:, C:]).astype(BF)
        kext_s[:, :C] = kv[:, :C]
        v_s[...] = kv[:, C:]
        gT_s[...] = dot_nt(wproj_ref[...], adj).astype(BF)
        chunks = T // KC
        held = {}

        def scores(h, c):
            ks = slice(c * KC, (c + 1) * KC)
            if opening and c == 0:
                bias_copy(h).wait()
                biasT_s[h] = bias_s[h].T * (1.0 / SCALE)
                out_copy(1, h).start()
            u = dot(kext_s[ks], qext_s[h]) + biasT_s[h, ks]
            u_s[h % 2, ks] = u
            top = jnp.max(u.reshape(KC // 8, 8, T), axis=0)
            held["top", h] = top if c == 0 else jnp.maximum(top, held["top", h])
            if c == chunks - 1:
                held["top", h] = jnp.max(held["top", h], axis=0, keepdims=True)

        def weights(h, c):
            ks = slice(c * KC, (c + 1) * KC)
            e = jnp.exp2((u_s[h % 2, ks] - held["top", h]) * EXPC).astype(BF)
            e_s[h % 3, ks] = e
            o = dot(vT_s[h, :, ks], e)
            held["o", h] = o if c == 0 else o + held["o", h]
            if c == chunks - 1:
                o = held["o", h]
                hs = slice(HD * h, HD * (h + 1))
                inverse = 1.0 / o[HD : HD + 1]
                gs = (gT_s[hs].astype(F32) * inverse).astype(BF)
                attended = o[:HD] * inverse
                attT_s[hs] = attended.astype(BF)
                held["delta", h] = jnp.sum(gs.astype(F32) * attended, axis=0, keepdims=True)
                gz_s[h, hs] = gs

        def score_grads(h, c):
            ks = slice(c * KC, (c + 1) * KC)
            dp = dot(v_s[ks], gz_s[h])
            ds = e_s[h % 3, ks].astype(F32) * (dp - held["delta", h])
            ds_s[h % 2, ks] = ds.astype(BF)
            if opening:
                dbias_ref[h, ks] = ds
            else:
                dbias_ref[h, ks] += ds
            if closing and c == chunks - 1:
                out_copy(0, h).start()

        def qkv_grads(h, c):
            hs = slice(HD * h, HD * (h + 1))
            if c == 0:
                dk = dot_nt(qext_s[h, hs], ds_s[h % 2]) * SCALE
                dT_ref[z, C + HD * h : C + HD * (h + 1)] = dk.astype(BF)
            if c == chunks - 1:
                dT_ref[z, 2 * C + HD * h : 2 * C + HD * (h + 1)] = dot_nt(gz_s[h, hs], e_s[h % 3]).astype(BF)
                dT_ref[z, hs] = (dot(kT_s[hs], ds_s[h % 2]) * SCALE).astype(BF)

        for turn in range(HEADS + 3):
            for c in range(chunks):
                for lag, stage in ((3, qkv_grads), (2, score_grads), (1, weights), (0, scores)):
                    if 0 <= turn - lag < HEADS:
                        stage(turn - lag, c)
        small_ref[:C] += dot(attT_s[...], adj)
        small_ref[C:] += dot(dT_ref[z], nrm)

    if first:
        for z in range(3):
            window(z, opening=z == 0, closing=z == 2)
        for h in range(HEADS):
            for n in range(2):
                out_copy(n, h).wait()
    else:
        lax.fori_loop(0, 3, lambda z, carry: (window(z), carry)[1], 0)

        @pl.when(step == pl.num_programs(0) - 1)
        def _():
            pltpu.make_async_copy(acc_hbm, acc_s, acc_sem).wait()
            mine = lax.axis_index("gx") % 2
            small = small_ref[...] + accs_ref[...]
            table = jnp.concatenate([small[:C], small[C:].T], axis=1)
            for j in range(2):
                h = 2 * (1 - mine) + j
                away_ref[j * T : (j + 1) * T] = (dbias_ref[h] + acc_s[h]).T.astype(BF)
                h = 2 * mine + j
                keep_ref[j * T : (j + 1) * T] = (dbias_ref[h] + acc_s[h]).T.astype(BF)
            away_ref[2 * T :] = jnp.where(mine == 1, table, 0.0).astype(BF)
            keep_ref[2 * T :] = jnp.where(mine == 0, table, 0.0).astype(BF)


def finish_kernel(first, *refs):
    pieces = INNER if first else RIM
    arrays = refs[:2] if first else refs[:5]
    refs = refs[len(arrays) :]
    gamma_ref, w_ref, dT_ref = refs[:3]
    ends = refs[4:5] if first else refs[3:7]
    in_sem, out_sem, blk_s, gin_s = refs[-4:]
    step = pl.program_id(0)

    def leaving(n):
        block, origin, x, y, bx, by, ex, ey = pieces[n]
        src = gin_s.at[block, pl.ds(bx, ex), pl.ds(by, ey)]
        return pltpu.make_async_copy(src, ends[origin].at[pl.ds(x, ex), pl.ds(y, ey)], out_sem.at[n])

    @pl.when(step == 0)
    def _():
        start_all(pieces, arrays, blk_s, in_sem)

    wait_block(pieces, arrays, blk_s, in_sem, step)
    low = lax.broadcasted_iota(jnp.int32, (64, 8, C), 1) < SHIFT
    ones = jnp.full((C, C), 1.0 / C, BF)
    xh, rstd = standardized(blk_s[0, step])
    a = blk_s[1, step].reshape(64, 3, 8, C).astype(F32)
    windows = [pltpu.roll(dot(w_ref[...], dT_ref[z]).T.reshape(64, 8, C), SHIFT, 1) for z in range(3)]
    for z in range(3):
        xhat = xh[:, z].reshape(T, C)
        g = jnp.where(low, windows[(z + 2) % 3], windows[z]).reshape(T, C) * gamma_ref[...]
        mean = dot(g.astype(BF), ones)
        slope = dot((g * xhat).astype(BF), ones)
        grad = a[:, z] + rstd[:, z] * (g - mean - xhat * slope).reshape(64, 8, C)
        gin_s[step, :, :, 8 * z : 8 * z + 8] = grad.astype(BF).reshape(8, 8, 8, C)
    for block in sorted({p[0] for p in pieces}):

        @pl.when(step == block)
        def _(block=block):
            for n, piece in enumerate(pieces):
                if piece[0] == block:
                    leaving(n).start()

    @pl.when(step == pl.num_programs(0) - 1)
    def _():
        for n in range(len(pieces)):
            leaving(n).wait()


def whole(shape):
    return pl.BlockSpec(shape, lambda i: (0,) * len(shape))


ANYWHERE = pl.BlockSpec(memory_space=pl.ANY)
DT_BLOCK = pl.BlockSpec((pl.Squeezed(), 3, 3 * C, T), lambda i: (i, 0, 0, 0))
DT_SHAPE = (3, 3 * C, T)


def sublayer(first, arrays, params, carried=()):
    square = (HEADS, T, T)
    small = (4 * C, C)
    blocks = 1 if first else 3
    pieces = INNER if first else RIM
    ins = [ANYWHERE] * len(arrays) + [whole((1, C)), whole((C, 3 * C)), whole((C, C)), ANYWHERE]
    if first:
        outs = [DT_BLOCK, whole(small), ANYWHERE, ANYWHERE]
        shapes = [((blocks,) + DT_SHAPE, BF), (small, F32), (square, F32), (square, F32)]
        scratch = [pltpu.VMEM(square, F32), pltpu.SemaphoreType.DMA((2, HEADS))]
    else:
        ins += [ANYWHERE, whole(small)]
        outs = [DT_BLOCK, whole((HALF, T)), whole((HALF, T))]
        shapes = [((blocks,) + DT_SHAPE, BF), ((HALF, T), BF), ((HALF, T), BF)]
        scratch = [pltpu.VMEM(small, F32), pltpu.VMEM(square, F32), pltpu.SemaphoreType.DMA]
    scratch += [
        pltpu.SemaphoreType.DMA((2, len(pieces))),
        pltpu.SemaphoreType.DMA((HEADS,)),
        pltpu.VMEM((2, blocks, 8, 8, 24, C), BF),
        pltpu.VMEM(square, F32),
        pltpu.VMEM(square, F32),
        pltpu.VMEM((3 * C, C), BF),
        pltpu.VMEM((3, T, C), BF),
        pltpu.VMEM((3, T, C), BF),
        pltpu.VMEM((HEADS, 2 * C, T), BF),
        pltpu.VMEM((HEADS, C, T), BF),
        pltpu.VMEM((T, 2 * C), BF),
        pltpu.VMEM((T, C), BF),
        pltpu.VMEM((C, T), BF),
        pltpu.VMEM((HEADS, 48, T), BF),
        pltpu.VMEM((C, T), BF),
        pltpu.VMEM((C, T), BF),
        pltpu.VMEM((2, T, T), F32),
        pltpu.VMEM((3, T, T), BF),
        pltpu.VMEM((2, T, T), BF),
    ]
    return pl.pallas_call(
        functools.partial(kernel, first),
        grid=(blocks,),
        in_specs=ins,
        out_specs=outs,
        out_shape=[jax.ShapeDtypeStruct(shape, dtype) for shape, dtype in shapes],
        scratch_shapes=scratch,
        compiler_params=pltpu.CompilerParams(vmem_limit_bytes=58 * 1024 * 1024),
        cost_estimate=pl.CostEstimate(flops=blocks * 12 * 10**9, bytes_accessed=blocks * 10**7, transcendentals=0),
        name="inner_windows" if first else "rim_windows",
    )(*arrays, *params, *carried)


def finish(first, arrays, gamma, w, dT, carried=()):
    blocks = 1 if first else 3
    pieces = INNER if first else RIM
    shapes = [(16, 16, 24, C)] if first else [(16, 16, 24, C), (4, 12, 24, C), (12, 4, 24, C), (4, 4, 24, C)]
    return pl.pallas_call(
        functools.partial(finish_kernel, first),
        grid=(blocks,),
        in_specs=[ANYWHERE] * len(arrays) + [whole((1, C)), whole((C, 3 * C)), DT_BLOCK] + [ANYWHERE] * len(carried),
        out_specs=[ANYWHERE] * len(shapes),
        out_shape=[jax.ShapeDtypeStruct(shape, BF) for shape in shapes],
        scratch_shapes=[
            pltpu.SemaphoreType.DMA((2, len(pieces))),
            pltpu.SemaphoreType.DMA((len(pieces),)),
            pltpu.VMEM((2, blocks, 8, 8, 24, C), BF),
            pltpu.VMEM((blocks, 8, 8, 24, C), BF),
        ],
        input_output_aliases={len(arrays) + 3: 0} if first else {},
        compiler_params=pltpu.CompilerParams(vmem_limit_bytes=60 * 1024 * 1024),
        cost_estimate=pl.CostEstimate(flops=blocks * 10**9, bytes_accessed=blocks * 3 * 10**6, transcendentals=0),
        name="inner_finish" if first else "rim_finish",
    )(*arrays, gamma, w, dT, *carried)


def spread_own_kernel(mine_ref, own_ref, out_ref):
    out_ref[...] = own_ref[...].astype(F32)


def spread_own(mine, own):
    return pl.pallas_call(
        spread_own_kernel,
        grid_spec=pltpu.PrefetchScalarGridSpec(
            num_scalar_prefetch=1,
            grid=(2,),
            in_specs=[pl.BlockSpec((T, T), lambda j, m: (j, 0))],
            out_specs=pl.BlockSpec((pl.Squeezed(), T, T), lambda j, m: (2 * m[0] + j, 0, 0)),
        ),
        out_shape=jax.ShapeDtypeStruct((HEADS, T, T), F32),
        compiler_params=pltpu.CompilerParams(vmem_limit_bytes=8 * 1024 * 1024),
        name="spread_own",
    )(mine, own)


def spread_got_kernel(mine_ref, got_ref, own_rest_ref, got_rest_ref, gamma_ref, w_ref, _, out_ref, proj_ref, qkv_ref, gain_ref):
    out_ref[...] = got_ref[...].astype(F32)

    @pl.when(pl.program_id(0) == 0)
    def _():
        table = jnp.where(mine_ref[0] == 0, own_rest_ref[...].astype(F32), got_rest_ref[...].astype(F32))
        proj_ref[...] = table[:, :C]
        qkv_ref[...] = table[:, C:]
        along = (table[:, C:] * w_ref[...].astype(F32)).T
        gain_ref[...] = jnp.sum(along, axis=0, keepdims=True) / gamma_ref[...]


def spread_got(mine, own, got, gamma, w, grad_bias):
    rest = pl.BlockSpec((C, T), lambda j, m: (2 * T // C, 0))

    def all_of(shape):
        return pl.BlockSpec(shape, lambda j, m: (0,) * len(shape))

    return pl.pallas_call(
        spread_got_kernel,
        grid_spec=pltpu.PrefetchScalarGridSpec(
            num_scalar_prefetch=1,
            grid=(2,),
            in_specs=[pl.BlockSpec((T, T), lambda j, m: (j, 0)), rest, rest, all_of((1, C)), all_of((C, 3 * C)), ANYWHERE],
            out_specs=[
                pl.BlockSpec((pl.Squeezed(), T, T), lambda j, m: (2 * (1 - m[0]) + j, 0, 0)),
                all_of((C, C)),
                all_of((C, 3 * C)),
                all_of((1, C)),
            ],
        ),
        out_shape=[
            jax.ShapeDtypeStruct((HEADS, T, T), F32),
            jax.ShapeDtypeStruct((C, C), F32),
            jax.ShapeDtypeStruct((C, 3 * C), F32),
            jax.ShapeDtypeStruct((1, C), F32),
        ],
        input_output_aliases={6: 0},
        compiler_params=pltpu.CompilerParams(vmem_limit_bytes=8 * 1024 * 1024),
        name="spread_got",
    )(mine, got, own, got, gamma, w, grad_bias)


def shifted(values, by_x, by_y):
    nx, ny = lax.axis_size("gx"), lax.axis_size("gy")
    if not by_y:
        return lax.ppermute(values, "gx", [(i, (i + by_x) % nx) for i in range(nx)])
    if not by_x:
        return lax.ppermute(values, "gy", [(i, (i + by_y) % ny) for i in range(ny)])
    pairs = [(i * ny + j, (i + by_x) % nx * ny + (j + by_y) % ny) for i in range(nx) for j in range(ny)]
    return lax.ppermute(values, ("gx", "gy"), pairs)


CORE = ("gx", 1, 2)
ACROSS_X = ("gx", 2, 4)
ACROSS_Z = ("gy", 1, 4)
ACROSS_Y = ("y", 0, 4)


def moved(i, j, digit, by):
    axis, stride, size = digit
    if axis == "y":
        y = (j // 4 * 2 + i // 8 + by) % 4
        return y % 2 * 8 + i % 8, y // 2 * 4 + j % 4
    place = i if axis == "gx" else j
    old = place // stride % size
    place += ((old + by) % size - old) * stride
    return (place, j) if axis == "gx" else (i, place)


def send(values, digits, by):
    pairs = []
    for i in range(16):
        for j in range(8):
            k, l = moved(i, j, digits[i % 2], by)
            pairs.append((i * 8 + j, k * 8 + l))
    return lax.ppermute(values, ("gx", "gy"), pairs)


def my_digit(digits):
    gx, gy = lax.axis_index("gx"), lax.axis_index("gy")
    return jnp.where(gx % 2 == 0, *[(gx if axis == "gx" else gy) // stride % size for axis, stride, size in digits])


def parts_sent(values, digits):
    mine = my_digit(digits)
    rows = values.shape[0] // 4
    got = [send(lax.dynamic_slice_in_dim(values, (mine + by) % 4 * rows, rows).astype(BF), digits, by) for by in (2, 1, 3)]
    return lax.dynamic_slice_in_dim(values, mine * rows, rows), got


def added(values, got):
    for part in got:
        values = values + part.astype(F32)
    return values


def all_sent(values, digits):
    return {by: send(values, digits, by) for by in (2, 1, 3)}


def gathered(values, got, digits):
    mine = my_digit(digits)
    rows = values.shape[0]
    out = jnp.zeros((4 * rows,) + values.shape[1:], values.dtype)
    out = lax.dynamic_update_slice_in_dim(out, values, mine * rows, 0)
    for by in (2, 1, 3):
        out = lax.dynamic_update_slice_in_dim(out, got[by], (mine - by) % 4 * rows, 0)
    return out


def body(retained_source, incoming_adjoint, rescale_multiplier, triple_projection_matrix, w_proj, pos_bias):
    both = (retained_source, incoming_adjoint)
    from_x = shifted(jnp.stack([v[:4, 4:] for v in both]), -1, 0)
    from_y = shifted(jnp.stack([v[4:, :4] for v in both]), 0, -1)
    from_xy = shifted(jnp.stack([v[:4, :4] for v in both]), -1, -1)
    w = triple_projection_matrix
    gamma = rescale_multiplier.reshape(1, C)
    inner_dT, acc_small, acc, biasT = sublayer(True, both, (gamma, w, w_proj, pos_bias))
    around = both + (from_x, from_y, from_xy)
    rim_dT, away, keep = sublayer(False, around, (gamma, w, w_proj, biasT), (acc, acc_small))

    first, second, third = (ACROSS_X, ACROSS_Z), (ACROSS_Z, ACROSS_X), (ACROSS_Y, ACROSS_Y)
    values = keep.astype(F32) + send(away, (CORE, CORE), 1).astype(F32)
    values, got = parts_sent(values, first)
    gin, back_x, back_y, back_xy = finish(False, around, gamma, w, rim_dT)
    values, got, back_x, back_y, back_xy = lax.optimization_barrier((values, got, back_x, back_y, back_xy))
    back = (shifted(back_x, 1, 0), shifted(back_y, 0, 1), shifted(back_xy, 1, 1))
    values, got = parts_sent(added(values, got), second)
    values = added(values, got)
    got = all_sent(values, third)
    values = ((values + got[2]) + (got[1] + got[3])).astype(BF)
    got = all_sent(values, second)
    values, got, back = lax.optimization_barrier((values, got, back))
    values = gathered(values, got, second)
    got = all_sent(values, first)
    (gin, inner_dT) = lax.optimization_barrier((gin, inner_dT, values))[:2]
    (gin,) = finish(True, both, gamma, w, inner_dT, (gin,))
    for part, place in zip(back, ((0, 4), (4, 0), (0, 0))):
        gin = lax.dynamic_update_slice(gin, part, place + (0, 0))
    values, got, gin = lax.optimization_barrier((values, got, gin))
    own = gathered(values, got, first)
    got = send(own, (CORE, CORE), 1)
    mine = (lax.axis_index("gx") % 2).reshape(1)
    grad_bias = spread_own(mine, own)
    grad_bias, got = lax.optimization_barrier((grad_bias, got))
    grad_bias, grad_proj, grad_qkv, gain = spread_got(mine, own, got, gamma, w, grad_bias)
    return (gin, grad_bias, grad_proj, grad_qkv, gain.reshape(C))


def solution(mesh):
    placed = (P("gx", "gy", None, None), P("gx", "gy", None, None), P(), P(), P(), P())
    return jax.shard_map(
        body,
        mesh=mesh,
        in_specs=placed,
        out_specs=(P("gx", "gy", None, None), P(), P(), P(), P()),
        check_vma=False,
    )
```

```python
import functools
import math

import jax
import jax.numpy as jnp
from jax import lax
from jax.experimental import pallas as pl
from jax.experimental.pallas import tpu as pltpu
from jax.sharding import PartitionSpec as P

HEADS = 4
HD = 32
C = 128
T = 512
KC = 256
HALF = 2 * T + C
SHIFT = 4
SCALE = HD**-0.5
EXPC = SCALE / math.log(2.0)
BLOCKED = -(2.0**100)
F32 = jnp.float32
BF = jnp.bfloat16


def dot(a, b):
    return lax.dot_general(a, b, (((1,), (0,)), ((), ())), preferred_element_type=F32)


def dot_nt(a, b):
    return lax.dot_general(a, b, (((1,), (1,)), ((), ())), preferred_element_type=F32)


def half_bits(shape, dim):
    token = lax.broadcasted_iota(jnp.int32, shape, dim)
    return [lax.shift_right_logical(token, s) & 1 for s in (8, 5, 2)]


def key_regions():
    lane = lax.broadcasted_iota(jnp.int32, (T, C), 1)
    out = jnp.zeros((T, C), F32)
    for n, bit in enumerate(half_bits((T, C), 0)):
        out = jnp.where(lane == 2 * n, bit.astype(F32), out)
        out = jnp.where(lane == 2 * n + 1, 1.0 - bit.astype(F32), out)
    return out.astype(BF)


def query_regions(edges):
    row = lax.broadcasted_iota(jnp.int32, (16, T), 0)
    out = jnp.zeros((16, T), F32)
    for n, (bit, edge) in enumerate(zip(half_bits((16, T), 1), edges)):
        weight = jnp.where(edge, BLOCKED, 0.0)
        out = jnp.where(row == 2 * n, (1.0 - bit.astype(F32)) * weight, out)
        out = jnp.where(row == 2 * n + 1, bit.astype(F32) * weight, out)
    return out.astype(BF)


INNER = [(0, 0, 4, 4, 0, 0, 8, 8)]
RIM = [
    (0, 0, 12, 4, 0, 0, 4, 8),
    (0, 1, 0, 0, 4, 0, 4, 8),
    (1, 0, 4, 12, 0, 0, 8, 4),
    (1, 2, 0, 0, 0, 4, 8, 4),
    (2, 0, 12, 12, 0, 0, 4, 4),
    (2, 1, 0, 8, 4, 0, 4, 4),
    (2, 2, 8, 0, 0, 4, 4, 4),
    (2, 3, 0, 0, 4, 4, 4, 4),
]


def arriving(pieces, arrays, blk_s, sem, n, which):
    block, origin, x, y, bx, by, ex, ey = pieces[n]
    if origin:
        src = arrays[1 + origin].at[which, pl.ds(x, ex), pl.ds(y, ey)]
    else:
        src = arrays[which].at[pl.ds(x, ex), pl.ds(y, ey)]
    return pltpu.make_async_copy(src, blk_s.at[which, block, pl.ds(bx, ex), pl.ds(by, ey)], sem.at[which, n])


def start_all(pieces, arrays, blk_s, sem):
    for n in range(len(pieces)):
        for which in range(2):
            arriving(pieces, arrays, blk_s, sem, n, which).start()


def wait_block(pieces, arrays, blk_s, sem, step):
    for block in sorted({p[0] for p in pieces}):

        @pl.when(step == block)
        def _(block=block):
            for n, piece in enumerate(pieces):
                if piece[0] == block:
                    for which in range(2):
                        arriving(pieces, arrays, blk_s, sem, n, which).wait()


def standardized(block):
    ones = jnp.full((C, C), 1.0 / C, BF)
    flat = block.reshape(64 * 24, C)
    centred = flat.astype(F32) - dot(flat, ones)
    rstd = lax.rsqrt(dot((centred * centred).astype(BF), ones) + 1e-5)
    return (centred * rstd).reshape(64, 3, 8, C), rstd.reshape(64, 3, 8, C)


def kernel(first, *refs):
    pieces = INNER if first else RIM
    arrays = refs[:2] if first else refs[:5]
    refs = refs[len(arrays) :]
    gamma_ref, w_ref, wproj_ref, bias_hbm = refs[:4]
    refs = refs[4:]
    if first:
        dT_ref, small_ref, acc_hbm, biasT_hbm = refs[:4]
        bias_s, out_sem = refs[4:6]
        refs = refs[6:]
    else:
        acc_hbm, accs_ref = refs[:2]
        dT_ref, away_ref, keep_ref = refs[2:5]
        small_ref, acc_s, acc_sem = refs[5:8]
        refs = refs[8:]
    (in_sem, bias_sem, blk_s, dbias_ref, biasT_s, wT_s, xh_s, adj_s, qext_s, gz_s, kext_s, v_s, kT_s, vT_s, gT_s, attT_s, u_s, e_s, ds_s) = refs
    step = pl.program_id(0)

    def bias_copy(h):
        return pltpu.make_async_copy(bias_hbm.at[h], (bias_s if first else biasT_s).at[h], bias_sem.at[h])

    def out_copy(n, h):
        src, dst = ((dbias_ref, acc_hbm), (biasT_s, biasT_hbm))[n]
        return pltpu.make_async_copy(src.at[h], dst.at[h], out_sem.at[n, h])

    @pl.when(step == 0)
    def _():
        start_all(pieces, arrays, blk_s, in_sem)
        for h in range(HEADS):
            bias_copy(h).start()
        if not first:
            pltpu.make_async_copy(acc_hbm, acc_s, acc_sem).start()
            dbias_ref[...] = jnp.zeros_like(dbias_ref)
        small_ref[...] = jnp.zeros_like(small_ref)
        wT_s[...] = w_ref[...].astype(F32).T.astype(BF)
        qext_s[...] = jnp.zeros_like(qext_s)
        gz_s[...] = jnp.zeros_like(gz_s)
        vT_s[...] = jnp.ones_like(vT_s)
        kext_s[:, C:] = key_regions()

    if first:
        edge_x = edge_y = False
    else:
        edge_x = (lax.axis_index("gx") == lax.axis_size("gx") - 1) & (step != 1)
        edge_y = (lax.axis_index("gy") == lax.axis_size("gy") - 1) & (step != 0)
    wait_block(pieces, arrays, blk_s, in_sem, step)
    low = lax.broadcasted_iota(jnp.int32, (64, 8, C), 1) < SHIFT
    xh, _ = standardized(blk_s[0, step])
    a = blk_s[1, step].reshape(64, 3, 8, C).astype(F32)
    for z in range(3):
        z1 = (z + 1) % 3
        xh_s[z] = pltpu.roll(jnp.where(low, xh[:, z1], xh[:, z]) * gamma_ref[...], SHIFT, 1).reshape(T, C).astype(BF)
        adj_s[z] = pltpu.roll(jnp.where(low, a[:, z1], a[:, z]), SHIFT, 1).reshape(T, C).astype(BF)

    if not first:

        @pl.when(step == 0)
        def _():
            for h in range(HEADS):
                bias_copy(h).wait()

    def window(z, opening=False, closing=False):
        nrm = xh_s[z]
        adj = adj_s[z]
        qkvT = dot_nt(wT_s[...], nrm).astype(BF)
        kT_s[...] = qkvT[C : 2 * C]
        regions = query_regions((edge_x, edge_y, z == 2))
        for h in range(HEADS):
            vT_s[h, :HD] = qkvT[2 * C + HD * h : 2 * C + HD * (h + 1)]
            qext_s[h, HD * h : HD * (h + 1)] = qkvT[HD * h : HD * (h + 1)]
            qext_s[h, C : C + 16] = regions
        kv = dot(nrm, w_ref[:, C:]).astype(BF)
        kext_s[:, :C] = kv[:, :C]
        v_s[...] = kv[:, C:]
        gT_s[...] = dot_nt(wproj_ref[...], adj).astype(BF)
        chunks = T // KC
        held = {}

        def scores(h, c):
            ks = slice(c * KC, (c + 1) * KC)
            if opening and c == 0:
                bias_copy(h).wait()
                biasT_s[h] = bias_s[h].T * (1.0 / SCALE)
                out_copy(1, h).start()
            u = dot(kext_s[ks], qext_s[h]) + biasT_s[h, ks]
            u_s[h % 2, ks] = u
            top = jnp.max(u.reshape(KC // 8, 8, T), axis=0)
            held["top", h] = top if c == 0 else jnp.maximum(top, held["top", h])
            if c == chunks - 1:
                held["top", h] = jnp.max(held["top", h], axis=0, keepdims=True)

        def weights(h, c):
            ks = slice(c * KC, (c + 1) * KC)
            e = jnp.exp2((u_s[h % 2, ks] - held["top", h]) * EXPC).astype(BF)
            e_s[h % 3, ks] = e
            o = dot(vT_s[h, :, ks], e)
            held["o", h] = o if c == 0 else o + held["o", h]
            if c == chunks - 1:
                o = held["o", h]
                hs = slice(HD * h, HD * (h + 1))
                inverse = 1.0 / o[HD : HD + 1]
                gs = (gT_s[hs].astype(F32) * inverse).astype(BF)
                attended = o[:HD] * inverse
                attT_s[hs] = attended.astype(BF)
                held["delta", h] = jnp.sum(gs.astype(F32) * attended, axis=0, keepdims=True)
                gz_s[h, hs] = gs

        def score_grads(h, c):
            ks = slice(c * KC, (c + 1) * KC)
            dp = dot(v_s[ks], gz_s[h])
            ds = e_s[h % 3, ks].astype(F32) * (dp - held["delta", h])
            ds_s[h % 2, ks] = ds.astype(BF)
            if opening:
                dbias_ref[h, ks] = ds
            else:
                dbias_ref[h, ks] += ds
            if closing and c == chunks - 1:
                out_copy(0, h).start()

        def qkv_grads(h, c):
            hs = slice(HD * h, HD * (h + 1))
            if c == 0:
                dk = dot_nt(qext_s[h, hs], ds_s[h % 2]) * SCALE
                dT_ref[z, C + HD * h : C + HD * (h + 1)] = dk.astype(BF)
            if c == chunks - 1:
                dT_ref[z, 2 * C + HD * h : 2 * C + HD * (h + 1)] = dot_nt(gz_s[h, hs], e_s[h % 3]).astype(BF)
                dT_ref[z, hs] = (dot(kT_s[hs], ds_s[h % 2]) * SCALE).astype(BF)

        for turn in range(HEADS + 3):
            for c in range(chunks):
                for lag, stage in ((3, qkv_grads), (2, score_grads), (1, weights), (0, scores)):
                    if 0 <= turn - lag < HEADS:
                        stage(turn - lag, c)
        small_ref[:C] += dot(attT_s[...], adj)
        small_ref[C:] += dot(dT_ref[z], nrm)

    if first:
        for z in range(3):
            window(z, opening=z == 0, closing=z == 2)
        for h in range(HEADS):
            for n in range(2):
                out_copy(n, h).wait()
    else:
        lax.fori_loop(0, 3, lambda z, carry: (window(z), carry)[1], 0)

        @pl.when(step == pl.num_programs(0) - 1)
        def _():
            pltpu.make_async_copy(acc_hbm, acc_s, acc_sem).wait()
            mine = lax.axis_index("gx") % 2
            small = small_ref[...] + accs_ref[...]
            table = jnp.concatenate([small[:C], small[C:].T], axis=1)
            for j in range(2):
                h = 2 * (1 - mine) + j
                away_ref[j * T : (j + 1) * T] = (dbias_ref[h] + acc_s[h]).T.astype(BF)
                h = 2 * mine + j
                keep_ref[j * T : (j + 1) * T] = (dbias_ref[h] + acc_s[h]).T.astype(BF)
            away_ref[2 * T :] = jnp.where(mine == 1, table, 0.0).astype(BF)
            keep_ref[2 * T :] = jnp.where(mine == 0, table, 0.0).astype(BF)


def finish_kernel(first, *refs):
    pieces = INNER if first else RIM
    arrays = refs[:2] if first else refs[:5]
    refs = refs[len(arrays) :]
    gamma_ref, w_ref, dT_ref = refs[:3]
    ends = refs[4:5] if first else refs[3:7]
    in_sem, out_sem, blk_s, gin_s = refs[-4:]
    step = pl.program_id(0)

    def leaving(n):
        block, origin, x, y, bx, by, ex, ey = pieces[n]
        src = gin_s.at[block, pl.ds(bx, ex), pl.ds(by, ey)]
        return pltpu.make_async_copy(src, ends[origin].at[pl.ds(x, ex), pl.ds(y, ey)], out_sem.at[n])

    @pl.when(step == 0)
    def _():
        start_all(pieces, arrays, blk_s, in_sem)

    wait_block(pieces, arrays, blk_s, in_sem, step)
    low = lax.broadcasted_iota(jnp.int32, (64, 8, C), 1) < SHIFT
    ones = jnp.full((C, C), 1.0 / C, BF)
    xh, rstd = standardized(blk_s[0, step])
    a = blk_s[1, step].reshape(64, 3, 8, C).astype(F32)
    windows = [pltpu.roll(dot(w_ref[...], dT_ref[z]).T.reshape(64, 8, C), SHIFT, 1) for z in range(3)]
    for z in range(3):
        xhat = xh[:, z].reshape(T, C)
        g = jnp.where(low, windows[(z + 2) % 3], windows[z]).reshape(T, C) * gamma_ref[...]
        mean = dot(g.astype(BF), ones)
        slope = dot((g * xhat).astype(BF), ones)
        grad = a[:, z] + rstd[:, z] * (g - mean - xhat * slope).reshape(64, 8, C)
        gin_s[step, :, :, 8 * z : 8 * z + 8] = grad.astype(BF).reshape(8, 8, 8, C)
    for block in sorted({p[0] for p in pieces}):

        @pl.when(step == block)
        def _(block=block):
            for n, piece in enumerate(pieces):
                if piece[0] == block:
                    leaving(n).start()

    @pl.when(step == pl.num_programs(0) - 1)
    def _():
        for n in range(len(pieces)):
            leaving(n).wait()


def whole(shape):
    return pl.BlockSpec(shape, lambda i: (0,) * len(shape))


ANYWHERE = pl.BlockSpec(memory_space=pl.ANY)
DT_BLOCK = pl.BlockSpec((pl.Squeezed(), 3, 3 * C, T), lambda i: (i, 0, 0, 0))
DT_SHAPE = (3, 3 * C, T)


def sublayer(first, arrays, params, carried=()):
    square = (HEADS, T, T)
    small = (4 * C, C)
    blocks = 1 if first else 3
    pieces = INNER if first else RIM
    ins = [ANYWHERE] * len(arrays) + [whole((1, C)), whole((C, 3 * C)), whole((C, C)), ANYWHERE]
    if first:
        outs = [DT_BLOCK, whole(small), ANYWHERE, ANYWHERE]
        shapes = [((blocks,) + DT_SHAPE, BF), (small, F32), (square, F32), (square, F32)]
        scratch = [pltpu.VMEM(square, F32), pltpu.SemaphoreType.DMA((2, HEADS))]
    else:
        ins += [ANYWHERE, whole(small)]
        outs = [DT_BLOCK, whole((HALF, T)), whole((HALF, T))]
        shapes = [((blocks,) + DT_SHAPE, BF), ((HALF, T), BF), ((HALF, T), BF)]
        scratch = [pltpu.VMEM(small, F32), pltpu.VMEM(square, F32), pltpu.SemaphoreType.DMA]
    scratch += [
        pltpu.SemaphoreType.DMA((2, len(pieces))),
        pltpu.SemaphoreType.DMA((HEADS,)),
        pltpu.VMEM((2, blocks, 8, 8, 24, C), BF),
        pltpu.VMEM(square, F32),
        pltpu.VMEM(square, F32),
        pltpu.VMEM((3 * C, C), BF),
        pltpu.VMEM((3, T, C), BF),
        pltpu.VMEM((3, T, C), BF),
        pltpu.VMEM((HEADS, 2 * C, T), BF),
        pltpu.VMEM((HEADS, C, T), BF),
        pltpu.VMEM((T, 2 * C), BF),
        pltpu.VMEM((T, C), BF),
        pltpu.VMEM((C, T), BF),
        pltpu.VMEM((HEADS, 48, T), BF),
        pltpu.VMEM((C, T), BF),
        pltpu.VMEM((C, T), BF),
        pltpu.VMEM((2, T, T), F32),
        pltpu.VMEM((3, T, T), BF),
        pltpu.VMEM((2, T, T), BF),
    ]
    return pl.pallas_call(
        functools.partial(kernel, first),
        grid=(blocks,),
        in_specs=ins,
        out_specs=outs,
        out_shape=[jax.ShapeDtypeStruct(shape, dtype) for shape, dtype in shapes],
        scratch_shapes=scratch,
        compiler_params=pltpu.CompilerParams(vmem_limit_bytes=58 * 1024 * 1024),
        cost_estimate=pl.CostEstimate(flops=blocks * 12 * 10**9, bytes_accessed=blocks * 10**7, transcendentals=0),
        name="inner_windows" if first else "rim_windows",
    )(*arrays, *params, *carried)


def finish(first, arrays, gamma, w, dT, carried=()):
    blocks = 1 if first else 3
    pieces = INNER if first else RIM
    shapes = [(16, 16, 24, C)] if first else [(16, 16, 24, C), (4, 12, 24, C), (12, 4, 24, C), (4, 4, 24, C)]
    return pl.pallas_call(
        functools.partial(finish_kernel, first),
        grid=(blocks,),
        in_specs=[ANYWHERE] * len(arrays) + [whole((1, C)), whole((C, 3 * C)), DT_BLOCK] + [ANYWHERE] * len(carried),
        out_specs=[ANYWHERE] * len(shapes),
        out_shape=[jax.ShapeDtypeStruct(shape, BF) for shape in shapes],
        scratch_shapes=[
            pltpu.SemaphoreType.DMA((2, len(pieces))),
            pltpu.SemaphoreType.DMA((len(pieces),)),
            pltpu.VMEM((2, blocks, 8, 8, 24, C), BF),
            pltpu.VMEM((blocks, 8, 8, 24, C), BF),
        ],
        input_output_aliases={len(arrays) + 3: 0} if first else {},
        compiler_params=pltpu.CompilerParams(vmem_limit_bytes=60 * 1024 * 1024),
        cost_estimate=pl.CostEstimate(flops=blocks * 10**9, bytes_accessed=blocks * 3 * 10**6, transcendentals=0),
        name="inner_finish" if first else "rim_finish",
    )(*arrays, gamma, w, dT, *carried)


def spread_own_kernel(mine_ref, own_ref, out_ref):
    out_ref[...] = own_ref[...].astype(F32)


def spread_own(mine, own):
    return pl.pallas_call(
        spread_own_kernel,
        grid_spec=pltpu.PrefetchScalarGridSpec(
            num_scalar_prefetch=1,
            grid=(2,),
            in_specs=[pl.BlockSpec((T, T), lambda j, m: (j, 0))],
            out_specs=pl.BlockSpec((pl.Squeezed(), T, T), lambda j, m: (2 * m[0] + j, 0, 0)),
        ),
        out_shape=jax.ShapeDtypeStruct((HEADS, T, T), F32),
        compiler_params=pltpu.CompilerParams(vmem_limit_bytes=8 * 1024 * 1024),
        name="spread_own",
    )(mine, own)


def spread_got_kernel(mine_ref, got_ref, own_rest_ref, got_rest_ref, gamma_ref, w_ref, _, out_ref, proj_ref, qkv_ref, gain_ref):
    out_ref[...] = got_ref[...].astype(F32)

    @pl.when(pl.program_id(0) == 0)
    def _():
        table = jnp.where(mine_ref[0] == 0, own_rest_ref[...].astype(F32), got_rest_ref[...].astype(F32))
        proj_ref[...] = table[:, :C]
        qkv_ref[...] = table[:, C:]
        along = (table[:, C:] * w_ref[...].astype(F32)).T
        gain_ref[...] = jnp.sum(along, axis=0, keepdims=True) / gamma_ref[...]


def spread_got(mine, own, got, gamma, w, grad_bias):
    rest = pl.BlockSpec((C, T), lambda j, m: (2 * T // C, 0))

    def all_of(shape):
        return pl.BlockSpec(shape, lambda j, m: (0,) * len(shape))

    return pl.pallas_call(
        spread_got_kernel,
        grid_spec=pltpu.PrefetchScalarGridSpec(
            num_scalar_prefetch=1,
            grid=(2,),
            in_specs=[pl.BlockSpec((T, T), lambda j, m: (j, 0)), rest, rest, all_of((1, C)), all_of((C, 3 * C)), ANYWHERE],
            out_specs=[
                pl.BlockSpec((pl.Squeezed(), T, T), lambda j, m: (2 * (1 - m[0]) + j, 0, 0)),
                all_of((C, C)),
                all_of((C, 3 * C)),
                all_of((1, C)),
            ],
        ),
        out_shape=[
            jax.ShapeDtypeStruct((HEADS, T, T), F32),
            jax.ShapeDtypeStruct((C, C), F32),
            jax.ShapeDtypeStruct((C, 3 * C), F32),
            jax.ShapeDtypeStruct((1, C), F32),
        ],
        input_output_aliases={6: 0},
        compiler_params=pltpu.CompilerParams(vmem_limit_bytes=8 * 1024 * 1024),
        name="spread_got",
    )(mine, got, own, got, gamma, w, grad_bias)


def shifted(values, by_x, by_y):
    nx, ny = lax.axis_size("gx"), lax.axis_size("gy")
    if not by_y:
        return lax.ppermute(values, "gx", [(i, (i + by_x) % nx) for i in range(nx)])
    if not by_x:
        return lax.ppermute(values, "gy", [(i, (i + by_y) % ny) for i in range(ny)])
    pairs = [(i * ny + j, (i + by_x) % nx * ny + (j + by_y) % ny) for i in range(nx) for j in range(ny)]
    return lax.ppermute(values, ("gx", "gy"), pairs)


CORE = ("gx", 1, 2)
ACROSS_X = ("gx", 2, 4)
ACROSS_Z = ("gy", 1, 4)
ACROSS_Y = ("y", 0, 4)


def moved(i, j, digit, by):
    axis, stride, size = digit
    if axis == "y":
        y = (j // 4 * 2 + i // 8 + by) % 4
        return y % 2 * 8 + i % 8, y // 2 * 4 + j % 4
    place = i if axis == "gx" else j
    old = place // stride % size
    place += ((old + by) % size - old) * stride
    return (place, j) if axis == "gx" else (i, place)


def send(values, digits, by):
    pairs = []
    for i in range(16):
        for j in range(8):
            k, l = moved(i, j, digits[i % 2], by)
            pairs.append((i * 8 + j, k * 8 + l))
    return lax.ppermute(values, ("gx", "gy"), pairs)


def my_digit(digits):
    gx, gy = lax.axis_index("gx"), lax.axis_index("gy")
    return jnp.where(gx % 2 == 0, *[(gx if axis == "gx" else gy) // stride % size for axis, stride, size in digits])


def parts_sent(values, digits):
    mine = my_digit(digits)
    rows = values.shape[0] // 4
    got = [send(lax.dynamic_slice_in_dim(values, (mine + by) % 4 * rows, rows).astype(BF), digits, by) for by in (2, 1, 3)]
    return lax.dynamic_slice_in_dim(values, mine * rows, rows), got


def added(values, got):
    for part in got:
        values = values + part.astype(F32)
    return values


def all_sent(values, digits):
    return {by: send(values, digits, by) for by in (2, 1, 3)}


def gathered(values, got, digits):
    mine = my_digit(digits)
    rows = values.shape[0]
    out = jnp.zeros((4 * rows,) + values.shape[1:], values.dtype)
    out = lax.dynamic_update_slice_in_dim(out, values, mine * rows, 0)
    for by in (2, 1, 3):
        out = lax.dynamic_update_slice_in_dim(out, got[by], (mine - by) % 4 * rows, 0)
    return out


def body(retained_source, incoming_adjoint, rescale_multiplier, triple_projection_matrix, w_proj, pos_bias):
    both = (retained_source, incoming_adjoint)
    from_x = shifted(jnp.stack([v[:4, 4:] for v in both]), -1, 0)
    from_y = shifted(jnp.stack([v[4:, :4] for v in both]), 0, -1)
    from_xy = shifted(jnp.stack([v[:4, :4] for v in both]), -1, -1)
    w = triple_projection_matrix
    gamma = rescale_multiplier.reshape(1, C)
    inner_dT, acc_small, acc, biasT = sublayer(True, both, (gamma, w, w_proj, pos_bias))
    around = both + (from_x, from_y, from_xy)
    rim_dT, away, keep = sublayer(False, around, (gamma, w, w_proj, biasT), (acc, acc_small))

    first, second, third = (ACROSS_X, ACROSS_Z), (ACROSS_Z, ACROSS_X), (ACROSS_Y, ACROSS_Y)
    values = keep.astype(F32) + send(away, (CORE, CORE), 1).astype(F32)
    values, got = parts_sent(values, first)
    gin, back_x, back_y, back_xy = finish(False, around, gamma, w, rim_dT)
    values, got, back_x, back_y, back_xy = lax.optimization_barrier((values, got, back_x, back_y, back_xy))
    back = (shifted(back_x, 1, 0), shifted(back_y, 0, 1), shifted(back_xy, 1, 1))
    values, got = parts_sent(added(values, got), second)
    values = added(values, got)
    got = all_sent(values, third)
    values = ((values + got[2]) + (got[1] + got[3])).astype(BF)
    got = all_sent(values, second)
    gin, inner_dT, _ = lax.optimization_barrier((gin, inner_dT, values))
    (gin,) = finish(True, both, gamma, w, inner_dT, (gin,))
    values, got, back, gin = lax.optimization_barrier((values, got, back, gin))
    values = gathered(values, got, second)
    got = all_sent(values, first)
    for part, place in zip(back, ((0, 4), (4, 0), (0, 0))):
        gin = lax.dynamic_update_slice(gin, part, place + (0, 0))
    values, got, gin = lax.optimization_barrier((values, got, gin))
    own = gathered(values, got, first)
    got = send(own, (CORE, CORE), 1)
    mine = (lax.axis_index("gx") % 2).reshape(1)
    grad_bias = spread_own(mine, own)
    grad_bias, got = lax.optimization_barrier((grad_bias, got))
    grad_bias, grad_proj, grad_qkv, gain = spread_got(mine, own, got, gamma, w, grad_bias)
    return (gin, grad_bias, grad_proj, grad_qkv, gain.reshape(C))


def solution(mesh):
    placed = (P("gx", "gy", None, None), P("gx", "gy", None, None), P(), P(), P(), P())
    return jax.shard_map(
        body,
        mesh=mesh,
        in_specs=placed,
        out_specs=(P("gx", "gy", None, None), P(), P(), P(), P()),
        check_vma=False,
    )
```

```python
import functools
import math

import jax
import jax.numpy as jnp
from jax import lax
from jax.experimental import pallas as pl
from jax.experimental.pallas import tpu as pltpu
from jax.sharding import PartitionSpec as P

HEADS = 4
HD = 32
C = 128
T = 512
KC = 256
HALF = 2 * T + C
SHIFT = 4
SCALE = HD**-0.5
EXPC = SCALE / math.log(2.0)
BLOCKED = -(2.0**100)
F32 = jnp.float32
BF = jnp.bfloat16


def dot(a, b):
    return lax.dot_general(a, b, (((1,), (0,)), ((), ())), preferred_element_type=F32)


def dot_nt(a, b):
    return lax.dot_general(a, b, (((1,), (1,)), ((), ())), preferred_element_type=F32)


def half_bits(shape, dim):
    token = lax.broadcasted_iota(jnp.int32, shape, dim)
    return [lax.shift_right_logical(token, s) & 1 for s in (8, 5, 2)]


def key_regions():
    lane = lax.broadcasted_iota(jnp.int32, (T, C), 1)
    out = jnp.zeros((T, C), F32)
    for n, bit in enumerate(half_bits((T, C), 0)):
        out = jnp.where(lane == 2 * n, bit.astype(F32), out)
        out = jnp.where(lane == 2 * n + 1, 1.0 - bit.astype(F32), out)
    return out.astype(BF)


def query_regions(edges):
    row = lax.broadcasted_iota(jnp.int32, (16, T), 0)
    out = jnp.zeros((16, T), F32)
    for n, (bit, edge) in enumerate(zip(half_bits((16, T), 1), edges)):
        weight = jnp.where(edge, BLOCKED, 0.0)
        out = jnp.where(row == 2 * n, (1.0 - bit.astype(F32)) * weight, out)
        out = jnp.where(row == 2 * n + 1, bit.astype(F32) * weight, out)
    return out.astype(BF)


INNER = [(0, 0, 4, 4, 0, 0, 8, 8)]
RIM = [
    (0, 0, 12, 4, 0, 0, 4, 8),
    (0, 1, 0, 0, 4, 0, 4, 8),
    (1, 0, 4, 12, 0, 0, 8, 4),
    (1, 2, 0, 0, 0, 4, 8, 4),
    (2, 0, 12, 12, 0, 0, 4, 4),
    (2, 1, 0, 8, 4, 0, 4, 4),
    (2, 2, 8, 0, 0, 4, 4, 4),
    (2, 3, 0, 0, 4, 4, 4, 4),
]


def arriving(pieces, arrays, blk_s, sem, n, which):
    block, origin, x, y, bx, by, ex, ey = pieces[n]
    if origin:
        src = arrays[1 + origin].at[which, pl.ds(x, ex), pl.ds(y, ey)]
    else:
        src = arrays[which].at[pl.ds(x, ex), pl.ds(y, ey)]
    return pltpu.make_async_copy(src, blk_s.at[which, block, pl.ds(bx, ex), pl.ds(by, ey)], sem.at[which, n])


def start_all(pieces, arrays, blk_s, sem):
    for n in range(len(pieces)):
        for which in range(2):
            arriving(pieces, arrays, blk_s, sem, n, which).start()


def wait_block(pieces, arrays, blk_s, sem, step):
    for block in sorted({p[0] for p in pieces}):

        @pl.when(step == block)
        def _(block=block):
            for n, piece in enumerate(pieces):
                if piece[0] == block:
                    for which in range(2):
                        arriving(pieces, arrays, blk_s, sem, n, which).wait()


def standardized(block):
    ones = jnp.full((C, C), 1.0 / C, BF)
    flat = block.reshape(64 * 24, C)
    centred = flat.astype(F32) - dot(flat, ones)
    rstd = lax.rsqrt(dot((centred * centred).astype(BF), ones) + 1e-5)
    return (centred * rstd).reshape(64, 3, 8, C), rstd.reshape(64, 3, 8, C)


def kernel(first, *refs):
    pieces = INNER if first else RIM
    arrays = refs[:2] if first else refs[:5]
    refs = refs[len(arrays) :]
    gamma_ref, w_ref, wproj_ref, bias_hbm = refs[:4]
    refs = refs[4:]
    if first:
        dT_ref, small_ref, acc_hbm, biasT_hbm = refs[:4]
        bias_s, out_sem = refs[4:6]
        refs = refs[6:]
    else:
        acc_hbm, accs_ref = refs[:2]
        dT_ref, away_ref, keep_ref = refs[2:5]
        small_ref, acc_s, acc_sem = refs[5:8]
        refs = refs[8:]
    (in_sem, bias_sem, blk_s, dbias_ref, biasT_s, wT_s, xh_s, adj_s, qext_s, gz_s, kext_s, v_s, kT_s, vT_s, gT_s, attT_s, u_s, e_s, ds_s) = refs
    step = pl.program_id(0)

    def bias_copy(h):
        return pltpu.make_async_copy(bias_hbm.at[h], (bias_s if first else biasT_s).at[h], bias_sem.at[h])

    def out_copy(n, h):
        src, dst = ((dbias_ref, acc_hbm), (biasT_s, biasT_hbm))[n]
        return pltpu.make_async_copy(src.at[h], dst.at[h], out_sem.at[n, h])

    @pl.when(step == 0)
    def _():
        start_all(pieces, arrays, blk_s, in_sem)
        for h in range(HEADS):
            bias_copy(h).start()
        if not first:
            pltpu.make_async_copy(acc_hbm, acc_s, acc_sem).start()
            dbias_ref[...] = jnp.zeros_like(dbias_ref)
        small_ref[...] = jnp.zeros_like(small_ref)
        wT_s[...] = w_ref[...].astype(F32).T.astype(BF)
        qext_s[...] = jnp.zeros_like(qext_s)
        gz_s[...] = jnp.zeros_like(gz_s)
        vT_s[...] = jnp.ones_like(vT_s)
        kext_s[:, C:] = key_regions()

    if first:
        edge_x = edge_y = False
    else:
        edge_x = (lax.axis_index("gx") == lax.axis_size("gx") - 1) & (step != 1)
        edge_y = (lax.axis_index("gy") == lax.axis_size("gy") - 1) & (step != 0)
    wait_block(pieces, arrays, blk_s, in_sem, step)
    low = lax.broadcasted_iota(jnp.int32, (64, 8, C), 1) < SHIFT
    xh, _ = standardized(blk_s[0, step])
    a = blk_s[1, step].reshape(64, 3, 8, C).astype(F32)
    for z in range(3):
        z1 = (z + 1) % 3
        xh_s[z] = pltpu.roll(jnp.where(low, xh[:, z1], xh[:, z]) * gamma_ref[...], SHIFT, 1).reshape(T, C).astype(BF)
        adj_s[z] = pltpu.roll(jnp.where(low, a[:, z1], a[:, z]), SHIFT, 1).reshape(T, C).astype(BF)

    if not first:

        @pl.when(step == 0)
        def _():
            for h in range(HEADS):
                bias_copy(h).wait()

    def window(z, opening=False, closing=False):
        nrm = xh_s[z]
        adj = adj_s[z]
        qkvT = dot_nt(wT_s[...], nrm).astype(BF)
        kT_s[...] = qkvT[C : 2 * C]
        regions = query_regions((edge_x, edge_y, z == 2))
        for h in range(HEADS):
            vT_s[h, :HD] = qkvT[2 * C + HD * h : 2 * C + HD * (h + 1)]
            qext_s[h, HD * h : HD * (h + 1)] = qkvT[HD * h : HD * (h + 1)]
            qext_s[h, C : C + 16] = regions
        kv = dot(nrm, w_ref[:, C:]).astype(BF)
        kext_s[:, :C] = kv[:, :C]
        v_s[...] = kv[:, C:]
        gT_s[...] = dot_nt(wproj_ref[...], adj).astype(BF)
        chunks = T // KC
        held = {}

        def scores(h, c):
            ks = slice(c * KC, (c + 1) * KC)
            if opening and c == 0:
                bias_copy(h).wait()
                biasT_s[h] = bias_s[h].T * (1.0 / SCALE)
                out_copy(1, h).start()
            u = dot(kext_s[ks], qext_s[h]) + biasT_s[h, ks]
            u_s[h % 2, ks] = u
            top = jnp.max(u.reshape(KC // 8, 8, T), axis=0)
            held["top", h] = top if c == 0 else jnp.maximum(top, held["top", h])
            if c == chunks - 1:
                held["top", h] = jnp.max(held["top", h], axis=0, keepdims=True)

        def weights(h, c):
            ks = slice(c * KC, (c + 1) * KC)
            e = jnp.exp2((u_s[h % 2, ks] - held["top", h]) * EXPC).astype(BF)
            e_s[h % 3, ks] = e
            o = dot(vT_s[h, :, ks], e)
            held["o", h] = o if c == 0 else o + held["o", h]
            if c == chunks - 1:
                o = held["o", h]
                hs = slice(HD * h, HD * (h + 1))
                inverse = 1.0 / o[HD : HD + 1]
                gs = (gT_s[hs].astype(F32) * inverse).astype(BF)
                attended = o[:HD] * inverse
                attT_s[hs] = attended.astype(BF)
                held["delta", h] = jnp.sum(gs.astype(F32) * attended, axis=0, keepdims=True)
                gz_s[h, hs] = gs

        def score_grads(h, c):
            ks = slice(c * KC, (c + 1) * KC)
            dp = dot(v_s[ks], gz_s[h])
            ds = e_s[h % 3, ks].astype(F32) * (dp - held["delta", h])
            ds_s[h % 2, ks] = ds.astype(BF)
            if opening:
                dbias_ref[h, ks] = ds
            else:
                dbias_ref[h, ks] += ds
            if closing and c == chunks - 1:
                out_copy(0, h).start()

        def qkv_grads(h, c):
            hs = slice(HD * h, HD * (h + 1))
            if c == 0:
                dk = dot_nt(qext_s[h, hs], ds_s[h % 2]) * SCALE
                dT_ref[z, C + HD * h : C + HD * (h + 1)] = dk.astype(BF)
            if c == chunks - 1:
                dT_ref[z, 2 * C + HD * h : 2 * C + HD * (h + 1)] = dot_nt(gz_s[h, hs], e_s[h % 3]).astype(BF)
                dT_ref[z, hs] = (dot(kT_s[hs], ds_s[h % 2]) * SCALE).astype(BF)

        for turn in range(HEADS + 3):
            for c in range(chunks):
                for lag, stage in ((0, scores), (3, qkv_grads), (2, score_grads), (1, weights)):
                    if 0 <= turn - lag < HEADS:
                        stage(turn - lag, c)
        small_ref[:C] += dot(attT_s[...], adj)
        small_ref[C:] += dot(dT_ref[z], nrm)

    if first:
        for z in range(3):
            window(z, opening=z == 0, closing=z == 2)
        for h in range(HEADS):
            for n in range(2):
                out_copy(n, h).wait()
    else:
        lax.fori_loop(0, 3, lambda z, carry: (window(z), carry)[1], 0)

        @pl.when(step == pl.num_programs(0) - 1)
        def _():
            pltpu.make_async_copy(acc_hbm, acc_s, acc_sem).wait()
            mine = lax.axis_index("gx") % 2
            small = small_ref[...] + accs_ref[...]
            table = jnp.concatenate([small[:C], small[C:].T], axis=1)
            for j in range(2):
                h = 2 * (1 - mine) + j
                away_ref[j * T : (j + 1) * T] = (dbias_ref[h] + acc_s[h]).T.astype(BF)
                h = 2 * mine + j
                keep_ref[j * T : (j + 1) * T] = (dbias_ref[h] + acc_s[h]).T.astype(BF)
            away_ref[2 * T :] = jnp.where(mine == 1, table, 0.0).astype(BF)
            keep_ref[2 * T :] = jnp.where(mine == 0, table, 0.0).astype(BF)


def finish_kernel(first, *refs):
    pieces = INNER if first else RIM
    arrays = refs[:2] if first else refs[:5]
    refs = refs[len(arrays) :]
    gamma_ref, w_ref, dT_ref = refs[:3]
    ends = refs[4:5] if first else refs[3:7]
    in_sem, out_sem, blk_s, gin_s = refs[-4:]
    step = pl.program_id(0)

    def leaving(n):
        block, origin, x, y, bx, by, ex, ey = pieces[n]
        src = gin_s.at[block, pl.ds(bx, ex), pl.ds(by, ey)]
        return pltpu.make_async_copy(src, ends[origin].at[pl.ds(x, ex), pl.ds(y, ey)], out_sem.at[n])

    @pl.when(step == 0)
    def _():
        start_all(pieces, arrays, blk_s, in_sem)

    wait_block(pieces, arrays, blk_s, in_sem, step)
    low = lax.broadcasted_iota(jnp.int32, (64, 8, C), 1) < SHIFT
    ones = jnp.full((C, C), 1.0 / C, BF)
    xh, rstd = standardized(blk_s[0, step])
    a = blk_s[1, step].reshape(64, 3, 8, C).astype(F32)
    windows = [pltpu.roll(dot(w_ref[...], dT_ref[z]).T.reshape(64, 8, C), SHIFT, 1) for z in range(3)]
    for z in range(3):
        xhat = xh[:, z].reshape(T, C)
        g = jnp.where(low, windows[(z + 2) % 3], windows[z]).reshape(T, C) * gamma_ref[...]
        mean = dot(g.astype(BF), ones)
        slope = dot((g * xhat).astype(BF), ones)
        grad = a[:, z] + rstd[:, z] * (g - mean - xhat * slope).reshape(64, 8, C)
        gin_s[step, :, :, 8 * z : 8 * z + 8] = grad.astype(BF).reshape(8, 8, 8, C)
    for block in sorted({p[0] for p in pieces}):

        @pl.when(step == block)
        def _(block=block):
            for n, piece in enumerate(pieces):
                if piece[0] == block:
                    leaving(n).start()

    @pl.when(step == pl.num_programs(0) - 1)
    def _():
        for n in range(len(pieces)):
            leaving(n).wait()


def whole(shape):
    return pl.BlockSpec(shape, lambda i: (0,) * len(shape))


ANYWHERE = pl.BlockSpec(memory_space=pl.ANY)
DT_BLOCK = pl.BlockSpec((pl.Squeezed(), 3, 3 * C, T), lambda i: (i, 0, 0, 0))
DT_SHAPE = (3, 3 * C, T)


def sublayer(first, arrays, params, carried=()):
    square = (HEADS, T, T)
    small = (4 * C, C)
    blocks = 1 if first else 3
    pieces = INNER if first else RIM
    ins = [ANYWHERE] * len(arrays) + [whole((1, C)), whole((C, 3 * C)), whole((C, C)), ANYWHERE]
    if first:
        outs = [DT_BLOCK, whole(small), ANYWHERE, ANYWHERE]
        shapes = [((blocks,) + DT_SHAPE, BF), (small, F32), (square, F32), (square, F32)]
        scratch = [pltpu.VMEM(square, F32), pltpu.SemaphoreType.DMA((2, HEADS))]
    else:
        ins += [ANYWHERE, whole(small)]
        outs = [DT_BLOCK, whole((HALF, T)), whole((HALF, T))]
        shapes = [((blocks,) + DT_SHAPE, BF), ((HALF, T), BF), ((HALF, T), BF)]
        scratch = [pltpu.VMEM(small, F32), pltpu.VMEM(square, F32), pltpu.SemaphoreType.DMA]
    scratch += [
        pltpu.SemaphoreType.DMA((2, len(pieces))),
        pltpu.SemaphoreType.DMA((HEADS,)),
        pltpu.VMEM((2, blocks, 8, 8, 24, C), BF),
        pltpu.VMEM(square, F32),
        pltpu.VMEM(square, F32),
        pltpu.VMEM((3 * C, C), BF),
        pltpu.VMEM((3, T, C), BF),
        pltpu.VMEM((3, T, C), BF),
        pltpu.VMEM((HEADS, 2 * C, T), BF),
        pltpu.VMEM((HEADS, C, T), BF),
        pltpu.VMEM((T, 2 * C), BF),
        pltpu.VMEM((T, C), BF),
        pltpu.VMEM((C, T), BF),
        pltpu.VMEM((HEADS, 48, T), BF),
        pltpu.VMEM((C, T), BF),
        pltpu.VMEM((C, T), BF),
        pltpu.VMEM((2, T, T), F32),
        pltpu.VMEM((3, T, T), BF),
        pltpu.VMEM((2, T, T), BF),
    ]
    return pl.pallas_call(
        functools.partial(kernel, first),
        grid=(blocks,),
        in_specs=ins,
        out_specs=outs,
        out_shape=[jax.ShapeDtypeStruct(shape, dtype) for shape, dtype in shapes],
        scratch_shapes=scratch,
        compiler_params=pltpu.CompilerParams(vmem_limit_bytes=58 * 1024 * 1024),
        cost_estimate=pl.CostEstimate(flops=blocks * 12 * 10**9, bytes_accessed=blocks * 10**7, transcendentals=0),
        name="inner_windows" if first else "rim_windows",
    )(*arrays, *params, *carried)


def finish(first, arrays, gamma, w, dT, carried=()):
    blocks = 1 if first else 3
    pieces = INNER if first else RIM
    shapes = [(16, 16, 24, C)] if first else [(16, 16, 24, C), (4, 12, 24, C), (12, 4, 24, C), (4, 4, 24, C)]
    return pl.pallas_call(
        functools.partial(finish_kernel, first),
        grid=(blocks,),
        in_specs=[ANYWHERE] * len(arrays) + [whole((1, C)), whole((C, 3 * C)), DT_BLOCK] + [ANYWHERE] * len(carried),
        out_specs=[ANYWHERE] * len(shapes),
        out_shape=[jax.ShapeDtypeStruct(shape, BF) for shape in shapes],
        scratch_shapes=[
            pltpu.SemaphoreType.DMA((2, len(pieces))),
            pltpu.SemaphoreType.DMA((len(pieces),)),
            pltpu.VMEM((2, blocks, 8, 8, 24, C), BF),
            pltpu.VMEM((blocks, 8, 8, 24, C), BF),
        ],
        input_output_aliases={len(arrays) + 3: 0} if first else {},
        compiler_params=pltpu.CompilerParams(vmem_limit_bytes=60 * 1024 * 1024),
        cost_estimate=pl.CostEstimate(flops=blocks * 10**9, bytes_accessed=blocks * 3 * 10**6, transcendentals=0),
        name="inner_finish" if first else "rim_finish",
    )(*arrays, gamma, w, dT, *carried)


def spread_own_kernel(mine_ref, own_ref, out_ref):
    out_ref[...] = own_ref[...].astype(F32)


def spread_own(mine, own):
    return pl.pallas_call(
        spread_own_kernel,
        grid_spec=pltpu.PrefetchScalarGridSpec(
            num_scalar_prefetch=1,
            grid=(2,),
            in_specs=[pl.BlockSpec((T, T), lambda j, m: (j, 0))],
            out_specs=pl.BlockSpec((pl.Squeezed(), T, T), lambda j, m: (2 * m[0] + j, 0, 0)),
        ),
        out_shape=jax.ShapeDtypeStruct((HEADS, T, T), F32),
        compiler_params=pltpu.CompilerParams(vmem_limit_bytes=8 * 1024 * 1024),
        name="spread_own",
    )(mine, own)


def spread_got_kernel(mine_ref, got_ref, own_rest_ref, got_rest_ref, gamma_ref, w_ref, _, out_ref, proj_ref, qkv_ref, gain_ref):
    out_ref[...] = got_ref[...].astype(F32)

    @pl.when(pl.program_id(0) == 0)
    def _():
        table = jnp.where(mine_ref[0] == 0, own_rest_ref[...].astype(F32), got_rest_ref[...].astype(F32))
        proj_ref[...] = table[:, :C]
        qkv_ref[...] = table[:, C:]
        along = (table[:, C:] * w_ref[...].astype(F32)).T
        gain_ref[...] = jnp.sum(along, axis=0, keepdims=True) / gamma_ref[...]


def spread_got(mine, own, got, gamma, w, grad_bias):
    rest = pl.BlockSpec((C, T), lambda j, m: (2 * T // C, 0))

    def all_of(shape):
        return pl.BlockSpec(shape, lambda j, m: (0,) * len(shape))

    return pl.pallas_call(
        spread_got_kernel,
        grid_spec=pltpu.PrefetchScalarGridSpec(
            num_scalar_prefetch=1,
            grid=(2,),
            in_specs=[pl.BlockSpec((T, T), lambda j, m: (j, 0)), rest, rest, all_of((1, C)), all_of((C, 3 * C)), ANYWHERE],
            out_specs=[
                pl.BlockSpec((pl.Squeezed(), T, T), lambda j, m: (2 * (1 - m[0]) + j, 0, 0)),
                all_of((C, C)),
                all_of((C, 3 * C)),
                all_of((1, C)),
            ],
        ),
        out_shape=[
            jax.ShapeDtypeStruct((HEADS, T, T), F32),
            jax.ShapeDtypeStruct((C, C), F32),
            jax.ShapeDtypeStruct((C, 3 * C), F32),
            jax.ShapeDtypeStruct((1, C), F32),
        ],
        input_output_aliases={6: 0},
        compiler_params=pltpu.CompilerParams(vmem_limit_bytes=8 * 1024 * 1024),
        name="spread_got",
    )(mine, got, own, got, gamma, w, grad_bias)


def shifted(values, by_x, by_y):
    nx, ny = lax.axis_size("gx"), lax.axis_size("gy")
    if not by_y:
        return lax.ppermute(values, "gx", [(i, (i + by_x) % nx) for i in range(nx)])
    if not by_x:
        return lax.ppermute(values, "gy", [(i, (i + by_y) % ny) for i in range(ny)])
    pairs = [(i * ny + j, (i + by_x) % nx * ny + (j + by_y) % ny) for i in range(nx) for j in range(ny)]
    return lax.ppermute(values, ("gx", "gy"), pairs)


CORE = ("gx", 1, 2)
ACROSS_X = ("gx", 2, 4)
ACROSS_Z = ("gy", 1, 4)
ACROSS_Y = ("y", 0, 4)


def moved(i, j, digit, by):
    axis, stride, size = digit
    if axis == "y":
        y = (j // 4 * 2 + i // 8 + by) % 4
        return y % 2 * 8 + i % 8, y // 2 * 4 + j % 4
    place = i if axis == "gx" else j
    old = place // stride % size
    place += ((old + by) % size - old) * stride
    return (place, j) if axis == "gx" else (i, place)


def send(values, digits, by):
    pairs = []
    for i in range(16):
        for j in range(8):
            k, l = moved(i, j, digits[i % 2], by)
            pairs.append((i * 8 + j, k * 8 + l))
    return lax.ppermute(values, ("gx", "gy"), pairs)


def my_digit(digits):
    gx, gy = lax.axis_index("gx"), lax.axis_index("gy")
    return jnp.where(gx % 2 == 0, *[(gx if axis == "gx" else gy) // stride % size for axis, stride, size in digits])


def parts_sent(values, digits):
    mine = my_digit(digits)
    rows = values.shape[0] // 4
    got = [send(lax.dynamic_slice_in_dim(values, (mine + by) % 4 * rows, rows).astype(BF), digits, by) for by in (2, 1, 3)]
    return lax.dynamic_slice_in_dim(values, mine * rows, rows), got


def added(values, got):
    for part in got:
        values = values + part.astype(F32)
    return values


def all_sent(values, digits):
    return {by: send(values, digits, by) for by in (2, 1, 3)}


def gathered(values, got, digits):
    mine = my_digit(digits)
    rows = values.shape[0]
    out = jnp.zeros((4 * rows,) + values.shape[1:], values.dtype)
    out = lax.dynamic_update_slice_in_dim(out, values, mine * rows, 0)
    for by in (2, 1, 3):
        out = lax.dynamic_update_slice_in_dim(out, got[by], (mine - by) % 4 * rows, 0)
    return out


def body(retained_source, incoming_adjoint, rescale_multiplier, triple_projection_matrix, w_proj, pos_bias):
    both = (retained_source, incoming_adjoint)
    from_x = shifted(jnp.stack([v[:4, 4:] for v in both]), -1, 0)
    from_y = shifted(jnp.stack([v[4:, :4] for v in both]), 0, -1)
    from_xy = shifted(jnp.stack([v[:4, :4] for v in both]), -1, -1)
    w = triple_projection_matrix
    gamma = rescale_multiplier.reshape(1, C)
    inner_dT, acc_small, acc, biasT = sublayer(True, both, (gamma, w, w_proj, pos_bias))
    around = both + (from_x, from_y, from_xy)
    rim_dT, away, keep = sublayer(False, around, (gamma, w, w_proj, biasT), (acc, acc_small))

    first, second, third = (ACROSS_X, ACROSS_Z), (ACROSS_Z, ACROSS_X), (ACROSS_Y, ACROSS_Y)
    values = keep.astype(F32) + send(away, (CORE, CORE), 1).astype(F32)
    values, got = parts_sent(values, first)
    gin, back_x, back_y, back_xy = finish(False, around, gamma, w, rim_dT)
    values, got, back_x, back_y, back_xy = lax.optimization_barrier((values, got, back_x, back_y, back_xy))
    back = (shifted(back_x, 1, 0), shifted(back_y, 0, 1), shifted(back_xy, 1, 1))
    values, got = parts_sent(added(values, got), second)
    values = added(values, got)
    got = all_sent(values, third)
    values = ((values + got[2]) + (got[1] + got[3])).astype(BF)
    got = all_sent(values, second)
    values, got, back = lax.optimization_barrier((values, got, back))
    values = gathered(values, got, second)
    got = all_sent(values, first)
    (gin, inner_dT) = lax.optimization_barrier((gin, inner_dT, values))[:2]
    (gin,) = finish(True, both, gamma, w, inner_dT, (gin,))
    for part, place in zip(back, ((0, 4), (4, 0), (0, 0))):
        gin = lax.dynamic_update_slice(gin, part, place + (0, 0))
    values, got, gin = lax.optimization_barrier((values, got, gin))
    own = gathered(values, got, first)
    got = send(own, (CORE, CORE), 1)
    mine = (lax.axis_index("gx") % 2).reshape(1)
    grad_bias = spread_own(mine, own)
    grad_bias, got = lax.optimization_barrier((grad_bias, got))
    grad_bias, grad_proj, grad_qkv, gain = spread_got(mine, own, got, gamma, w, grad_bias)
    return (gin, grad_bias, grad_proj, grad_qkv, gain.reshape(C))


def solution(mesh):
    placed = (P("gx", "gy", None, None), P("gx", "gy", None, None), P(), P(), P(), P())
    return jax.shard_map(
        body,
        mesh=mesh,
        in_specs=placed,
        out_specs=(P("gx", "gy", None, None), P(), P(), P(), P()),
        check_vma=False,
    )
```
